32 devices in a mesh: dp: 8 (over y, x, core), tensor: 4 (over z).
Axes of the slice: x: 2, y: 2, z: 4, core: 2. Of those that a mesh axis runs over, the one named last changes fastest.
Arguments:
- tokens: bfloat16 [1152, 8, 1024], P('tensor', 'dp'), may hold values from -6 to 6
- segment_ids: int32 [8, 1152], P('dp'), may hold values from 0 to 2, as said below
- norm1_gain: float32 [1024], replicated, may hold values from 0.5 to 1.5
- w_query: bfloat16 [1024, 1024], P(None, 'tensor'), may hold values from -0.046875 to 0.046875
- w_key: bfloat16 [1024, 1024], P(None, 'tensor'), may hold values from -0.1875 to 0.1875
- w_value: bfloat16 [1024, 1024], P(None, 'tensor'), may hold values from -0.1875 to 0.1875
- w_out: bfloat16 [1024, 1024], P('tensor'), may hold values from -0.375 to 0.375
- rel_bias: float32 [32, 16], P(None, 'tensor'), may hold values from -4 to 4
- norm2_gain: float32 [1024], replicated, may hold values from 0.5 to 1.5
- gate_weight_matrix: bfloat16 [1024, 2816], P(None, 'tensor'), may hold values from -0.1875 to 0.1875
- upward_weight: bfloat16 [1024, 2816], P(None, 'tensor'), may hold values from -0.1875 to 0.1875
- downward_weight: bfloat16 [2816, 1024], P('tensor'), may hold values from -0.15625 to 0.15625
- cotangent: bfloat16 [1152, 8, 1024], P('tensor', 'dp'), may hold values from -6 to 6
Outputs:
- out_tokens: bfloat16 [1152, 8, 1024], P('tensor', 'dp')
- grad_tokens: bfloat16 [1152, 8, 1024], P('tensor', 'dp')
- grad_norm1: float32 [1024], replicated
- grad_query: float32 [1024, 1024], P(None, 'tensor')
- grad_key: float32 [1024, 1024], P(None, 'tensor')
- grad_value: float32 [1024, 1024], P(None, 'tensor')
- grad_out: float32 [1024, 1024], P('tensor')
- grad_bias: float32 [32, 16], P(None, 'tensor')
- grad_norm2: float32 [1024], replicated
- gate_weight_gradient: float32 [1024, 2816], P(None, 'tensor')
- upward_weight_gradient: float32 [1024, 2816], P(None, 'tensor')
- downward_weight_gradient: float32 [2816, 1024], P('tensor')
- rms_stats: float32 [3], replicated
The draws below stay inside these ranges and needn't reach their ends.
Inputs may be any that keep to these rules, and one draw needn't show every extreme that they name: `segment_ids`: in each row the ids are either all 0 (one example) or position // (384) (three examples of equal length); both kinds occur in every draw.
All inputs are finite; a program needn't handle non-finite values.
Results may differ from the reference program's by a relative error of at most 0.02.
Values may be sent and summed in bfloat16 or wider, within the bound.
No kernel may reach another device: no remote copies, remote signals or barrier semaphores. Data moves between devices by JAX's collectives and lax.ppermute only.
A program may use at most 192 MiB of HBM per device.

```python
import jax
import jax.numpy as jnp
from jax import lax

D = 1024
HEADS = 16
DKV = 64
FF = 2816
BUCKETS = 32
LEN = 1152
ROWS = 8


def draw_segment_ids(key, part):
    row_kinds = jax.random.randint(key, (ROWS,), 0, 2)
    row_kinds = row_kinds.at[0].set(1).at[1].set(0)
    positions = jnp.arange(LEN, dtype=jnp.int32)
    return jnp.where(row_kinds[:, None] == 1, positions[None, :] // (LEN // 3), 0).astype(jnp.int32)


def shard_levels(rng, extent, cuts, low, high):
    level = 1.0
    for dim, shards_of in cuts:
        steps = jax.random.uniform(jax.random.fold_in(jax.random.fold_in(rng, 6), dim), (shards_of,), jnp.float32, low / len(cuts), high / len(cuts))
        level = level * jnp.repeat(jnp.exp(steps), extent[dim] // shards_of).reshape((-1,) + (1,) * (len(extent) - 1 - dim))
    return level


def normal_values(key, shape, scale, bound, cuts=(), held_as=jnp.bfloat16):
    level = shard_levels(key, shape, cuts, -0.22, 0.18) if cuts else 1.0
    array = jax.random.normal(key, shape, jnp.float32) * scale * level
    return jnp.minimum(jnp.maximum(array, -bound), bound).astype(held_as)


def setup_inputs(seed: int = 0) -> dict:
    splits = jax.random.split(jax.random.key(seed), 14)
    return {
        "tokens": normal_values(splits[0], (LEN, ROWS, D), 1.0, 6.0, ((0, 4), (1, 8))),
        "segment_ids": draw_segment_ids(jax.random.fold_in(splits[13], 71), 0),
        "norm1_gain": jnp.clip(1.0 + 0.1 * jax.random.normal(splits[2], (D,), jnp.float32), 0.5, 1.5),
        "w_query": normal_values(splits[3], (D, HEADS * DKV), (16 * D) ** -0.5, 0.046875, ((1, 4),)),
        "w_key": normal_values(splits[4], (D, HEADS * DKV), D ** -0.5, 0.1875, ((1, 4),)),
        "w_value": normal_values(splits[5], (D, HEADS * DKV), D ** -0.5, 0.1875, ((1, 4),)),
        "w_out": normal_values(splits[6], (HEADS * DKV, D), (HEADS * DKV // 4) ** -0.5, 0.375, ((0, 4),)),
        "rel_bias": normal_values(splits[7], (BUCKETS, HEADS), 1.0, 4.0, ((1, 4),), jnp.float32),
        "norm2_gain": jnp.clip(1.0 + 0.1 * jax.random.normal(splits[8], (D,), jnp.float32), 0.5, 1.5),
        "gate_weight_matrix": normal_values(splits[9], (D, FF), D ** -0.5, 0.1875, ((1, 4),)),
        "upward_weight": normal_values(splits[10], (D, FF), D ** -0.5, 0.1875, ((1, 4),)),
        "downward_weight": normal_values(splits[11], (FF, D), (FF // 2) ** -0.5, 0.15625, ((0, 4),)),
        "cotangent": normal_values(splits[12], (LEN, ROWS, D), 1.0, 6.0, ((0, 4), (1, 8))),
    }


EPSILON = 1e-06
THRESHOLDS = (12, 16, 23, 32, 46, 64, 91)

@jax.custom_vjp
def low(v):
    return lax.optimization_barrier(v.astype(jnp.bfloat16)).astype(jnp.float32)

@jax.custom_vjp
def low_back(v):
    return v

def low_keep(v):
    return (low(v), None)

def low_pass(kept, grad):
    return (grad,)

def back_keep(v):
    return (v, None)

def back_low(kept, grad):
    return (low(grad),)
low.defvjp(low_keep, low_pass)
low_back.defvjp(back_keep, back_low)

def bucket_of(offset):
    distance = jnp.abs(offset)
    far_bucket = 8 + sum(((distance >= threshold).astype(jnp.int32) for threshold in THRESHOLDS))
    return jnp.where(distance < 8, distance, far_bucket) + 16 * (offset > 0).astype(jnp.int32)

def rms_norm(values, gain):
    return values * lax.rsqrt(lax.optimization_barrier(jnp.mean(values * values, axis=-1, keepdims=True)) + EPSILON) * gain

def matmul_hi(left, right):
    return jnp.dot(left, right, precision=lax.Precision.HIGHEST)

def row_layer(params, x_row, seg_row):
    gain_one, query_w, key_w, value_w, out_w, bias_w, gain_two, gate_w, up_w, down_w = params
    length = x_row.shape[0]
    norm_one = low(rms_norm(x_row, gain_one))
    queries = low_back(low(matmul_hi(norm_one, query_w))).reshape(length, HEADS, DKV)
    key_rows = low_back(low(matmul_hi(norm_one, key_w))).reshape(length, HEADS, DKV)
    value_rows = low_back(low(matmul_hi(norm_one, value_w))).reshape(length, HEADS, DKV)
    positions = jnp.arange(length, dtype=jnp.int32)
    offsets = positions[None, :] - positions[:, None]
    bias_full = jnp.transpose(jnp.take(bias_w, bucket_of(offsets), axis=0), (2, 0, 1))
    raw_scores = jnp.einsum('qhd,khd->hqk', queries, key_rows, precision=lax.Precision.HIGHEST)
    scores = low_back(raw_scores) + bias_full
    same_seg = seg_row[:, None] == seg_row[None, :]
    scores = jnp.where(same_seg[None], scores, -1000000000.0)
    soft_weights = jax.nn.softmax(scores, axis=-1)
    mixed = jnp.einsum('hqk,khd->qhd', low(soft_weights), value_rows, precision=lax.Precision.HIGHEST)
    mixed = low_back(low(mixed.reshape(length, HEADS * DKV)))
    attn_branch = low_back(matmul_hi(mixed, out_w))
    hidden_in = x_row + attn_branch
    norm_two = low(rms_norm(hidden_in, gain_two))
    gate_preactivation = low_back(matmul_hi(norm_two, gate_w))
    upward_preactivation = low_back(matmul_hi(norm_two, up_w))
    hidden_state = low(jax.nn.gelu(gate_preactivation, approximate=True) * upward_preactivation)
    ffn_branch = low_back(matmul_hi(hidden_state, down_w))
    return (hidden_in + ffn_branch, jnp.sum(attn_branch * attn_branch), jnp.sum(ffn_branch * ffn_branch))

def reference(tokens, segment_ids, norm1_gain, w_query, w_key, w_value, w_out, rel_bias, norm2_gain, gate_weight_matrix, upward_weight, downward_weight, cotangent):
    inputs = jnp.transpose(tokens.astype(jnp.float32), (1, 0, 2))
    cot_rows = jnp.transpose(cotangent.astype(jnp.float32), (1, 0, 2))
    params = (norm1_gain, w_query.astype(jnp.float32), w_key.astype(jnp.float32), w_value.astype(jnp.float32), w_out.astype(jnp.float32), rel_bias, norm2_gain, gate_weight_matrix.astype(jnp.float32), upward_weight.astype(jnp.float32), downward_weight.astype(jnp.float32))

    def forward(inputs_in, params_in):

        def one_row(row_items):
            return row_layer(params_in, row_items[0], row_items[1])
        out_rows, attn_sq, ffn_sq = lax.map(jax.checkpoint(one_row), (inputs_in, segment_ids))
        return (out_rows, (attn_sq, ffn_sq))
    out_rows, back_fn, squares = jax.vjp(forward, inputs, params, has_aux=True)
    grad_inputs, grad_params = back_fn(cot_rows)
    count = out_rows.size
    stat_sums = jnp.stack([jnp.sum(squares[0]), jnp.sum(squares[1]), jnp.sum(out_rows * out_rows)])
    rms_stats = jnp.sqrt(stat_sums / count)
    out_tokens = jnp.transpose(out_rows, (1, 0, 2)).astype(jnp.bfloat16)
    grad_tokens = jnp.transpose(grad_inputs, (1, 0, 2)).astype(jnp.bfloat16)
    return (out_tokens, grad_tokens, grad_params[0], grad_params[1], grad_params[2], grad_params[3], grad_params[4], grad_params[5], grad_params[6], grad_params[7], grad_params[8], grad_params[9], rms_stats)
```

```python
import functools
from jax.sharding import PartitionSpec as P
import jax
import jax.numpy as jnp
from jax import lax
from jax.experimental import pallas as pl
from jax.experimental.pallas import tpu as pltpu

EPSILON = 1e-06
THRESHOLDS = (12, 16, 23, 32, 46, 64, 91)
TILE = 128
SEG = 384
NT = (((1,), (1,)), ((), ()))
TN = (((0,), (0,)), ((), ()))
F32 = jnp.float32
BF16 = jnp.bfloat16


def bucket_of(offset):
    distance = jnp.abs(offset)
    far_bucket = 8 + sum(((distance >= threshold).astype(jnp.int32) for threshold in THRESHOLDS))
    return jnp.where(distance < 8, distance, far_bucket) + 16 * (offset > 0).astype(jnp.int32)


def tile_bucket(delta, key_axis):
    keys = lax.broadcasted_iota(jnp.int32, (TILE, TILE), key_axis)
    queries = lax.broadcasted_iota(jnp.int32, (TILE, TILE), 1 - key_axis)
    return bucket_of(TILE * delta + keys - queries)


def bias_tiles_kernel(bias_ref, rows_ref, cols_ref):
    buckets, heads = bias_ref.shape
    for out_ref, key_axis in ((rows_ref, 1), (cols_ref, 0)):
        for delta in (-1, 0, 1):
            bucket = tile_bucket(delta, key_axis)
            tiles = [jnp.zeros((TILE, TILE), F32) for _ in range(heads)]
            for b in range(buckets):
                hit = bucket == b
                tiles = [jnp.where(hit, bias_ref[b, h], t) for h, t in enumerate(tiles)]
            for h in range(heads):
                out_ref[h, delta + 1] = tiles[h]


def bias_tiles(rel_bias):
    heads = rel_bias.shape[1]
    shape = jax.ShapeDtypeStruct((heads, 3, TILE, TILE), F32)
    return pl.pallas_call(
        bias_tiles_kernel,
        out_shape=(shape, shape),
        in_specs=[pl.BlockSpec(memory_space=pltpu.SMEM)],
        out_specs=(pl.BlockSpec(memory_space=pltpu.VMEM),) * 2,
        name="bias_tiles",
    )(rel_bias)


def bias_grad_kernel(near_ref, far_ref, out_ref):
    heads = near_ref.shape[0]
    row = lax.broadcasted_iota(jnp.int32, (32, TILE), 0)
    lane = lax.broadcasted_iota(jnp.int32, (32, TILE), 1)
    bucket = [tile_bucket(delta, 0) for delta in (-1, 0, 1)]
    total = jnp.zeros((32, TILE), F32)
    for h in range(heads):
        near = [near_ref[h, d] for d in range(3)]
        for b in range(32):
            deltas = (0, 1) if b < 16 else (1, 2)
            part = sum(jnp.where(bucket[d] == b, near[d], 0.0) for d in deltas)
            part = jnp.sum(part.reshape(16, 8, TILE), axis=0)
            if b == 15:
                part = part + far_ref[h, 0]
            if b == 31:
                part = part + far_ref[h, 1]
            line = jnp.sum(part, axis=0, keepdims=True)
            total = jnp.where((row == b) & (lane == h), jnp.sum(line, axis=1, keepdims=True), total)
    out_ref[...] = total


def bias_grad(near, far):
    return pl.pallas_call(
        bias_grad_kernel,
        out_shape=jax.ShapeDtypeStruct((32, TILE), F32),
        name="bias_grad",
    )(near, far)


def attn_fwd_kernel(seg_ref, bias_ref, q_ref, k_ref, v_ref, tile_ref, o_ref, lse_ref, s_ref, p_ref, l_ref):
    length, width = q_ref.shape
    heads = width // 64
    n_tiles = length // TILE
    lane = lax.broadcasted_iota(jnp.int32, (1, width), 1)
    one_example = seg_ref[0, length - 1] == seg_ref[0, 0]

    def blocks(h, mask, spans):
        for lo, hi in spans:
            qh = jnp.where(mask, q_ref[lo:hi], jnp.zeros((), BF16))
            s_ref[lo:hi, lo:hi] = lax.dot_general(qh, k_ref[lo:hi], NT, preferred_element_type=F32)
            below = bias_ref[15, h]
            above = bias_ref[31, h]
            for i in range(lo // TILE, hi // TILE):
                rows = slice(i * TILE, (i + 1) * TILE)
                near = range(max(lo // TILE, i - 1), min(hi // TILE, i + 2))
                parts = {j: s_ref[rows, j * TILE : (j + 1) * TILE] for j in range(lo // TILE, hi // TILE)}
                top = None
                for j in near:
                    parts[j] = parts[j] + tile_ref[h, j - i + 1]
                    top = parts[j] if top is None else jnp.maximum(top, parts[j])
                for side, constant in ((range(lo // TILE, near[0]), below), (range(near[-1] + 1, hi // TILE), above)):
                    if len(side):
                        far = functools.reduce(jnp.maximum, [parts[j] for j in side])
                        top = jnp.maximum(top, far + constant)
                top = jnp.max(top, axis=1, keepdims=True)
                total = None
                for j, part in parts.items():
                    if j < near[0]:
                        shift = top - below
                    elif j > near[-1]:
                        shift = top - above
                    else:
                        shift = top
                    e = jnp.exp(part - shift)
                    total = e if total is None else total + e
                    p_ref[rows, j * TILE : (j + 1) * TILE] = e.astype(BF16)
                total = jnp.sum(total, axis=1, keepdims=True)
                l_ref[rows] = jnp.broadcast_to(1.0 / total, (TILE, TILE))
                lse = jnp.broadcast_to(top + jnp.log(total), (TILE, TILE))
                lse_ref[h, :, rows] = jnp.transpose(lse)[:8]
            oh = lax.dot_general(p_ref[lo:hi, lo:hi], v_ref[lo:hi], (((1,), (0,)), ((), ())), preferred_element_type=F32)
            scale = l_ref[lo:hi, :1]
            o_ref[lo:hi] = jnp.where(mask, (oh * scale).astype(BF16), o_ref[lo:hi])

    @pl.loop(0, heads)
    def _(h):
        mask = (lane // 64) == h

        @pl.when(one_example)
        def _():
            blocks(h, mask, ((0, length),))

        @pl.when(jnp.logical_not(one_example))
        def _():
            blocks(h, mask, tuple((lo, lo + SEG) for lo in range(0, length, SEG)))


def attn_fwd(seg, bias, q, k, v, tiles):
    length, width = q.shape
    heads = width // 64
    vmem = pl.BlockSpec(memory_space=pltpu.VMEM)
    smem = pl.BlockSpec(memory_space=pltpu.SMEM)
    return pl.pallas_call(
        attn_fwd_kernel,
        out_shape=(
            jax.ShapeDtypeStruct((length, width), BF16),
            jax.ShapeDtypeStruct((heads, 8, length), F32),
        ),
        in_specs=[smem, smem, vmem, vmem, vmem, vmem],
        out_specs=(vmem, vmem),
        scratch_shapes=[
            pltpu.VMEM((length, length), F32),
            pltpu.VMEM((length, length), BF16),
            pltpu.VMEM((length, TILE), F32),
        ],
        compiler_params=pltpu.CompilerParams(vmem_limit_bytes=40 << 20),
        cost_estimate=pl.CostEstimate(flops=20_000_000_000, bytes_accessed=4_000_000, transcendentals=5_000_000),
        name="attn_fwd",
    )(seg, bias, q, k, v, tiles)


def attn_bwd_kernel(
    seg_ref, bias_ref, q_ref, k_ref, v_ref, o_ref, do_ref, lse_ref, tile_ref,
    dq_ref, dk_ref, dv_ref, near_ref, far_ref,
    s_ref, dp_ref, p_ref, ds_ref, dsum_ref, kt_ref, dqt_ref, dka_ref, dva_ref,
):
    length, width = q_ref.shape
    heads = width // 64
    lane = lax.broadcasted_iota(jnp.int32, (1, width), 1)
    one_example = seg_ref[0, length - 1] == seg_ref[0, 0]
    kt_ref[...] = jnp.transpose(k_ref[...])
    prod = o_ref[...].astype(F32) * do_ref[...].astype(F32)
    high = prod.astype(BF16)
    low = (prod - high.astype(F32)).astype(BF16)
    head_rows = (
        lax.broadcasted_iota(jnp.int32, (8 * heads, width), 1) // 64
        == lax.broadcasted_iota(jnp.int32, (8 * heads, width), 0) // 8
    ).astype(BF16)
    dsum_ref[...] = lax.dot_general(head_rows, high, NT, preferred_element_type=F32) + lax.dot_general(
        head_rows, low, NT, preferred_element_type=F32
    )
    NN = (((1,), (0,)), ((), ()))

    def blocks(h, mask, spans):
        below = bias_ref[15, h]
        above = bias_ref[31, h]
        near_sum = [None, None, None]
        far_sum = [jnp.zeros((8, TILE), F32)] * 2
        zero = jnp.zeros((), BF16)
        for d in range(3):
            near_ref[h, d] = jnp.zeros((TILE, TILE), F32)
        for lo, hi in spans:
            qh = jnp.where(mask, q_ref[lo:hi], zero)
            dh = jnp.where(mask, do_ref[lo:hi], zero)
            s_ref[lo:hi, lo:hi] = lax.dot_general(k_ref[lo:hi], qh, NT, preferred_element_type=F32)
            dp_ref[lo:hi, lo:hi] = lax.dot_general(v_ref[lo:hi], dh, NT, preferred_element_type=F32)
            for i in range(lo // TILE, hi // TILE):
                cols = slice(i * TILE, (i + 1) * TILE)
                lse = lse_ref[h, 0:1, cols]
                dsum = dsum_ref[pl.ds(pl.multiple_of(h * 8, 8), 1), cols]
                for j in range(lo // TILE, hi // TILE):
                    rows = slice(j * TILE, (j + 1) * TILE)
                    s = s_ref[rows, cols]
                    if abs(j - i) <= 1:
                        e = jnp.exp(s + tile_ref[h, j - i + 1] - lse)
                    else:
                        e = jnp.exp(s - (lse - (below if j < i else above)))
                    ds = e * (dp_ref[rows, cols] - dsum)
                    p_ref[rows, cols] = e.astype(BF16)
                    ds_ref[rows, cols] = ds.astype(BF16)
                    if abs(j - i) <= 1:
                        near_ref[h, j - i + 1] += ds
                    else:
                        side = int(j > i)
                        far_sum[side] = far_sum[side] + jnp.sum(ds.reshape(TILE // 8, 8, TILE), axis=0)
            dv = lax.dot_general(p_ref[lo:hi, lo:hi], dh, NN, preferred_element_type=F32)
            dk = lax.dot_general(ds_ref[lo:hi, lo:hi], qh, NN, preferred_element_type=F32)
            dva_ref[lo:hi] = jnp.where(mask, dv, dva_ref[lo:hi])
            dka_ref[lo:hi] = jnp.where(mask, dk, dka_ref[lo:hi])
            head = pl.ds(pl.multiple_of(h * 64, 64), 64)
            dqt_ref[head, lo:hi] = lax.dot_general(
                kt_ref[head, lo:hi], ds_ref[lo:hi, lo:hi], NN, preferred_element_type=F32
            )
        far_ref[h, 0] = far_sum[0]
        far_ref[h, 1] = far_sum[1]

    @pl.loop(0, heads)
    def _(h):
        mask = (lane // 64) == h

        @pl.when(one_example)
        def _():
            blocks(h, mask, ((0, length),))

        @pl.when(jnp.logical_not(one_example))
        def _():
            blocks(h, mask, tuple((lo, lo + SEG) for lo in range(0, length, SEG)))

    dk_ref[...] = dka_ref[...].astype(BF16)
    dv_ref[...] = dva_ref[...].astype(BF16)
    dq_ref[...] = jnp.transpose(dqt_ref[...]).astype(BF16)


def attn_bwd(seg, bias, q, k, v, o, do, lse, tiles):
    length, width = q.shape
    heads = width // 64
    vmem = pl.BlockSpec(memory_space=pltpu.VMEM)
    smem = pl.BlockSpec(memory_space=pltpu.SMEM)
    grad = jax.ShapeDtypeStruct((length, width), BF16)
    return pl.pallas_call(
        attn_bwd_kernel,
        out_shape=(
            grad, grad, grad,
            jax.ShapeDtypeStruct((heads, 3, TILE, TILE), F32),
            jax.ShapeDtypeStruct((heads, 2, 8, TILE), F32),
        ),
        in_specs=[smem, smem] + [vmem] * 7,
        out_specs=(vmem,) * 5,
        scratch_shapes=[
            pltpu.VMEM((length, length), F32),
            pltpu.VMEM((length, length), F32),
            pltpu.VMEM((length, length), BF16),
            pltpu.VMEM((length, length), BF16),
            pltpu.VMEM((8 * heads, length), F32),
            pltpu.VMEM((width, length), BF16),
            pltpu.VMEM((width, length), F32),
            pltpu.VMEM((length, width), F32),
            pltpu.VMEM((length, width), F32),
        ],
        compiler_params=pltpu.CompilerParams(vmem_limit_bytes=48 << 20),
        cost_estimate=pl.CostEstimate(flops=40_000_000_000, bytes_accessed=6_000_000, transcendentals=5_000_000),
        name="attn_bwd",
    )(seg, bias, q, k, v, o, do, lse, tiles)


def rms_norm(values, gain):
    return values * lax.rsqrt(jnp.mean(values * values, axis=-1, keepdims=True) + EPSILON) * gain


def norm_back(values, gain, grad):
    _, back_fn = jax.vjp(rms_norm, values, gain)
    return back_fn(grad)


def gelu_mix(gate_preactivation, upward_preactivation):
    return jax.nn.gelu(gate_preactivation, approximate=True) * upward_preactivation


def local(
    tokens,
    segment_ids,
    norm1_gain,
    w_query,
    w_key,
    w_value,
    w_out,
    rel_bias,
    norm2_gain,
    gate_weight_matrix,
    upward_weight,
    downward_weight,
    cotangent,
):
    shard_len, rows_here, model_width = tokens.shape
    length = segment_ids.shape[1]
    num_buckets, heads_here = rel_bias.shape
    head_dim = w_query.shape[1] // heads_here
    row_tiles, col_tiles = bias_tiles(rel_bias)
    x_in = tokens.astype(jnp.float32)
    norm_one = rms_norm(x_in, norm1_gain).astype(jnp.bfloat16)
    full_one = lax.all_gather(norm_one, "tensor", axis=0, tiled=True)

    def project(weight):
        return jnp.einsum(
            "trd,dc->rtc", full_one, weight, preferred_element_type=jnp.float32
        ).astype(jnp.bfloat16)

    q = project(w_query)
    k = project(w_key)
    v = project(w_value)
    mixed, lse = attn_fwd(segment_ids, rel_bias, q[0], k[0], v[0], row_tiles)
    mixed_flat = mixed[None]
    portion = lax.slice_in_dim(mixed_flat, 0, shard_len * lax.axis_size("tensor"), axis=1)
    attn_sum = lax.psum_scatter(
        jnp.einsum("rtc,cd->trd", portion, w_out, preferred_element_type=jnp.float32).astype(
            jnp.bfloat16
        ),
        "tensor",
        scatter_dimension=0,
        tiled=True,
    ).astype(jnp.float32)
    hidden_in = x_in + attn_sum
    norm_two = rms_norm(hidden_in, norm2_gain).astype(jnp.bfloat16)
    whole_second = lax.all_gather(norm_two, "tensor", axis=0, tiled=True)
    gate_preactivation = jnp.einsum(
        "hzo,on->hzn", whole_second, gate_weight_matrix, preferred_element_type=jnp.float32
    )
    upward_preactivation = jnp.einsum(
        "hzo,on->hzn", whole_second, upward_weight, preferred_element_type=jnp.float32
    )
    hidden_state = gelu_mix(gate_preactivation, upward_preactivation).astype(jnp.bfloat16)
    portion = lax.slice_in_dim(hidden_state, 0, lax.axis_size("tensor") * shard_len, axis=0)
    ffn_sum = lax.psum_scatter(
        jnp.einsum(
            "kwc,cn->kwn", portion, downward_weight, preferred_element_type=jnp.float32
        ).astype(jnp.bfloat16),
        "tensor",
        scatter_dimension=0,
        tiled=True,
    ).astype(jnp.float32)
    out_value = hidden_in + ffn_sum
    out_tokens = out_value.astype(jnp.bfloat16)
    stat_parts = jnp.stack(
        [jnp.sum(attn_sum * attn_sum), jnp.sum(ffn_sum * ffn_sum), jnp.sum(out_value * out_value)]
    )
    _, mix_back = jax.vjp(gelu_mix, gate_preactivation, upward_preactivation)
    cotangent_whole = lax.all_gather(cotangent, "tensor", axis=0, tiled=True)
    downward_weight_gradient = jnp.einsum(
        "kpo,kpb->ob", hidden_state, cotangent_whole, preferred_element_type=jnp.float32
    )
    hidden_gradient = jnp.einsum(
        "gqm,zm->gqz", cotangent_whole, downward_weight, preferred_element_type=jnp.float32
    )
    d_gate_f, d_up_f = mix_back(hidden_gradient)
    gate_gradient = d_gate_f.astype(jnp.bfloat16)
    upward_gradient = d_up_f.astype(jnp.bfloat16)
    gate_weight_gradient = jnp.einsum(
        "zyv,zya->va", whole_second, gate_gradient, preferred_element_type=jnp.float32
    )
    upward_weight_gradient = jnp.einsum(
        "zyv,zya->va", whole_second, upward_gradient, preferred_element_type=jnp.float32
    )
    row_count = lax.axis_size("tensor") * shard_len
    gate_portion = lax.slice_in_dim(gate_gradient, 0, row_count, axis=0)
    upward_portion = lax.slice_in_dim(upward_gradient, 0, row_count, axis=0)
    d_norm_two = lax.psum_scatter(
        (
            jnp.einsum(
                "xas,ks->xak", gate_portion, gate_weight_matrix, preferred_element_type=jnp.float32
            )
            + jnp.einsum(
                "xas,ks->xak", upward_portion, upward_weight, preferred_element_type=jnp.float32
            )
        ).astype(jnp.bfloat16),
        "tensor",
        scatter_dimension=0,
        tiled=True,
    ).astype(jnp.float32)
    d_from_two, grad_two_part = norm_back(hidden_in, norm2_gain, d_norm_two)
    d_hidden_in = cotangent.astype(jnp.float32) + d_from_two
    d_attn = d_hidden_in.astype(jnp.bfloat16)
    d_attn_full = lax.all_gather(d_attn, "tensor", axis=0, tiled=True)
    grad_out = jnp.einsum(
        "rtc,trd->cd", mixed_flat, d_attn_full, preferred_element_type=jnp.float32
    )
    d_mixed = jnp.einsum(
        "trd,cd->rtc", d_attn_full, w_out, preferred_element_type=jnp.float32
    ).astype(jnp.bfloat16)
    dq, dk, dv, near, far = attn_bwd(
        segment_ids, rel_bias, q[0], k[0], v[0], mixed, d_mixed[0], lse, col_tiles
    )
    grad_bias = bias_grad(near, far)[:, :heads_here]
    dq_flat, dk_flat, dv_flat = dq[None], dk[None], dv[None]
    grad_query = jnp.einsum("trd,rtc->dc", full_one, dq_flat, preferred_element_type=jnp.float32)
    grad_key = jnp.einsum("trd,rtc->dc", full_one, dk_flat, preferred_element_type=jnp.float32)
    grad_value = jnp.einsum("trd,rtc->dc", full_one, dv_flat, preferred_element_type=jnp.float32)
    row_count = lax.axis_size("tensor") * shard_len
    term_sum = jnp.einsum(
        "rtc,dc->trd",
        lax.slice_in_dim(dq_flat, 0, row_count, axis=1),
        w_query,
        preferred_element_type=jnp.float32,
    )
    term_sum = term_sum + jnp.einsum(
        "rtc,dc->trd",
        lax.slice_in_dim(dk_flat, 0, row_count, axis=1),
        w_key,
        preferred_element_type=jnp.float32,
    )
    d_norm_one = lax.psum_scatter(
        (
            term_sum
            + jnp.einsum(
                "rtc,dc->trd",
                lax.slice_in_dim(dv_flat, 0, row_count, axis=1),
                w_value,
                preferred_element_type=jnp.float32,
            )
        ).astype(jnp.bfloat16),
        "tensor",
        scatter_dimension=0,
        tiled=True,
    ).astype(jnp.float32)
    d_from_one, grad_one_part = norm_back(x_in, norm1_gain, d_norm_one)
    grad_tokens = (d_hidden_in + d_from_one).astype(jnp.bfloat16)
    big = (
        grad_query,
        grad_key,
        grad_value,
        grad_out,
        gate_weight_gradient,
        upward_weight_gradient,
        downward_weight_gradient,
    )
    big = lax.psum(tuple(g.astype(jnp.bfloat16) for g in big), "dp")
    (
        grad_query,
        grad_key,
        grad_value,
        grad_out,
        gate_weight_gradient,
        upward_weight_gradient,
        downward_weight_gradient,
    ) = (g.astype(jnp.float32) for g in big)
    grad_bias = lax.psum(grad_bias, "dp")
    grad_norm1, grad_norm2, stat_sums = lax.psum(
        (grad_one_part, grad_two_part, stat_parts), ("dp", "tensor")
    )
    element_count = (
        shard_len * rows_here * model_width * lax.axis_size("dp") * lax.axis_size("tensor")
    )
    rms_stats = jnp.sqrt(stat_sums / element_count)
    return (
        out_tokens,
        grad_tokens,
        grad_norm1,
        grad_query,
        grad_key,
        grad_value,
        grad_out,
        grad_bias,
        grad_norm2,
        gate_weight_gradient,
        upward_weight_gradient,
        downward_weight_gradient,
        rms_stats,
    )


def solution(mesh):
    in_specs = (
        P("tensor", "dp", None),
        P("dp", None),
        P(),
        P(None, "tensor"),
        P(None, "tensor"),
        P(None, "tensor"),
        P("tensor", None),
        P(None, "tensor"),
        P(),
        P(None, "tensor"),
        P(None, "tensor"),
        P("tensor", None),
        P("tensor", "dp", None),
    )
    out_specs = (
        P("tensor", "dp", None),
        P("tensor", "dp", None),
        P(),
        P(None, "tensor"),
        P(None, "tensor"),
        P(None, "tensor"),
        P("tensor", None),
        P(None, "tensor"),
        P(),
        P(None, "tensor"),
        P(None, "tensor"),
        P("tensor", None),
        P(),
    )
    return jax.shard_map(local, mesh=mesh, in_specs=in_specs, out_specs=out_specs, check_vma=False)
```

```python
import functools
import jax
import jax.numpy as jnp
from jax import lax
from jax.experimental import pallas as pl
from jax.experimental.pallas import tpu as pltpu
from jax.sharding import PartitionSpec as P

EPSILON = 1e-06
THRESHOLDS = (12, 16, 23, 32, 46, 64, 91)
TILE = 128
SEG = 384
NT = (((1,), (1,)), ((), ()))
NN = (((1,), (0,)), ((), ()))
TN = (((0,), (0,)), ((), ()))
F32 = jnp.float32
BF16 = jnp.bfloat16


def bucket_of(offset):
    distance = jnp.abs(offset)
    far_bucket = 8 + sum(((distance >= threshold).astype(jnp.int32) for threshold in THRESHOLDS))
    return jnp.where(distance < 8, distance, far_bucket) + 16 * (offset > 0).astype(jnp.int32)


def tile_bucket(delta, key_axis):
    keys = lax.broadcasted_iota(jnp.int32, (TILE, TILE), key_axis)
    queries = lax.broadcasted_iota(jnp.int32, (TILE, TILE), 1 - key_axis)
    return bucket_of(TILE * delta + keys - queries)


def bias_tiles_kernel(bias_ref, rows_ref, cols_ref):
    buckets, heads = bias_ref.shape
    for out_ref, key_axis in ((rows_ref, 1), (cols_ref, 0)):
        for delta in (-1, 0, 1):
            bucket = tile_bucket(delta, key_axis)
            tiles = [jnp.zeros((TILE, TILE), F32) for _ in range(heads)]
            for b in range(buckets):
                hit = bucket == b
                tiles = [jnp.where(hit, bias_ref[b, h], t) for h, t in enumerate(tiles)]
            for h in range(heads):
                out_ref[h, delta + 1] = tiles[h]


def bias_tiles(rel_bias):
    heads = rel_bias.shape[1]
    shape = jax.ShapeDtypeStruct((heads, 3, TILE, TILE), F32)
    return pl.pallas_call(
        bias_tiles_kernel,
        out_shape=(shape, shape),
        in_specs=[pl.BlockSpec(memory_space=pltpu.SMEM)],
        out_specs=(pl.BlockSpec(memory_space=pltpu.VMEM),) * 2,
        name="bias_tiles",
    )(rel_bias)


def bias_grad_kernel(near_ref, far_ref, out_ref):
    heads = near_ref.shape[0]
    row = lax.broadcasted_iota(jnp.int32, (32, TILE), 0)
    lane = lax.broadcasted_iota(jnp.int32, (32, TILE), 1)
    bucket = [tile_bucket(delta, 0) for delta in (-1, 0, 1)]
    total = jnp.zeros((32, TILE), F32)
    for h in range(heads):
        near = [near_ref[h, d] for d in range(3)]
        for b in range(32):
            deltas = (0, 1) if b < 16 else (1, 2)
            part = sum(jnp.where(bucket[d] == b, near[d], 0.0) for d in deltas)
            part = jnp.sum(part.reshape(16, 8, TILE), axis=0)
            if b == 15:
                part = part + far_ref[h, 0]
            if b == 31:
                part = part + far_ref[h, 1]
            line = jnp.sum(part, axis=0, keepdims=True)
            total = jnp.where((row == b) & (lane == h), jnp.sum(line, axis=1, keepdims=True), total)
    out_ref[...] = total


def bias_grad(near, far):
    return pl.pallas_call(
        bias_grad_kernel,
        out_shape=jax.ShapeDtypeStruct((32, TILE), F32),
        name="bias_grad",
    )(near, far)


def attn_fwd_kernel(seg_ref, bias_ref, qkv_ref, tile_ref, o_ref, lse_ref, s_ref, p_ref, l_ref):
    length, width = o_ref.shape
    q_ref, k_ref, v_ref = (qkv_ref.at[:, n * width : (n + 1) * width] for n in range(3))
    heads = width // 64
    n_tiles = length // TILE
    lane = lax.broadcasted_iota(jnp.int32, (1, width), 1)
    one_example = seg_ref[0, length - 1] == seg_ref[0, 0]

    def blocks(h, mask, spans):
        for lo, hi in spans:
            qh = jnp.where(mask, q_ref[lo:hi], jnp.zeros((), BF16))
            s_ref[lo:hi, lo:hi] = lax.dot_general(qh, k_ref[lo:hi], NT, preferred_element_type=F32)
            below = bias_ref[15, h]
            above = bias_ref[31, h]
            for i in range(lo // TILE, hi // TILE):
                rows = slice(i * TILE, (i + 1) * TILE)
                near = range(max(lo // TILE, i - 1), min(hi // TILE, i + 2))
                parts = {j: s_ref[rows, j * TILE : (j + 1) * TILE] for j in range(lo // TILE, hi // TILE)}
                top = None
                for j in near:
                    parts[j] = parts[j] + tile_ref[h, j - i + 1]
                    top = parts[j] if top is None else jnp.maximum(top, parts[j])
                for side, constant in ((range(lo // TILE, near[0]), below), (range(near[-1] + 1, hi // TILE), above)):
                    if len(side):
                        far = functools.reduce(jnp.maximum, [parts[j] for j in side])
                        top = jnp.maximum(top, far + constant)
                top = jnp.max(top, axis=1, keepdims=True)
                total = None
                for j, part in parts.items():
                    if j < near[0]:
                        shift = top - below
                    elif j > near[-1]:
                        shift = top - above
                    else:
                        shift = top
                    e = jnp.exp(part - shift)
                    total = e if total is None else total + e
                    p_ref[rows, j * TILE : (j + 1) * TILE] = e.astype(BF16)
                total = jnp.sum(total, axis=1, keepdims=True)
                l_ref[rows] = jnp.broadcast_to(1.0 / total, (TILE, TILE))
                lse = jnp.broadcast_to(top + jnp.log(total), (TILE, TILE))
                lse_ref[h, :, rows] = jnp.transpose(lse)[:8]
            oh = lax.dot_general(p_ref[lo:hi, lo:hi], v_ref[lo:hi], (((1,), (0,)), ((), ())), preferred_element_type=F32)
            scale = l_ref[lo:hi, :1]
            o_ref[lo:hi] = jnp.where(mask, (oh * scale).astype(BF16), o_ref[lo:hi])

    @pl.loop(0, heads)
    def _(h):
        mask = (lane // 64) == h

        @pl.when(one_example)
        def _():
            blocks(h, mask, ((0, length),))

        @pl.when(jnp.logical_not(one_example))
        def _():
            blocks(h, mask, tuple((lo, lo + SEG) for lo in range(0, length, SEG)))


def attn_fwd(seg, bias, qkv, tiles):
    length, width = qkv.shape[0], qkv.shape[1] // 3
    heads = width // 64
    vmem = pl.BlockSpec(memory_space=pltpu.VMEM)
    smem = pl.BlockSpec(memory_space=pltpu.SMEM)
    return pl.pallas_call(
        attn_fwd_kernel,
        out_shape=(
            jax.ShapeDtypeStruct((length, width), BF16),
            jax.ShapeDtypeStruct((heads, 8, length), F32),
        ),
        in_specs=[smem, smem, vmem, vmem],
        out_specs=(vmem, vmem),
        scratch_shapes=[
            pltpu.VMEM((length, length), F32),
            pltpu.VMEM((length, length), BF16),
            pltpu.VMEM((length, TILE), F32),
        ],
        compiler_params=pltpu.CompilerParams(vmem_limit_bytes=40 << 20),
        cost_estimate=pl.CostEstimate(flops=20_000_000_000, bytes_accessed=4_000_000, transcendentals=5_000_000),
        name="attn_fwd",
    )(seg, bias, qkv, tiles)


def attn_bwd_kernel(
    seg_ref, bias_ref, qkv_ref, o_ref, do_ref, lse_ref, tile_ref,
    dqkv_ref, near_ref, far_ref,
    s_ref, dp_ref, p_ref, ds_ref, dsum_ref, kt_ref, dqt_ref, dka_ref, dva_ref,
):
    length, width = o_ref.shape
    q_ref, k_ref, v_ref = (qkv_ref.at[:, n * width : (n + 1) * width] for n in range(3))
    heads = width // 64
    lane = lax.broadcasted_iota(jnp.int32, (1, width), 1)
    one_example = seg_ref[0, length - 1] == seg_ref[0, 0]
    kt_ref[...] = jnp.transpose(k_ref[...])
    prod = o_ref[...].astype(F32) * do_ref[...].astype(F32)
    high = prod.astype(BF16)
    low = (prod - high.astype(F32)).astype(BF16)
    head_rows = (
        lax.broadcasted_iota(jnp.int32, (8 * heads, width), 1) // 64
        == lax.broadcasted_iota(jnp.int32, (8 * heads, width), 0) // 8
    ).astype(BF16)
    dsum_ref[...] = lax.dot_general(head_rows, high, NT, preferred_element_type=F32) + lax.dot_general(
        head_rows, low, NT, preferred_element_type=F32
    )
    def blocks(h, mask, spans):
        below = bias_ref[15, h]
        above = bias_ref[31, h]
        near_sum = [None, None, None]
        far_sum = [jnp.zeros((8, TILE), F32)] * 2
        zero = jnp.zeros((), BF16)
        for d in range(3):
            near_ref[h, d] = jnp.zeros((TILE, TILE), F32)
        for lo, hi in spans:
            qh = jnp.where(mask, q_ref[lo:hi], zero)
            dh = jnp.where(mask, do_ref[lo:hi], zero)
            s_ref[lo:hi, lo:hi] = lax.dot_general(k_ref[lo:hi], qh, NT, preferred_element_type=F32)
            dp_ref[lo:hi, lo:hi] = lax.dot_general(v_ref[lo:hi], dh, NT, preferred_element_type=F32)
            for i in range(lo // TILE, hi // TILE):
                cols = slice(i * TILE, (i + 1) * TILE)
                lse = lse_ref[h, 0:1, cols]
                dsum = dsum_ref[pl.ds(pl.multiple_of(h * 8, 8), 1), cols]
                for j in range(lo // TILE, hi // TILE):
                    rows = slice(j * TILE, (j + 1) * TILE)
                    s = s_ref[rows, cols]
                    if abs(j - i) <= 1:
                        e = jnp.exp(s + tile_ref[h, j - i + 1] - lse)
                    else:
                        e = jnp.exp(s - (lse - (below if j < i else above)))
                    ds = e * (dp_ref[rows, cols] - dsum)
                    p_ref[rows, cols] = e.astype(BF16)
                    ds_ref[rows, cols] = ds.astype(BF16)
                    if abs(j - i) <= 1:
                        near_ref[h, j - i + 1] += ds
                    else:
                        side = int(j > i)
                        far_sum[side] = far_sum[side] + jnp.sum(ds.reshape(TILE // 8, 8, TILE), axis=0)
            dv = lax.dot_general(p_ref[lo:hi, lo:hi], dh, NN, preferred_element_type=F32)
            dk = lax.dot_general(ds_ref[lo:hi, lo:hi], qh, NN, preferred_element_type=F32)
            dva_ref[lo:hi] = jnp.where(mask, dv, dva_ref[lo:hi])
            dka_ref[lo:hi] = jnp.where(mask, dk, dka_ref[lo:hi])
            head = pl.ds(pl.multiple_of(h * 64, 64), 64)
            dqt_ref[head, lo:hi] = lax.dot_general(
                kt_ref[head, lo:hi], ds_ref[lo:hi, lo:hi], NN, preferred_element_type=F32
            )
        far_ref[h, 0] = far_sum[0]
        far_ref[h, 1] = far_sum[1]

    @pl.loop(0, heads)
    def _(h):
        mask = (lane // 64) == h

        @pl.when(one_example)
        def _():
            blocks(h, mask, ((0, length),))

        @pl.when(jnp.logical_not(one_example))
        def _():
            blocks(h, mask, tuple((lo, lo + SEG) for lo in range(0, length, SEG)))

    dqkv_ref[:, :width] = jnp.transpose(dqt_ref[...]).astype(BF16)
    dqkv_ref[:, width : 2 * width] = dka_ref[...].astype(BF16)
    dqkv_ref[:, 2 * width :] = dva_ref[...].astype(BF16)


def attn_bwd(seg, bias, qkv, o, do, lse, tiles):
    length, width = o.shape
    heads = width // 64
    vmem = pl.BlockSpec(memory_space=pltpu.VMEM)
    smem = pl.BlockSpec(memory_space=pltpu.SMEM)
    return pl.pallas_call(
        attn_bwd_kernel,
        out_shape=(
            jax.ShapeDtypeStruct((length, 3 * width), BF16),
            jax.ShapeDtypeStruct((heads, 3, TILE, TILE), F32),
            jax.ShapeDtypeStruct((heads, 2, 8, TILE), F32),
        ),
        in_specs=[smem, smem] + [vmem] * 5,
        out_specs=(vmem,) * 3,
        scratch_shapes=[
            pltpu.VMEM((length, length), F32),
            pltpu.VMEM((length, length), F32),
            pltpu.VMEM((length, length), BF16),
            pltpu.VMEM((length, length), BF16),
            pltpu.VMEM((8 * heads, length), F32),
            pltpu.VMEM((width, length), BF16),
            pltpu.VMEM((width, length), F32),
            pltpu.VMEM((length, width), F32),
            pltpu.VMEM((length, width), F32),
        ],
        compiler_params=pltpu.CompilerParams(vmem_limit_bytes=48 << 20),
        cost_estimate=pl.CostEstimate(flops=40_000_000_000, bytes_accessed=6_000_000, transcendentals=5_000_000),
        name="attn_bwd",
    )(seg, bias, qkv, o, do, lse, tiles)


def tanh_gelu(u):
    scale = 0.7978845608028654
    t = jnp.tanh(scale * (u + 0.044715 * (u * u * u)))
    half = 0.5 * (1.0 + t)
    slope = half + (0.5 * u) * (1.0 - t * t) * (scale * (1.0 + 0.134145 * (u * u)))
    return u * half, slope


def ffn_kernel(
    where_ref, x_ref, c_ref, mine_ref, other_ref,
    dtwo_ref, ffo_ref, hidden_ref, dgate_ref, dup_ref,
    gate_w, up_w, down_w, sems,
):
    core = where_ref[0]
    ring, rows, half = mine_ref.shape
    units = rows // 3
    scratches = (gate_w, up_w, down_w)
    copies = [[], [], []]
    for m in range(3):
        for q in range(ring):
            for n, ref in enumerate((mine_ref, other_ref)):
                start = pl.multiple_of((core ^ n) * half, 128)
                copies[m].append(
                    pltpu.make_async_copy(
                        ref.at[q, m * units : (m + 1) * units],
                        scratches[m].at[q * units : (q + 1) * units, pl.ds(start, half)],
                        sems.at[m, 2 * q + n],
                    )
                )
    for group in copies:
        for copy in group:
            copy.start()
    for copy in copies[0]:
        copy.wait()
    gate = lax.dot_general(x_ref[...], gate_w[...], NT, preferred_element_type=F32)
    for copy in copies[1]:
        copy.wait()
    up = lax.dot_general(x_ref[...], up_w[...], NT, preferred_element_type=F32)
    for copy in copies[2]:
        copy.wait()
    d_hidden = lax.dot_general(c_ref[...], down_w[...], NT, preferred_element_type=F32)
    value, slope = tanh_gelu(gate)
    hidden = (value * up).astype(BF16)
    d_gate = (d_hidden * up * slope).astype(BF16)
    d_up = (d_hidden * value).astype(BF16)
    hidden_ref[...] = hidden
    dgate_ref[...] = d_gate
    dup_ref[...] = d_up
    dtwo_ref[...] = (
        lax.dot_general(d_gate, gate_w[...], NN, preferred_element_type=F32)
        + lax.dot_general(d_up, up_w[...], NN, preferred_element_type=F32)
    ).astype(dtwo_ref.dtype)
    ffo_ref[...] = lax.dot_general(hidden, down_w[...], NN, preferred_element_type=F32).astype(ffo_ref.dtype)


def ffn(where, x, c, mine, other):
    tokens, width = x.shape
    ring, rows, half = mine.shape
    units = ring * rows // 3
    vmem = pl.BlockSpec(memory_space=pltpu.VMEM)
    anywhere = pl.BlockSpec(memory_space=pl.ANY)
    wide = jax.ShapeDtypeStruct((tokens, width), BF16)
    inner = jax.ShapeDtypeStruct((tokens, units), BF16)
    return pl.pallas_call(
        ffn_kernel,
        out_shape=(wide, wide, inner, inner, inner),
        in_specs=[pl.BlockSpec(memory_space=pltpu.SMEM), vmem, vmem, anywhere, anywhere],
        out_specs=(vmem,) * 5,
        scratch_shapes=[pltpu.VMEM((units, width), BF16)] * 3 + [pltpu.SemaphoreType.DMA((3, 2 * ring))],
        compiler_params=pltpu.CompilerParams(vmem_limit_bytes=40 << 20),
        cost_estimate=pl.CostEstimate(
            flops=16 * tokens * width * units, bytes_accessed=6 * units * width + 10 * tokens * width, transcendentals=tokens * units
        ),
        name="ffn",
    )(where, x, c, mine, other)


def ffn_grads_kernel(n, where_ref, *refs):
    sources = [refs[i * n : (i + 1) * n] for i in range(5)]
    keep_ref, give_ref = refs[5 * n : 5 * n + 2]
    held = refs[5 * n + 2 : 5 * n + 7]
    sems = refs[5 * n + 7]
    core = where_ref[0]
    ring, _, units, half = keep_ref.shape
    rows = sources[0][0].shape[0]
    copies = [
        [
            pltpu.make_async_copy(ref, target.at[j * rows : (j + 1) * rows], sems.at[i, j])
            for j, ref in enumerate(group)
        ]
        for i, (group, target) in enumerate(zip(sources, held))
    ]
    for group in copies:
        for copy in group:
            copy.start()
    waited = set()
    for m, (lhs, rhs) in ((2, (0, 1)), (0, (2, 3)), (1, (4, 3))):
        for i in (lhs, rhs):
            if i not in waited:
                waited.add(i)
                for copy in copies[i]:
                    copy.wait()
        for n_half, out_ref in enumerate((give_ref, keep_ref)):
            start = pl.multiple_of((core ^ (1 - n_half)) * half, 128)
            grad = lax.dot_general(
                held[lhs][...], held[rhs][:, pl.ds(start, half)], TN, preferred_element_type=F32
            ).astype(BF16)
            for q in range(ring):
                out_ref[q, m] = grad[q * units : (q + 1) * units]


def ffn_grads(where, hs, cs, gs, xs, us, ring):
    rows, width = xs[0].shape
    units = hs[0].shape[1]
    n = len(xs)
    vmem = pl.BlockSpec(memory_space=pltpu.VMEM)
    anywhere = pl.BlockSpec(memory_space=pl.ANY)
    shape = jax.ShapeDtypeStruct((ring, 3, units // ring, width // 2), BF16)
    wide, inner = pltpu.VMEM((n * rows, width), BF16), pltpu.VMEM((n * rows, units), BF16)
    return pl.pallas_call(
        functools.partial(ffn_grads_kernel, n),
        out_shape=(shape, shape),
        in_specs=[pl.BlockSpec(memory_space=pltpu.SMEM)] + [anywhere] * (5 * n),
        out_specs=(vmem, vmem),
        scratch_shapes=[inner, wide, inner, wide, inner, pltpu.SemaphoreType.DMA((5, n))],
        compiler_params=pltpu.CompilerParams(vmem_limit_bytes=48 << 20),
        cost_estimate=pl.CostEstimate(
            flops=6 * n * rows * width * units, bytes_accessed=4 * n * rows * width + 6 * n * rows * units, transcendentals=0
        ),
        name="ffn_grads",
    )(where, *hs, *cs, *gs, *xs, *us)


def place_kernel(masks, where_ref, own_ref, other_ref, gate_ref, up_ref, down_ref):
    core, chip = where_ref[0], where_ref[1]
    _, _, units, half = own_ref.shape
    for m, out_ref in enumerate((gate_ref, up_ref, down_ref)):
        for r, mask in enumerate(masks):
            rows = pl.ds(pl.multiple_of((chip ^ mask) * units, 8), units)
            for n, ref in enumerate((own_ref, other_ref)):
                columns = pl.ds(pl.multiple_of((core ^ n) * half, 128), half)
                out_ref[rows, columns] = ref[r, m].astype(F32)


def place(where, own, other, masks):
    _, _, units, half = own.shape
    vmem = pl.BlockSpec(memory_space=pltpu.VMEM)
    shape = jax.ShapeDtypeStruct((4 * units, 2 * half), F32)
    return pl.pallas_call(
        functools.partial(place_kernel, masks),
        out_shape=(shape,) * 3,
        in_specs=[pl.BlockSpec(memory_space=pltpu.SMEM), vmem, vmem],
        out_specs=(vmem,) * 3,
        compiler_params=pltpu.CompilerParams(vmem_limit_bytes=40 << 20),
        cost_estimate=pl.CostEstimate(flops=0, bytes_accessed=12 * own.size * 2, transcendentals=0),
        name="place",
    )(where, own, other)


def place_rows_kernel(masks, where_ref, pieces_ref, *out_refs):
    _, rows, width = pieces_ref.shape
    part = width // len(out_refs)
    for r, mask in enumerate(masks):
        target = pl.ds(pl.multiple_of((where_ref[2] ^ mask) * rows, 8), rows)
        value = pieces_ref[r].astype(F32)
        for i, out_ref in enumerate(out_refs):
            out_ref[target] = value[:, i * part : (i + 1) * part]


def place_rows(where, pieces, masks, n_out):
    count, rows, width = pieces.shape
    vmem = pl.BlockSpec(memory_space=pltpu.VMEM)
    return pl.pallas_call(
        functools.partial(place_rows_kernel, masks),
        out_shape=(jax.ShapeDtypeStruct((count * rows, width // n_out), F32),) * n_out,
        in_specs=[pl.BlockSpec(memory_space=pltpu.SMEM), vmem],
        out_specs=(vmem,) * n_out,
        cost_estimate=pl.CostEstimate(flops=0, bytes_accessed=6 * pieces.size, transcendentals=0),
        name="place_rows",
    )(where, pieces)


def swap(value, mask):
    size = lax.axis_size("dp")
    return lax.ppermute(value, "dp", [(i, i ^ mask) for i in range(size)])


def shift(value, step):
    size = lax.axis_size("tensor")
    return lax.ppermute(value, "tensor", [(i, (i + step) % size) for i in range(size)])


def add(left, right):
    return (left.astype(F32) + right.astype(F32)).astype(BF16)


def after(value, *others):
    return lax.optimization_barrier((value, *others))[0]


def bits_from(first):
    bit = first
    while bit < lax.axis_size("dp"):
        yield bit
        bit *= 2


def gather_all(piece):
    pieces, masks = piece[None], [0]
    for bit in (*bits_from(2), 1):
        pieces = jnp.concatenate([pieces, swap(pieces, bit)], axis=0)
        masks = masks + [mask | bit for mask in masks]
    return pieces, tuple(masks)


def sum_rows(value):
    for bit in bits_from(1):
        value = value + swap(value, bit)
    return value


def sum_ring(value):
    return value + shift(value, 1) + shift(value, 2) + shift(value, 3)


def dot(left, right, dims=NN):
    return lax.dot_general(left, right, dims, preferred_element_type=F32)


def inverse_rms(values):
    return lax.rsqrt(jnp.mean(values * values, axis=-1, keepdims=True) + EPSILON)


CHIPS = (0, 1, 2, 3)


def to_chips(value):
    return [value] + [swap(value, 2 * mask) for mask in CHIPS[1:]]


def local(
    tokens,
    segment_ids,
    norm1_gain,
    w_query,
    w_key,
    w_value,
    w_out,
    rel_bias,
    norm2_gain,
    gate_weight_matrix,
    upward_weight,
    downward_weight,
    cotangent,
):
    shard, rows_here, width = tokens.shape
    length = segment_ids.shape[1]
    heads = rel_bias.shape[1]
    feats = w_query.shape[1]
    units = downward_weight.shape[0]
    ring = lax.axis_size("tensor")
    n_dp = lax.axis_size("dp")
    z = lax.axis_index("tensor")
    dp = lax.axis_index("dp")
    core = dp & 1
    chip = (dp >> 1) & 3
    where = jnp.stack([core, chip, dp]).astype(jnp.int32)

    x_low = tokens.reshape(shard, width)
    cot = cotangent.reshape(shard, width)
    row_tiles, col_tiles = bias_tiles(rel_bias)
    w_qkv = jnp.concatenate([w_query, w_key, w_value], axis=1)

    blocks = [x_low]
    blocks.append(shift(blocks[-1], 1))
    blocks.append(shift(blocks[-1], 1))
    cs = to_chips(cot)
    blocks.append(shift(after(blocks[-1], *cs), 1))
    out_rows = feats // n_dp
    out_piece = lax.dynamic_slice_in_dim(w_out, dp * out_rows, out_rows, 0)
    out_ring = lax.all_to_all(jnp.broadcast_to(out_piece, (ring, *out_piece.shape)), "tensor", 0, 0, tiled=True)
    out_ring = after(out_ring, *cs)
    out_all = lax.all_to_all(jnp.broadcast_to(out_ring, (n_dp, *out_ring.shape)), "dp", 0, 0, tiled=True)
    out_all = jnp.moveaxis(out_all, 0, 1).reshape(ring * feats, width)

    def unit_rows(array):
        return lax.dynamic_slice(array, (chip * (units // 4), core * (width // 2)), (units // 4, width // 2))

    pack = jnp.concatenate(
        [
            unit_rows(jnp.transpose(gate_weight_matrix)),
            unit_rows(jnp.transpose(upward_weight)),
            unit_rows(downward_weight),
        ],
        axis=0,
    )
    mine_w = lax.all_gather(after(pack, blocks[2]), "tensor", axis=0)
    other_w = swap(mine_w, 1)

    qkv = jnp.zeros((length, 3 * feats), BF16)
    norm_full = jnp.zeros((length, width), BF16)
    for s, block in enumerate(blocks):
        values = block.astype(F32)
        normed = (values * inverse_rms(values) * norm1_gain).astype(BF16)
        start = ((z - s) % ring) * shard
        norm_full = lax.dynamic_update_slice_in_dim(norm_full, normed, start, 0)
        qkv = lax.dynamic_update_slice_in_dim(qkv, dot(normed, w_qkv).astype(BF16), start, 0)

    o_row, lse = attn_fwd(segment_ids, rel_bias, qkv, row_tiles)
    o_home = lax.all_to_all(o_row, "tensor", 0, 1, tiled=True)
    attn = dot(o_home, out_all)
    x_one = x_low.astype(F32) + attn
    r_two = inverse_rms(x_one)
    norm_two = (x_one * r_two * norm2_gain).astype(BF16)

    xs = to_chips(norm_two)
    parts = [ffn(where, x, c, mine_w, other_w) for x, c in zip(xs, cs)]

    keep, give = ffn_grads(
        where, [part[2] for part in parts], cs, [part[3] for part in parts], xs, [part[4] for part in parts], ring
    )

    def sum_chips(terms):
        total = terms[0].astype(F32)
        for mask in CHIPS[1:]:
            total = total + swap(terms[mask], 2 * mask).astype(F32)
        return total

    d_two = sum_chips([after(parts[0][0], keep)] + [part[0] for part in parts[1:]])
    u_two = d_two * norm2_gain
    d_x_one = cot.astype(F32) + r_two * u_two - x_one * (
        r_two * r_two * r_two * jnp.mean(u_two * x_one, axis=-1, keepdims=True)
    )
    d_attn = d_x_one.astype(BF16)
    d_o = dot(d_attn, out_all, NT).astype(BF16)
    do_row = lax.all_to_all(d_o, "tensor", 1, 0, tiled=True)
    ffo = sum_chips([after(part[1], d_o) for part in parts])
    y = x_one + ffo
    out_tokens = y.astype(BF16)
    grad_two = jnp.sum(d_two * x_one * r_two, axis=0)
    stats = jnp.stack([jnp.sum(attn * attn), jnp.sum(ffo * ffo), jnp.sum(y * y)])

    dqkv, near, far = attn_bwd(segment_ids, rel_bias, qkv, o_row, do_row, lse, col_tiles)
    d_one_part = dot(dqkv, w_qkv, NT).astype(BF16)
    d_one = lax.psum_scatter(d_one_part, "tensor", scatter_dimension=0, tiled=True).astype(F32)
    x_in = x_low.astype(F32)
    r_one = inverse_rms(x_in)
    u_one = d_one * norm1_gain
    grad_tokens = (
        d_x_one + r_one * u_one - x_in * (r_one * r_one * r_one * jnp.mean(u_one * x_in, axis=-1, keepdims=True))
    ).astype(BF16)

    keep = add(keep, swap(give, 1))

    def share_of(s):
        return lax.dynamic_index_in_dim(keep, (z - s) % ring, 0, keepdims=False)

    piece = after(share_of(1), d_o)
    for s in (2, 3, 0):
        piece = add(shift(piece, 1), share_of(s))
    for bit in bits_from(8):
        piece = add(piece, swap(piece, bit))
    own = jnp.stack(to_chips(piece))
    grad_gate, grad_up, grad_down = place(where, own, swap(own, 1), CHIPS)
    grad_gate, grad_up = jnp.transpose(grad_gate), jnp.transpose(grad_up)

    grad_o = dot(o_home, d_attn, TN).astype(BF16).reshape(ring, n_dp, out_rows, width)
    got = lax.all_to_all(jnp.moveaxis(grad_o, 1, 0), "dp", 0, 0, tiled=True)
    got = jnp.sum(got.astype(F32), axis=0).astype(BF16)
    got = lax.all_to_all(got, "tensor", 0, 0, tiled=True)
    pieces, masks = gather_all(jnp.sum(got.astype(F32), axis=0).astype(BF16))
    (grad_out,) = place_rows(where, pieces, masks, 1)

    grad_qkv = dot(norm_full, after(dqkv, d_one_part), TN)
    grad_one = jnp.sum(grad_qkv * w_qkv.astype(F32), axis=1) / norm1_gain
    got = lax.all_to_all(grad_qkv.astype(BF16).reshape(n_dp, width // n_dp, 3 * feats), "dp", 0, 0, tiled=True)
    pieces, masks = gather_all(jnp.sum(got.astype(F32), axis=0).astype(BF16))
    grad_query, grad_key, grad_value = place_rows(where, pieces, masks, 3)

    small = jnp.concatenate([grad_two, stats, grad_one, bias_grad(near, far)[:, :heads].reshape(-1)])
    small = sum_rows(small)
    grad_bias = small[2 * width + 3 :].reshape(-1, heads)
    small = sum_ring(small[: 2 * width + 3])
    grad_norm2, stat_sums, grad_norm1 = small[:width], small[width : width + 3], small[width + 3 :]
    count = shard * rows_here * width * n_dp * ring
    rms_stats = jnp.sqrt(stat_sums / count)
    shape = (shard, rows_here, width)
    return (
        out_tokens.reshape(shape),
        grad_tokens.reshape(shape),
        grad_norm1,
        grad_query,
        grad_key,
        grad_value,
        grad_out,
        grad_bias,
        grad_norm2,
        grad_gate,
        grad_up,
        grad_down,
        rms_stats,
    )


def solution(mesh):
    in_specs = (
        P("tensor", "dp", None),
        P("dp", None),
        P(),
        P(None, "tensor"),
        P(None, "tensor"),
        P(None, "tensor"),
        P("tensor", None),
        P(None, "tensor"),
        P(),
        P(None, "tensor"),
        P(None, "tensor"),
        P("tensor", None),
        P("tensor", "dp", None),
    )
    out_specs = (
        P("tensor", "dp", None),
        P("tensor", "dp", None),
        P(),
        P(None, "tensor"),
        P(None, "tensor"),
        P(None, "tensor"),
        P("tensor", None),
        P(None, "tensor"),
        P(),
        P(None, "tensor"),
        P(None, "tensor"),
        P("tensor", None),
        P(),
    )
    return jax.shard_map(local, mesh=mesh, in_specs=in_specs, out_specs=out_specs, check_vma=False)
```

```python
import functools
import jax
import jax.numpy as jnp
from jax import lax
from jax.experimental import pallas as pl
from jax.experimental.pallas import tpu as pltpu
from jax.sharding import PartitionSpec as P

EPSILON = 1e-06
THRESHOLDS = (12, 16, 23, 32, 46, 64, 91)
TILE = 128
SEG = 384
NT = (((1,), (1,)), ((), ()))
NN = (((1,), (0,)), ((), ()))
TN = (((0,), (0,)), ((), ()))
F32 = jnp.float32
BF16 = jnp.bfloat16
SMALL = pl.CostEstimate(flops=1000, bytes_accessed=1000, transcendentals=0)


def bucket_of(offset):
    distance = jnp.abs(offset)
    far_bucket = 8 + sum(((distance >= threshold).astype(jnp.int32) for threshold in THRESHOLDS))
    return jnp.where(distance < 8, distance, far_bucket) + 16 * (offset > 0).astype(jnp.int32)


def tile_bucket(delta, key_axis):
    keys = lax.broadcasted_iota(jnp.int32, (TILE, TILE), key_axis)
    queries = lax.broadcasted_iota(jnp.int32, (TILE, TILE), 1 - key_axis)
    return bucket_of(TILE * delta + keys - queries)


def bias_tiles_kernel(bias_ref, rows_ref, cols_ref):
    buckets, heads = bias_ref.shape
    for out_ref, key_axis in ((rows_ref, 1), (cols_ref, 0)):
        for delta in (-1, 0, 1):
            bucket = tile_bucket(delta, key_axis)
            tiles = [jnp.zeros((TILE, TILE), F32) for _ in range(heads)]
            for b in range(buckets):
                hit = bucket == b
                tiles = [jnp.where(hit, bias_ref[b, h], t) for h, t in enumerate(tiles)]
            for h in range(heads):
                out_ref[h, delta + 1] = tiles[h]


def bias_tiles(rel_bias):
    heads = rel_bias.shape[1]
    shape = jax.ShapeDtypeStruct((heads, 3, TILE, TILE), F32)
    return pl.pallas_call(
        bias_tiles_kernel,
        out_shape=(shape, shape),
        in_specs=[pl.BlockSpec(memory_space=pltpu.SMEM)],
        out_specs=(pl.BlockSpec(memory_space=pltpu.VMEM),) * 2,
        name="bias_tiles",
    )(rel_bias)


def bias_grad_kernel(near_ref, far_ref, out_ref):
    heads = near_ref.shape[0]
    row = lax.broadcasted_iota(jnp.int32, (32, TILE), 0)
    lane = lax.broadcasted_iota(jnp.int32, (32, TILE), 1)
    bucket = [tile_bucket(delta, 0) for delta in (-1, 0, 1)]
    total = jnp.zeros((32, TILE), F32)
    for h in range(heads):
        near = [near_ref[h, d] for d in range(3)]
        for b in range(32):
            deltas = (0, 1) if b < 16 else (1, 2)
            part = sum(jnp.where(bucket[d] == b, near[d], 0.0) for d in deltas)
            part = jnp.sum(part.reshape(16, 8, TILE), axis=0)
            if b == 15:
                part = part + far_ref[h, 0]
            if b == 31:
                part = part + far_ref[h, 1]
            line = jnp.sum(part, axis=0, keepdims=True)
            total = jnp.where((row == b) & (lane == h), jnp.sum(line, axis=1, keepdims=True), total)
    out_ref[...] = total


def bias_grad(near, far):
    return pl.pallas_call(
        bias_grad_kernel,
        out_shape=jax.ShapeDtypeStruct((32, TILE), F32),
        name="bias_grad",
    )(near, far)


def attn_fwd_kernel(seg_ref, bias_ref, qkv_ref, tile_ref, o_ref, lse_ref, s_ref, p_ref, l_ref):
    length, width = o_ref.shape
    q_ref, k_ref, v_ref = (qkv_ref.at[:, n * width : (n + 1) * width] for n in range(3))
    heads = width // 64
    n_tiles = length // TILE
    lane = lax.broadcasted_iota(jnp.int32, (1, width), 1)
    one_example = seg_ref[0, length - 1] == seg_ref[0, 0]

    def blocks(h, mask, spans):
        for lo, hi in spans:
            qh = jnp.where(mask, q_ref[lo:hi], jnp.zeros((), BF16))
            s_ref[lo:hi, lo:hi] = lax.dot_general(qh, k_ref[lo:hi], NT, preferred_element_type=F32)
            below = bias_ref[15, h]
            above = bias_ref[31, h]
            for i in range(lo // TILE, hi // TILE):
                rows = slice(i * TILE, (i + 1) * TILE)
                near = range(max(lo // TILE, i - 1), min(hi // TILE, i + 2))
                parts = {j: s_ref[rows, j * TILE : (j + 1) * TILE] for j in range(lo // TILE, hi // TILE)}
                top = None
                for j in near:
                    parts[j] = parts[j] + tile_ref[h, j - i + 1]
                    top = parts[j] if top is None else jnp.maximum(top, parts[j])
                for side, constant in ((range(lo // TILE, near[0]), below), (range(near[-1] + 1, hi // TILE), above)):
                    if len(side):
                        far = functools.reduce(jnp.maximum, [parts[j] for j in side])
                        top = jnp.maximum(top, far + constant)
                top = jnp.max(top, axis=1, keepdims=True)
                total = None
                for j, part in parts.items():
                    if j < near[0]:
                        shift = top - below
                    elif j > near[-1]:
                        shift = top - above
                    else:
                        shift = top
                    e = jnp.exp(part - shift)
                    total = e if total is None else total + e
                    p_ref[rows, j * TILE : (j + 1) * TILE] = e.astype(BF16)
                total = jnp.sum(total, axis=1, keepdims=True)
                l_ref[rows] = jnp.broadcast_to(1.0 / total, (TILE, TILE))
                lse = jnp.broadcast_to(top + jnp.log(total), (TILE, TILE))
                lse_ref[h, :, rows] = jnp.transpose(lse)[:8]
            oh = lax.dot_general(p_ref[lo:hi, lo:hi], v_ref[lo:hi], (((1,), (0,)), ((), ())), preferred_element_type=F32)
            scale = l_ref[lo:hi, :1]
            o_ref[lo:hi] = jnp.where(mask, (oh * scale).astype(BF16), o_ref[lo:hi])

    @pl.loop(0, heads)
    def _(h):
        mask = (lane // 64) == h

        @pl.when(one_example)
        def _():
            blocks(h, mask, ((0, length),))

        @pl.when(jnp.logical_not(one_example))
        def _():
            blocks(h, mask, tuple((lo, lo + SEG) for lo in range(0, length, SEG)))


def attn_fwd(seg, bias, qkv, tiles):
    length, width = qkv.shape[0], qkv.shape[1] // 3
    heads = width // 64
    vmem = pl.BlockSpec(memory_space=pltpu.VMEM)
    smem = pl.BlockSpec(memory_space=pltpu.SMEM)
    return pl.pallas_call(
        attn_fwd_kernel,
        out_shape=(
            jax.ShapeDtypeStruct((length, width), BF16),
            jax.ShapeDtypeStruct((heads, 8, length), F32),
        ),
        in_specs=[smem, smem, vmem, vmem],
        out_specs=(vmem, vmem),
        scratch_shapes=[
            pltpu.VMEM((length, length), F32),
            pltpu.VMEM((length, length), BF16),
            pltpu.VMEM((length, TILE), F32),
        ],
        compiler_params=pltpu.CompilerParams(vmem_limit_bytes=40 << 20),
        cost_estimate=SMALL,
        name="attn_fwd",
    )(seg, bias, qkv, tiles)


def attn_bwd_kernel(
    seg_ref, bias_ref, qkv_ref, o_ref, do_ref, lse_ref, tile_ref,
    dqkv_ref, near_ref, far_ref,
    s_ref, dp_ref, p_ref, ds_ref, dsum_ref, kt_ref, dqt_ref, dka_ref, dva_ref,
):
    length, width = o_ref.shape
    q_ref, k_ref, v_ref = (qkv_ref.at[:, n * width : (n + 1) * width] for n in range(3))
    heads = width // 64
    lane = lax.broadcasted_iota(jnp.int32, (1, width), 1)
    one_example = seg_ref[0, length - 1] == seg_ref[0, 0]
    kt_ref[...] = jnp.transpose(k_ref[...])
    prod = o_ref[...].astype(F32) * do_ref[...].astype(F32)
    high = prod.astype(BF16)
    low = (prod - high.astype(F32)).astype(BF16)
    head_rows = (
        lax.broadcasted_iota(jnp.int32, (8 * heads, width), 1) // 64
        == lax.broadcasted_iota(jnp.int32, (8 * heads, width), 0) // 8
    ).astype(BF16)
    dsum_ref[...] = lax.dot_general(head_rows, high, NT, preferred_element_type=F32) + lax.dot_general(
        head_rows, low, NT, preferred_element_type=F32
    )
    def blocks(h, mask, spans):
        below = bias_ref[15, h]
        above = bias_ref[31, h]
        near_sum = [None, None, None]
        far_sum = [jnp.zeros((8, TILE), F32)] * 2
        zero = jnp.zeros((), BF16)
        for d in range(3):
            near_ref[h, d] = jnp.zeros((TILE, TILE), F32)
        for lo, hi in spans:
            qh = jnp.where(mask, q_ref[lo:hi], zero)
            dh = jnp.where(mask, do_ref[lo:hi], zero)
            s_ref[lo:hi, lo:hi] = lax.dot_general(k_ref[lo:hi], qh, NT, preferred_element_type=F32)
            dp_ref[lo:hi, lo:hi] = lax.dot_general(v_ref[lo:hi], dh, NT, preferred_element_type=F32)
            for i in range(lo // TILE, hi // TILE):
                cols = slice(i * TILE, (i + 1) * TILE)
                lse = lse_ref[h, 0:1, cols]
                dsum = dsum_ref[pl.ds(pl.multiple_of(h * 8, 8), 1), cols]
                for j in range(lo // TILE, hi // TILE):
                    rows = slice(j * TILE, (j + 1) * TILE)
                    s = s_ref[rows, cols]
                    if abs(j - i) <= 1:
                        e = jnp.exp(s + tile_ref[h, j - i + 1] - lse)
                    else:
                        e = jnp.exp(s - (lse - (below if j < i else above)))
                    ds = e * (dp_ref[rows, cols] - dsum)
                    p_ref[rows, cols] = e.astype(BF16)
                    ds_ref[rows, cols] = ds.astype(BF16)
                    if abs(j - i) <= 1:
                        near_ref[h, j - i + 1] += ds
                    else:
                        side = int(j > i)
                        far_sum[side] = far_sum[side] + jnp.sum(ds.reshape(TILE // 8, 8, TILE), axis=0)
            dv = lax.dot_general(p_ref[lo:hi, lo:hi], dh, NN, preferred_element_type=F32)
            dk = lax.dot_general(ds_ref[lo:hi, lo:hi], qh, NN, preferred_element_type=F32)
            dva_ref[lo:hi] = jnp.where(mask, dv, dva_ref[lo:hi])
            dka_ref[lo:hi] = jnp.where(mask, dk, dka_ref[lo:hi])
            head = pl.ds(pl.multiple_of(h * 64, 64), 64)
            dqt_ref[head, lo:hi] = lax.dot_general(
                kt_ref[head, lo:hi], ds_ref[lo:hi, lo:hi], NN, preferred_element_type=F32
            )
        far_ref[h, 0] = far_sum[0]
        far_ref[h, 1] = far_sum[1]

    @pl.loop(0, heads)
    def _(h):
        mask = (lane // 64) == h

        @pl.when(one_example)
        def _():
            blocks(h, mask, ((0, length),))

        @pl.when(jnp.logical_not(one_example))
        def _():
            blocks(h, mask, tuple((lo, lo + SEG) for lo in range(0, length, SEG)))

    dqkv_ref[:, :width] = jnp.transpose(dqt_ref[...]).astype(BF16)
    dqkv_ref[:, width : 2 * width] = dka_ref[...].astype(BF16)
    dqkv_ref[:, 2 * width :] = dva_ref[...].astype(BF16)


def attn_bwd(seg, bias, qkv, o, do, lse, tiles):
    length, width = o.shape
    heads = width // 64
    vmem = pl.BlockSpec(memory_space=pltpu.VMEM)
    smem = pl.BlockSpec(memory_space=pltpu.SMEM)
    return pl.pallas_call(
        attn_bwd_kernel,
        out_shape=(
            jax.ShapeDtypeStruct((length, 3 * width), BF16),
            jax.ShapeDtypeStruct((heads, 3, TILE, TILE), F32),
            jax.ShapeDtypeStruct((heads, 2, 8, TILE), F32),
        ),
        in_specs=[smem, smem] + [vmem] * 5,
        out_specs=(vmem,) * 3,
        scratch_shapes=[
            pltpu.VMEM((length, length), F32),
            pltpu.VMEM((length, length), F32),
            pltpu.VMEM((length, length), BF16),
            pltpu.VMEM((length, length), BF16),
            pltpu.VMEM((8 * heads, length), F32),
            pltpu.VMEM((width, length), BF16),
            pltpu.VMEM((width, length), F32),
            pltpu.VMEM((length, width), F32),
            pltpu.VMEM((length, width), F32),
        ],
        compiler_params=pltpu.CompilerParams(vmem_limit_bytes=48 << 20),
        cost_estimate=SMALL,
        name="attn_bwd",
    )(seg, bias, qkv, o, do, lse, tiles)


def tanh_gelu(u):
    scale = 0.7978845608028654
    t = jnp.tanh(scale * (u + 0.044715 * (u * u * u)))
    half = 0.5 * (1.0 + t)
    slope = half + (0.5 * u) * (1.0 - t * t) * (scale * (1.0 + 0.134145 * (u * u)))
    return u * half, slope


def ffn_kernel(
    where_ref, x_ref, c_ref, mine_ref, other_ref,
    dtwo_ref, ffo_ref, hidden_ref, dgate_ref, dup_ref,
    gate_w, up_w, down_w, sems,
):
    core = where_ref[0]
    ring, rows, half = mine_ref.shape
    units = rows // 3
    scratches = (gate_w, up_w, down_w)
    copies = [[], [], []]
    for m in range(3):
        for q in range(ring):
            for n, ref in enumerate((mine_ref, other_ref)):
                start = pl.multiple_of((core ^ n) * half, 128)
                copies[m].append(
                    pltpu.make_async_copy(
                        ref.at[q, m * units : (m + 1) * units],
                        scratches[m].at[q * units : (q + 1) * units, pl.ds(start, half)],
                        sems.at[m, 2 * q + n],
                    )
                )
    for group in copies:
        for copy in group:
            copy.start()
    for copy in copies[0]:
        copy.wait()
    gate = lax.dot_general(x_ref[...], gate_w[...], NT, preferred_element_type=F32)
    for copy in copies[1]:
        copy.wait()
    up = lax.dot_general(x_ref[...], up_w[...], NT, preferred_element_type=F32)
    for copy in copies[2]:
        copy.wait()
    d_hidden = lax.dot_general(c_ref[...], down_w[...], NT, preferred_element_type=F32)
    value, slope = tanh_gelu(gate)
    hidden = (value * up).astype(BF16)
    d_gate = (d_hidden * up * slope).astype(BF16)
    d_up = (d_hidden * value).astype(BF16)
    hidden_ref[...] = hidden
    dgate_ref[...] = d_gate
    dup_ref[...] = d_up
    dtwo_ref[...] = (
        lax.dot_general(d_gate, gate_w[...], NN, preferred_element_type=F32)
        + lax.dot_general(d_up, up_w[...], NN, preferred_element_type=F32)
    ).astype(dtwo_ref.dtype)
    ffo_ref[...] = lax.dot_general(hidden, down_w[...], NN, preferred_element_type=F32).astype(ffo_ref.dtype)


def ffn(where, x, c, mine, other):
    tokens, width = x.shape
    ring, rows, half = mine.shape
    units = ring * rows // 3
    vmem = pl.BlockSpec(memory_space=pltpu.VMEM)
    anywhere = pl.BlockSpec(memory_space=pl.ANY)
    wide = jax.ShapeDtypeStruct((tokens, width), BF16)
    inner = jax.ShapeDtypeStruct((tokens, units), BF16)
    return pl.pallas_call(
        ffn_kernel,
        out_shape=(wide, wide, inner, inner, inner),
        in_specs=[pl.BlockSpec(memory_space=pltpu.SMEM), vmem, vmem, anywhere, anywhere],
        out_specs=(vmem,) * 5,
        scratch_shapes=[pltpu.VMEM((units, width), BF16)] * 3 + [pltpu.SemaphoreType.DMA((3, 2 * ring))],
        compiler_params=pltpu.CompilerParams(vmem_limit_bytes=40 << 20),
        cost_estimate=SMALL,
        name="ffn",
    )(where, x, c, mine, other)


def ffn_grads_kernel(n, where_ref, *refs):
    sources = [refs[i * n : (i + 1) * n] for i in range(5)]
    keep_ref, give_ref = refs[5 * n : 5 * n + 2]
    held = refs[5 * n + 2 : 5 * n + 7]
    sems = refs[5 * n + 7]
    core = where_ref[0]
    ring, _, units, half = keep_ref.shape
    rows = sources[0][0].shape[0]
    copies = [
        [
            pltpu.make_async_copy(ref, target.at[j * rows : (j + 1) * rows], sems.at[i, j])
            for j, ref in enumerate(group)
        ]
        for i, (group, target) in enumerate(zip(sources, held))
    ]
    for group in copies:
        for copy in group:
            copy.start()
    waited = set()
    for m, (lhs, rhs) in ((2, (0, 1)), (0, (2, 3)), (1, (4, 3))):
        for i in (lhs, rhs):
            if i not in waited:
                waited.add(i)
                for copy in copies[i]:
                    copy.wait()
        for n_half, out_ref in enumerate((give_ref, keep_ref)):
            start = pl.multiple_of((core ^ (1 - n_half)) * half, 128)
            grad = lax.dot_general(
                held[lhs][...], held[rhs][:, pl.ds(start, half)], TN, preferred_element_type=F32
            ).astype(BF16)
            for q in range(ring):
                out_ref[q, m] = grad[q * units : (q + 1) * units]


def ffn_grads(where, hs, cs, gs, xs, us, ring):
    rows, width = xs[0].shape
    units = hs[0].shape[1]
    n = len(xs)
    vmem = pl.BlockSpec(memory_space=pltpu.VMEM)
    anywhere = pl.BlockSpec(memory_space=pl.ANY)
    shape = jax.ShapeDtypeStruct((ring, 3, units // ring, width // 2), BF16)
    wide, inner = pltpu.VMEM((n * rows, width), BF16), pltpu.VMEM((n * rows, units), BF16)
    return pl.pallas_call(
        functools.partial(ffn_grads_kernel, n),
        out_shape=(shape, shape),
        in_specs=[pl.BlockSpec(memory_space=pltpu.SMEM)] + [anywhere] * (5 * n),
        out_specs=(vmem, vmem),
        scratch_shapes=[inner, wide, inner, wide, inner, pltpu.SemaphoreType.DMA((5, n))],
        compiler_params=pltpu.CompilerParams(vmem_limit_bytes=48 << 20),
        cost_estimate=SMALL,
        name="ffn_grads",
    )(where, *hs, *cs, *gs, *xs, *us)


def out_grads_kernel(where_ref, o_ref, d_ref, keep_ref, give_ref, held):
    core, chip = where_ref[0], where_ref[1]
    chips, ring, rows, half = keep_ref.shape
    for n, out_ref in enumerate((give_ref, keep_ref)):
        start = pl.multiple_of((core ^ (1 - n)) * half, 128)
        held[...] = lax.dot_general(
            o_ref[...], d_ref[:, pl.ds(start, half)], TN, preferred_element_type=F32
        ).astype(BF16)
        for r in range(chips):
            for q in range(ring):
                first = (q * chips + (chip ^ r)) * rows
                out_ref[r, q] = held[pl.ds(pl.multiple_of(first, rows), rows)]


def out_grads(where, o, d, ring):
    width = d.shape[1]
    vmem = pl.BlockSpec(memory_space=pltpu.VMEM)
    shape = jax.ShapeDtypeStruct((4, ring, o.shape[1] // (4 * ring), width // 2), BF16)
    return pl.pallas_call(
        out_grads_kernel,
        out_shape=(shape, shape),
        in_specs=[pl.BlockSpec(memory_space=pltpu.SMEM), vmem, vmem],
        out_specs=(vmem, vmem),
        scratch_shapes=[pltpu.VMEM((o.shape[1], width // 2), BF16)],
        compiler_params=pltpu.CompilerParams(vmem_limit_bytes=24 << 20),
        cost_estimate=SMALL,
        name="out_grads",
    )(where, o, d)


def normed_grad_kernel(d_ref, w_ref, out_ref):
    out_ref[...] = lax.dot_general(d_ref[...], w_ref[...], NT, preferred_element_type=F32).astype(BF16)


def normed_grad(d, w):
    vmem = pl.BlockSpec(memory_space=pltpu.VMEM)
    return pl.pallas_call(
        normed_grad_kernel,
        out_shape=jax.ShapeDtypeStruct((d.shape[0], w.shape[0]), BF16),
        in_specs=[vmem, vmem],
        out_specs=vmem,
        compiler_params=pltpu.CompilerParams(vmem_limit_bytes=24 << 20),
        cost_estimate=SMALL,
        name="normed_grad",
    )(d, w)


def qkv_grads_kernel(where_ref, x_ref, d_ref, w_ref, keep_ref, give_ref, gain_ref):
    core, chip = where_ref[0], where_ref[1]
    chips, rows, _ = keep_ref.shape
    for n, out_ref in enumerate((give_ref, keep_ref)):
        for r in range(chips):
            block = (core ^ (1 - n)) * chips + (chip ^ r)
            start = pl.multiple_of(block * rows, 128)
            grad = lax.dot_general(x_ref[:, pl.ds(start, rows)], d_ref[...], TN, preferred_element_type=F32)
            out_ref[r] = grad.astype(BF16)
            line = jnp.sum(grad * w_ref[pl.ds(start, rows)].astype(F32), axis=1, keepdims=True)
            gain_ref[pl.ds(block, 1)] = jnp.transpose(jnp.broadcast_to(line, (rows, rows)))[:1]


def qkv_grads(where, x, d, w):
    rows = x.shape[1] // 8
    vmem = pl.BlockSpec(memory_space=pltpu.VMEM)
    shape = jax.ShapeDtypeStruct((4, rows, d.shape[1]), BF16)
    return pl.pallas_call(
        qkv_grads_kernel,
        out_shape=(shape, shape, jax.ShapeDtypeStruct((8, rows), F32)),
        in_specs=[pl.BlockSpec(memory_space=pltpu.SMEM), vmem, vmem, vmem],
        out_specs=(vmem,) * 3,
        compiler_params=pltpu.CompilerParams(vmem_limit_bytes=24 << 20),
        cost_estimate=SMALL,
        name="qkv_grads",
    )(where, x, d, w)


def place_kernel(where_ref, own_ref, other_ref, *out_refs):
    core, chip = where_ref[0], where_ref[1]
    chips, _, half = own_ref.shape
    first = 0
    for target in out_refs:
        units = target.shape[0] // chips
        for r in range(chips):
            rows = pl.ds(pl.multiple_of((chip ^ r) * units, 8), units)
            for n, ref in enumerate((own_ref, other_ref)):
                columns = pl.ds(pl.multiple_of((core ^ n) * half, 128), half)
                target[rows, columns] = ref[r, first : first + units].astype(F32)
        first += units


def place(where, own, other, sizes):
    chips, _, half = own.shape
    vmem = pl.BlockSpec(memory_space=pltpu.VMEM)
    return pl.pallas_call(
        place_kernel,
        out_shape=tuple(jax.ShapeDtypeStruct((chips * size, 2 * half), F32) for size in sizes),
        in_specs=[pl.BlockSpec(memory_space=pltpu.SMEM), vmem, vmem],
        out_specs=(vmem,) * len(sizes),
        compiler_params=pltpu.CompilerParams(vmem_limit_bytes=40 << 20),
        cost_estimate=SMALL,
        name="place",
    )(where, own, other)


def place_late_kernel(where_ref, own_ref, other_ref, *out_refs):
    core, chip = where_ref[0], where_ref[1]
    chips, total, width = own_ref.shape
    projections, out_ref = out_refs[:3], out_refs[3]
    rows = projections[0].shape[0] // (2 * chips)
    part, half = width // 3, out_ref.shape[1] // 2
    for n, ref in enumerate((own_ref, other_ref)):
        for r in range(chips):
            start = ((core ^ n) * chips + (chip ^ r)) * rows
            value = ref[r, :rows].astype(F32)
            for i, target in enumerate(projections):
                target[pl.ds(pl.multiple_of(start, 8), rows)] = value[:, i * part : (i + 1) * part]
            start = pl.multiple_of((chip ^ r) * (total - rows), 8)
            columns = pl.ds(pl.multiple_of((core ^ n) * half, 128), half)
            out_ref[pl.ds(start, total - rows), columns] = ref[r, rows:, :half].astype(F32)


def place_late(where, own, other, rows, half):
    chips, total, width = own.shape
    vmem = pl.BlockSpec(memory_space=pltpu.VMEM)
    projection = jax.ShapeDtypeStruct((2 * chips * rows, width // 3), F32)
    return pl.pallas_call(
        place_late_kernel,
        out_shape=(projection,) * 3 + (jax.ShapeDtypeStruct((chips * (total - rows), 2 * half), F32),),
        in_specs=[pl.BlockSpec(memory_space=pltpu.SMEM), vmem, vmem],
        out_specs=(vmem,) * 4,
        cost_estimate=SMALL,
        name="place_late",
    )(where, own, other)


def place_out_kernel(where_ref, mine_ref, other_ref, out_ref):
    chips, ring, rows, _ = mine_ref.shape
    core, chip, z = where_ref[0], where_ref[1], where_ref[3]
    for s in range(ring):
        quarter = lax.rem(z + ring - s, ring)
        for r in range(chips):
            for n, ref in enumerate((mine_ref, other_ref)):
                start = ((quarter * chips + (chip ^ r)) * 2 + (core ^ n)) * rows
                out_ref[pl.ds(pl.multiple_of(start, rows), rows)] = ref[r, s]


def place_out(where, mine, other):
    chips, ring, rows, width = mine.shape
    vmem = pl.BlockSpec(memory_space=pltpu.VMEM)
    return pl.pallas_call(
        place_out_kernel,
        out_shape=jax.ShapeDtypeStruct((2 * chips * ring * rows, width), mine.dtype),
        in_specs=[pl.BlockSpec(memory_space=pltpu.SMEM), vmem, vmem],
        out_specs=vmem,
        cost_estimate=SMALL,
        name="place_out",
    )(where, mine, other)


def swap(value, mask):
    size = lax.axis_size("dp")
    return lax.ppermute(value, "dp", [(i, i ^ mask) for i in range(size)])


def shift(value, step):
    size = lax.axis_size("tensor")
    return lax.ppermute(value, "tensor", [(i, (i + step) % size) for i in range(size)])


def add(left, right):
    return (left.astype(F32) + right.astype(F32)).astype(BF16)


def after(value, *others):
    return lax.optimization_barrier((value, *others))[0]


def bits_from(first):
    bit = first
    while bit < lax.axis_size("dp"):
        yield bit
        bit *= 2


def sum_rows(value):
    for bit in bits_from(1):
        value = value + swap(value, bit)
    return value


def sum_ring(value):
    return value + shift(value, 1) + shift(value, 2) + shift(value, 3)


def dot(left, right, dims=NN):
    return lax.dot_general(left, right, dims, preferred_element_type=F32)


def inverse_rms(values):
    return lax.rsqrt(jnp.mean(values * values, axis=-1, keepdims=True) + EPSILON)


CHIPS = (0, 1, 2, 3)


def to_chips(value):
    return [value] + [swap(value, 2 * mask) for mask in CHIPS[1:]]


def local(
    tokens,
    segment_ids,
    norm1_gain,
    w_query,
    w_key,
    w_value,
    w_out,
    rel_bias,
    norm2_gain,
    gate_weight_matrix,
    upward_weight,
    downward_weight,
    cotangent,
):
    shard, rows_here, width = tokens.shape
    length = segment_ids.shape[1]
    heads = rel_bias.shape[1]
    feats = w_query.shape[1]
    units = downward_weight.shape[0]
    ring = lax.axis_size("tensor")
    n_dp = lax.axis_size("dp")
    z = lax.axis_index("tensor")
    dp = lax.axis_index("dp")
    core = dp & 1
    chip = (dp >> 1) & 3
    where = jnp.stack([core, chip, dp, z]).astype(jnp.int32)

    x_low = tokens.reshape(shard, width)
    cot = cotangent.reshape(shard, width)
    row_tiles, col_tiles = bias_tiles(rel_bias)
    w_qkv = jnp.concatenate([w_query, w_key, w_value], axis=1)

    out_rows = feats // 8
    out_piece = lax.dynamic_slice_in_dim(w_out, (2 * chip + core) * out_rows, out_rows, 0)
    blocks = [jnp.concatenate([x_low, out_piece], axis=0)]
    blocks.append(shift(blocks[-1], 1))
    cs = to_chips(after(cot, blocks[1]))
    blocks.append(shift(blocks[-1], 1))
    blocks.append(shift(blocks[-1], 1))
    out_ring = jnp.stack([block[shard:] for block in blocks])
    out_chips = to_chips(out_ring)

    def unit_rows(array):
        return lax.dynamic_slice(array, (chip * (units // 4), core * (width // 2)), (units // 4, width // 2))

    pack = jnp.concatenate(
        [
            unit_rows(jnp.transpose(gate_weight_matrix)),
            unit_rows(jnp.transpose(upward_weight)),
            unit_rows(downward_weight),
        ],
        axis=0,
    )
    mine_w = lax.all_gather(after(pack, blocks[3]), "tensor", axis=0)

    qkv = jnp.zeros((length, 3 * feats), BF16)
    norm_full = jnp.zeros((length, width), BF16)
    for s, block in enumerate(blocks):
        values = block[:shard].astype(F32)
        normed = (values * inverse_rms(values) * norm1_gain).astype(BF16)
        start = ((z - s) % ring) * shard
        norm_full = lax.dynamic_update_slice_in_dim(norm_full, normed, start, 0)
        qkv = lax.dynamic_update_slice_in_dim(qkv, dot(normed, w_qkv).astype(BF16), start, 0)

    o_row, lse = attn_fwd(segment_ids, rel_bias, after(qkv, *cs), row_tiles)
    out_mine = after(jnp.stack(out_chips), o_row)
    out_all = place_out(where, out_mine, swap(out_mine, 1))
    o_home = lax.all_to_all(o_row, "tensor", 0, 1, tiled=True)
    attn = dot(o_home, out_all)
    x_one = x_low.astype(F32) + attn
    r_two = inverse_rms(x_one)
    norm_two = (x_one * r_two * norm2_gain).astype(BF16)

    mine_w = after(mine_w, norm_two)
    other_w = swap(mine_w, 1)
    xs = to_chips(norm_two)
    parts = []
    for x, c in zip(xs, cs):
        if parts:
            x = after(x, parts[-1][0])
        parts.append(ffn(where, x, c, mine_w, other_w))

    def returns(which, *others):
        terms = [after(part[which], *others) if others else part[which] for part in parts]
        return [terms[0]] + [swap(terms[mask], 2 * mask) for mask in CHIPS[1:]]

    def total_of(terms):
        return sum(term.astype(F32) for term in terms)

    back = returns(0)
    keep, give = ffn_grads(
        where,
        [part[2] for part in parts],
        cs,
        [part[3] for part in parts],
        xs,
        [part[4] for part in parts],
        ring,
    )
    d_two = total_of([after(back[0], keep)] + back[1:])
    u_two = d_two * norm2_gain
    d_x_one = cot.astype(F32) + r_two * u_two - x_one * (
        r_two * r_two * r_two * jnp.mean(u_two * x_one, axis=-1, keepdims=True)
    )
    d_attn = d_x_one.astype(BF16)
    d_o = dot(d_attn, out_all, NT).astype(BF16)
    do_row = lax.all_to_all(d_o, "tensor", 1, 0, tiled=True)

    give, o_done = after(give, d_o), after(o_home, d_o)
    keep = add(keep, swap(give, 1))
    ffn_piece = lax.psum_scatter(keep, "tensor", scatter_dimension=0).reshape(-1, width // 2)

    def sum_chips(pieces):
        return total_of([pieces[0]] + [swap(pieces[r], 2 * r) for r in CHIPS[1:]])

    out_keep, out_give = out_grads(where, o_done, d_attn, ring)
    out_keep = add(out_keep, swap(out_give, 1))
    got = sum_chips(out_keep).astype(BF16)
    ffo_back = returns(1, out_keep)
    ffo = total_of(ffo_back)
    y = x_one + ffo
    out_tokens = y.astype(BF16)
    grad_two = jnp.sum(d_two * x_one * r_two, axis=0)
    stats = jnp.stack([jnp.sum(attn * attn), jnp.sum(ffo * ffo), jnp.sum(y * y)])

    dqkv, near, far = attn_bwd(segment_ids, rel_bias, qkv, o_row, do_row, lse, col_tiles)
    dqkv = after(dqkv, ffn_piece, got, *ffo_back)
    d_one_part = normed_grad(dqkv, w_qkv)
    d_one = lax.psum_scatter(d_one_part, "tensor", scatter_dimension=0, tiled=True).astype(F32)
    piece = after(ffn_piece, dqkv)
    for bit in bits_from(8):
        piece = add(piece, swap(piece, bit))
    own = jnp.stack(to_chips(piece))

    qkv_keep, qkv_give, grad_one = qkv_grads(where, norm_full, after(dqkv, d_one_part), w_qkv)
    qkv_piece = sum_chips(add(qkv_keep, swap(qkv_give, 1))).astype(BF16)
    got = after(got, dqkv)
    out_parts = [lax.dynamic_index_in_dim(got, (z + s) % ring, 0, keepdims=False) for s in range(ring)]
    out_piece = total_of([out_parts[0]] + [shift(out_parts[s], s) for s in range(1, ring)]).astype(BF16)
    late = jnp.concatenate(
        [qkv_piece, jnp.pad(out_piece, ((0, 0), (0, 3 * feats - width // 2)))], axis=0
    )
    for bit in bits_from(8):
        late = add(late, swap(late, bit))
    grad_gate, grad_up, grad_down = place(where, own, swap(own, 1), (units // 4,) * 3)
    grad_gate, grad_up = jnp.transpose(grad_gate), jnp.transpose(grad_up)
    late = jnp.stack(to_chips(after(late, own)))
    grad_query, grad_key, grad_value, grad_out = place_late(where, late, swap(late, 1), width // 8, width // 2)

    near = after(near, qkv_give)
    row = width // 8
    stats = jnp.pad(stats, (0, row - 3)).reshape(1, row)
    small = jnp.concatenate([grad_two.reshape(8, row), grad_one, stats, bias_grad(near, far)], axis=0)
    small = sum_rows(small)
    grad_bias = small[17:, :heads]
    small = sum_ring(small[:17])
    grad_norm2, grad_norm1 = small[:8].reshape(width), small[8:16].reshape(width) / norm1_gain
    stat_sums = small[16, :3]
    count = shard * rows_here * width * n_dp * ring
    rms_stats = jnp.sqrt(stat_sums / count)

    d_one = after(d_one, grad_query, small, grad_bias)
    x_in = x_low.astype(F32)
    r_one = inverse_rms(x_in)
    u_one = d_one * norm1_gain
    grad_tokens = (
        d_x_one + r_one * u_one - x_in * (r_one * r_one * r_one * jnp.mean(u_one * x_in, axis=-1, keepdims=True))
    ).astype(BF16)

    shape = (shard, rows_here, width)
    return (
        out_tokens.reshape(shape),
        grad_tokens.reshape(shape),
        grad_norm1,
        grad_query,
        grad_key,
        grad_value,
        grad_out,
        grad_bias,
        grad_norm2,
        grad_gate,
        grad_up,
        grad_down,
        rms_stats,
    )


def solution(mesh):
    in_specs = (
        P("tensor", "dp", None),
        P("dp", None),
        P(),
        P(None, "tensor"),
        P(None, "tensor"),
        P(None, "tensor"),
        P("tensor", None),
        P(None, "tensor"),
        P(),
        P(None, "tensor"),
        P(None, "tensor"),
        P("tensor", None),
        P("tensor", "dp", None),
    )
    out_specs = (
        P("tensor", "dp", None),
        P("tensor", "dp", None),
        P(),
        P(None, "tensor"),
        P(None, "tensor"),
        P(None, "tensor"),
        P("tensor", None),
        P(None, "tensor"),
        P(),
        P(None, "tensor"),
        P(None, "tensor"),
        P("tensor", None),
        P(),
    )
    return jax.shard_map(local, mesh=mesh, in_specs=in_specs, out_specs=out_specs, check_vma=False)
```

```python
import functools
import jax
import jax.numpy as jnp
from jax import lax
from jax.experimental import pallas as pl
from jax.experimental.pallas import tpu as pltpu
from jax.sharding import Mesh, PartitionSpec as P

EPSILON = 1e-06
THRESHOLDS = (12, 16, 23, 32, 46, 64, 91)
TILE = 128
SEG = 384
NT = (((1,), (1,)), ((), ()))
NN = (((1,), (0,)), ((), ()))
NN = (((1,), (0,)), ((), ()))
TN = (((0,), (0,)), ((), ()))
F32 = jnp.float32
BF16 = jnp.bfloat16
SMALL = pl.CostEstimate(flops=1000, bytes_accessed=1000, transcendentals=0)


def bucket_of(offset):
    distance = jnp.abs(offset)
    far_bucket = 8 + sum(((distance >= threshold).astype(jnp.int32) for threshold in THRESHOLDS))
    return jnp.where(distance < 8, distance, far_bucket) + 16 * (offset > 0).astype(jnp.int32)


def tile_bucket(delta, key_axis):
    keys = lax.broadcasted_iota(jnp.int32, (TILE, TILE), key_axis)
    queries = lax.broadcasted_iota(jnp.int32, (TILE, TILE), 1 - key_axis)
    return bucket_of(TILE * delta + keys - queries)


def bias_tiles_kernel(bias_ref, out_ref):
    buckets, heads = bias_ref.shape
    for delta in (-1, 0, 1):
        bucket = tile_bucket(delta, 0)
        tiles = [jnp.zeros((TILE, TILE), F32) for _ in range(heads)]
        for b in range(buckets):
            hit = bucket == b
            tiles = [jnp.where(hit, bias_ref[b, h], t) for h, t in enumerate(tiles)]
        for h in range(heads):
            out_ref[h, delta + 1] = tiles[h]


def bias_tiles(rel_bias):
    return pl.pallas_call(
        bias_tiles_kernel,
        out_shape=jax.ShapeDtypeStruct((rel_bias.shape[1], 3, TILE, TILE), F32),
        in_specs=[pl.BlockSpec(memory_space=pltpu.SMEM)],
        out_specs=pl.BlockSpec(memory_space=pltpu.VMEM),
        name="bias_tiles",
    )(rel_bias)


def bias_grad_kernel(near_ref, far_ref, out_ref):
    heads = near_ref.shape[0]
    row = lax.broadcasted_iota(jnp.int32, (32, TILE), 0)
    lane = lax.broadcasted_iota(jnp.int32, (32, TILE), 1)
    bucket = [tile_bucket(delta, 0) for delta in (-1, 0, 1)]
    total = jnp.zeros((32, TILE), F32)
    for h in range(heads):
        near = [near_ref[h, d] for d in range(3)]
        for b in range(32):
            deltas = (0, 1) if b < 16 else (1, 2)
            part = sum(jnp.where(bucket[d] == b, near[d], 0.0) for d in deltas)
            part = jnp.sum(part.reshape(16, 8, TILE), axis=0)
            if b == 15:
                part = part + far_ref[h, 0]
            if b == 31:
                part = part + far_ref[h, 1]
            line = jnp.sum(part, axis=0, keepdims=True)
            total = jnp.where((row == b) & (lane == h), jnp.sum(line, axis=1, keepdims=True), total)
    out_ref[...] = total


def bias_grad(near, far):
    return pl.pallas_call(
        bias_grad_kernel,
        out_shape=jax.ShapeDtypeStruct((32, TILE), F32),
        name="bias_grad",
    )(near, far)


def attn_fwd_kernel(seg_ref, bias_ref, qkv_ref, tile_ref, o_ref, lse_ref, s_ref, p_ref, l_ref, vt_ref, ot_ref):
    length, width = o_ref.shape
    q_ref, k_ref, v_ref = (qkv_ref.at[:, n * width : (n + 1) * width] for n in range(3))
    heads = width // 64
    lane = lax.broadcasted_iota(jnp.int32, (1, width), 1)
    one_example = seg_ref[0, length - 1] == seg_ref[0, 0]
    vt_ref[...] = jnp.transpose(v_ref[...])

    def blocks(h, mask, spans):
        below = bias_ref[15, h]
        above = bias_ref[31, h]
        head = pl.ds(pl.multiple_of(h * 64, 64), 64)
        for lo, hi in spans:
            qh = jnp.where(mask, q_ref[lo:hi], jnp.zeros((), BF16))
            s_ref[lo:hi, lo:hi] = lax.dot_general(k_ref[lo:hi], qh, NT, preferred_element_type=F32)
            tiles = range(lo // TILE, hi // TILE)
            for i in tiles:
                cols = slice(i * TILE, (i + 1) * TILE)
                near_top, sides = None, {-1: None, 1: None}
                for j in tiles:
                    part = s_ref[j * TILE : (j + 1) * TILE, cols]
                    if abs(j - i) <= 1:
                        part = part + tile_ref[h, j - i + 1]
                        s_ref[j * TILE : (j + 1) * TILE, cols] = part
                    part = jnp.max(part.reshape(TILE // 8, 8, TILE), axis=0)
                    if abs(j - i) <= 1:
                        near_top = part if near_top is None else jnp.maximum(near_top, part)
                    else:
                        side = 1 if j > i else -1
                        sides[side] = part if sides[side] is None else jnp.maximum(sides[side], part)
                top = near_top
                for side, constant in ((-1, below), (1, above)):
                    if sides[side] is not None:
                        top = jnp.maximum(top, sides[side] + constant)
                top = jnp.max(top, axis=0, keepdims=True)
                total = jnp.zeros((8, TILE), F32)
                for j in tiles:
                    shift = top
                    if abs(j - i) > 1:
                        shift = top - (below if j < i else above)
                    e = jnp.exp(s_ref[j * TILE : (j + 1) * TILE, cols] - shift)
                    total = total + jnp.sum(e.reshape(TILE // 8, 8, TILE), axis=0)
                    p_ref[j * TILE : (j + 1) * TILE, cols] = e.astype(BF16)
                total = jnp.sum(total, axis=0, keepdims=True)
                l_ref[0:1, cols] = 1.0 / total
                lse_ref[h, 0:1, cols] = top + jnp.log(total)
            ot_ref[head, lo:hi] = (
                lax.dot_general(vt_ref[head, lo:hi], p_ref[lo:hi, lo:hi], NN, preferred_element_type=F32)
                * l_ref[0:1, lo:hi]
            )

    @pl.loop(0, heads)
    def _(h):
        mask = (lane // 64) == h

        @pl.when(one_example)
        def _():
            blocks(h, mask, ((0, length),))

        @pl.when(jnp.logical_not(one_example))
        def _():
            blocks(h, mask, tuple((lo, lo + SEG) for lo in range(0, length, SEG)))

    o_ref[...] = jnp.transpose(ot_ref[...]).astype(BF16)


def attn_fwd(seg, bias, qkv, tiles):
    length, width = qkv.shape[0], qkv.shape[1] // 3
    heads = width // 64
    vmem = pl.BlockSpec(memory_space=pltpu.VMEM)
    smem = pl.BlockSpec(memory_space=pltpu.SMEM)
    return pl.pallas_call(
        attn_fwd_kernel,
        out_shape=(
            jax.ShapeDtypeStruct((length, width), BF16),
            jax.ShapeDtypeStruct((heads, 8, length), F32),
        ),
        in_specs=[smem, smem, vmem, vmem],
        out_specs=(vmem, vmem),
        scratch_shapes=[
            pltpu.VMEM((length, length), F32),
            pltpu.VMEM((length, length), BF16),
            pltpu.VMEM((8, length), F32),
            pltpu.VMEM((width, length), BF16),
            pltpu.VMEM((width, length), F32),
        ],
        compiler_params=pltpu.CompilerParams(vmem_limit_bytes=40 << 20),
        cost_estimate=SMALL,
        name="attn_fwd",
    )(seg, bias, qkv, tiles)


def attn_bwd_kernel(
    seg_ref, bias_ref, qkv_ref, o_ref, do_ref, lse_ref, tile_ref,
    dqkv_ref, near_ref, far_ref,
    s_ref, dp_ref, p_ref, ds_ref, dsum_ref, kt_ref, dqt_ref, dka_ref, dva_ref,
):
    length, width = o_ref.shape
    q_ref, k_ref, v_ref = (qkv_ref.at[:, n * width : (n + 1) * width] for n in range(3))
    heads = width // 64
    lane = lax.broadcasted_iota(jnp.int32, (1, width), 1)
    one_example = seg_ref[0, length - 1] == seg_ref[0, 0]
    kt_ref[...] = jnp.transpose(k_ref[...])
    prod = o_ref[...].astype(F32) * do_ref[...].astype(F32)
    high = prod.astype(BF16)
    low = (prod - high.astype(F32)).astype(BF16)
    head_rows = (
        lax.broadcasted_iota(jnp.int32, (8 * heads, width), 1) // 64
        == lax.broadcasted_iota(jnp.int32, (8 * heads, width), 0) // 8
    ).astype(BF16)
    dsum_ref[...] = lax.dot_general(head_rows, high, NT, preferred_element_type=F32) + lax.dot_general(
        head_rows, low, NT, preferred_element_type=F32
    )
    def blocks(h, mask, spans):
        below = bias_ref[15, h]
        above = bias_ref[31, h]
        near_sum = [None, None, None]
        far_sum = [jnp.zeros((8, TILE), F32)] * 2
        zero = jnp.zeros((), BF16)
        for d in range(3):
            near_ref[h, d] = jnp.zeros((TILE, TILE), F32)
        for lo, hi in spans:
            qh = jnp.where(mask, q_ref[lo:hi], zero)
            dh = jnp.where(mask, do_ref[lo:hi], zero)
            s_ref[lo:hi, lo:hi] = lax.dot_general(k_ref[lo:hi], qh, NT, preferred_element_type=F32)
            dp_ref[lo:hi, lo:hi] = lax.dot_general(v_ref[lo:hi], dh, NT, preferred_element_type=F32)
            for i in range(lo // TILE, hi // TILE):
                cols = slice(i * TILE, (i + 1) * TILE)
                lse = lse_ref[h, 0:1, cols]
                dsum = dsum_ref[pl.ds(pl.multiple_of(h * 8, 8), 1), cols]
                for j in range(lo // TILE, hi // TILE):
                    rows = slice(j * TILE, (j + 1) * TILE)
                    s = s_ref[rows, cols]
                    if abs(j - i) <= 1:
                        e = jnp.exp(s + tile_ref[h, j - i + 1] - lse)
                    else:
                        e = jnp.exp(s - (lse - (below if j < i else above)))
                    ds = e * (dp_ref[rows, cols] - dsum)
                    p_ref[rows, cols] = e.astype(BF16)
                    ds_ref[rows, cols] = ds.astype(BF16)
                    if abs(j - i) <= 1:
                        near_ref[h, j - i + 1] += ds
                    else:
                        side = int(j > i)
                        far_sum[side] = far_sum[side] + jnp.sum(ds.reshape(TILE // 8, 8, TILE), axis=0)
            dv = lax.dot_general(p_ref[lo:hi, lo:hi], dh, NN, preferred_element_type=F32)
            dk = lax.dot_general(ds_ref[lo:hi, lo:hi], qh, NN, preferred_element_type=F32)
            dva_ref[lo:hi] = jnp.where(mask, dv, dva_ref[lo:hi])
            dka_ref[lo:hi] = jnp.where(mask, dk, dka_ref[lo:hi])
            head = pl.ds(pl.multiple_of(h * 64, 64), 64)
            dqt_ref[head, lo:hi] = lax.dot_general(
                kt_ref[head, lo:hi], ds_ref[lo:hi, lo:hi], NN, preferred_element_type=F32
            )
        far_ref[h, 0] = far_sum[0]
        far_ref[h, 1] = far_sum[1]

    @pl.loop(0, heads)
    def _(h):
        mask = (lane // 64) == h

        @pl.when(one_example)
        def _():
            blocks(h, mask, ((0, length),))

        @pl.when(jnp.logical_not(one_example))
        def _():
            blocks(h, mask, tuple((lo, lo + SEG) for lo in range(0, length, SEG)))

    dqkv_ref[:, :width] = jnp.transpose(dqt_ref[...]).astype(BF16)
    dqkv_ref[:, width : 2 * width] = dka_ref[...].astype(BF16)
    dqkv_ref[:, 2 * width :] = dva_ref[...].astype(BF16)


def attn_bwd(seg, bias, qkv, o, do, lse, tiles):
    length, width = o.shape
    heads = width // 64
    vmem = pl.BlockSpec(memory_space=pltpu.VMEM)
    smem = pl.BlockSpec(memory_space=pltpu.SMEM)
    return pl.pallas_call(
        attn_bwd_kernel,
        out_shape=(
            jax.ShapeDtypeStruct((length, 3 * width), BF16),
            jax.ShapeDtypeStruct((heads, 3, TILE, TILE), F32),
            jax.ShapeDtypeStruct((heads, 2, 8, TILE), F32),
        ),
        in_specs=[smem, smem] + [vmem] * 5,
        out_specs=(vmem,) * 3,
        scratch_shapes=[
            pltpu.VMEM((length, length), F32),
            pltpu.VMEM((length, length), F32),
            pltpu.VMEM((length, length), BF16),
            pltpu.VMEM((length, length), BF16),
            pltpu.VMEM((8 * heads, length), F32),
            pltpu.VMEM((width, length), BF16),
            pltpu.VMEM((width, length), F32),
            pltpu.VMEM((length, width), F32),
            pltpu.VMEM((length, width), F32),
        ],
        compiler_params=pltpu.CompilerParams(vmem_limit_bytes=48 << 20),
        cost_estimate=SMALL,
        name="attn_bwd",
    )(seg, bias, qkv, o, do, lse, tiles)


def tanh_gelu(u):
    scale = 0.7978845608028654
    t = jnp.tanh(scale * (u + 0.044715 * (u * u * u)))
    half = 0.5 * (1.0 + t)
    slope = half + (0.5 * u) * (1.0 - t * t) * (scale * (1.0 + 0.134145 * (u * u)))
    return u * half, slope


def ffn_kernel(
    x_ref, c_ref, weights_ref,
    dtwo_ref, ffo_ref, hidden_ref, dgate_ref, dup_ref,
    gate_w, up_w, down_w, sems,
):
    ring, halves, rows, half = weights_ref.shape
    units = rows // 3
    scratches = (gate_w, up_w, down_w)
    copies = [[], [], []]
    for m in range(3):
        for q in range(ring):
            for n in range(halves):
                copies[m].append(
                    pltpu.make_async_copy(
                        weights_ref.at[q, n, m * units : (m + 1) * units],
                        scratches[m].at[q * units : (q + 1) * units, n * half : (n + 1) * half],
                        sems.at[m, halves * q + n],
                    )
                )
    for group in copies:
        for copy in group:
            copy.start()
    for copy in copies[0]:
        copy.wait()
    gate = lax.dot_general(x_ref[...], gate_w[...], NT, preferred_element_type=F32)
    for copy in copies[1]:
        copy.wait()
    up = lax.dot_general(x_ref[...], up_w[...], NT, preferred_element_type=F32)
    for copy in copies[2]:
        copy.wait()
    d_hidden = lax.dot_general(c_ref[...], down_w[...], NT, preferred_element_type=F32)
    value, slope = tanh_gelu(gate)
    hidden = (value * up).astype(BF16)
    d_gate = (d_hidden * up * slope).astype(BF16)
    d_up = (d_hidden * value).astype(BF16)
    hidden_ref[...] = hidden
    dgate_ref[...] = d_gate
    dup_ref[...] = d_up
    dtwo_ref[...] = (
        lax.dot_general(d_gate, gate_w[...], NN, preferred_element_type=F32)
        + lax.dot_general(d_up, up_w[...], NN, preferred_element_type=F32)
    ).astype(dtwo_ref.dtype)
    ffo_ref[...] = lax.dot_general(hidden, down_w[...], NN, preferred_element_type=F32).astype(ffo_ref.dtype)


def ffn(x, c, weights):
    tokens, width = x.shape
    ring, halves, rows, _ = weights.shape
    units = ring * rows // 3
    vmem = pl.BlockSpec(memory_space=pltpu.VMEM)
    anywhere = pl.BlockSpec(memory_space=pl.ANY)
    wide = jax.ShapeDtypeStruct((tokens, width), BF16)
    inner = jax.ShapeDtypeStruct((tokens, units), BF16)
    return pl.pallas_call(
        ffn_kernel,
        out_shape=(wide, wide, inner, inner, inner),
        in_specs=[vmem, vmem, anywhere],
        out_specs=(vmem,) * 5,
        scratch_shapes=[pltpu.VMEM((units, width), BF16)] * 3 + [pltpu.SemaphoreType.DMA((3, halves * ring))],
        compiler_params=pltpu.CompilerParams(vmem_limit_bytes=40 << 20),
        cost_estimate=SMALL,
        name="ffn",
    )(x, c, weights)


def ffn_grads_kernel(n, *refs):
    sources = [refs[i * n : (i + 1) * n] for i in range(5)]
    out_ref = refs[5 * n]
    held = refs[5 * n + 1 : 5 * n + 6]
    sems = refs[5 * n + 6]
    ring, halves, rows, half = out_ref.shape
    units = rows // 3
    tokens = sources[0][0].shape[0]
    copies = [
        [
            pltpu.make_async_copy(ref, target.at[j * tokens : (j + 1) * tokens], sems.at[i, j])
            for j, ref in enumerate(group)
        ]
        for i, (group, target) in enumerate(zip(sources, held))
    ]
    for group in copies:
        for copy in group:
            copy.start()
    waited = set()
    for m, (lhs, rhs) in ((2, (0, 1)), (0, (2, 3)), (1, (4, 3))):
        for i in (lhs, rhs):
            if i not in waited:
                waited.add(i)
                for copy in copies[i]:
                    copy.wait()
        grad = lax.dot_general(held[lhs][...], held[rhs][...], TN, preferred_element_type=F32).astype(BF16)
        for q in range(ring):
            for k in range(halves):
                out_ref[q, k, m * units : (m + 1) * units] = grad[
                    q * units : (q + 1) * units, k * half : (k + 1) * half
                ]


def ffn_grads(hs, cs, gs, xs, us, ring):
    rows, width = xs[0].shape
    units = hs[0].shape[1]
    n = len(xs)
    vmem = pl.BlockSpec(memory_space=pltpu.VMEM)
    anywhere = pl.BlockSpec(memory_space=pl.ANY)
    shape = jax.ShapeDtypeStruct((ring, 2, 3 * units // ring, width // 2), BF16)
    wide, inner = pltpu.VMEM((n * rows, width), BF16), pltpu.VMEM((n * rows, units), BF16)
    return pl.pallas_call(
        functools.partial(ffn_grads_kernel, n),
        out_shape=shape,
        in_specs=[anywhere] * (5 * n),
        out_specs=vmem,
        scratch_shapes=[inner, wide, inner, wide, inner, pltpu.SemaphoreType.DMA((5, n))],
        compiler_params=pltpu.CompilerParams(vmem_limit_bytes=58 << 20),
        cost_estimate=SMALL,
        name="ffn_grads",
    )(*hs, *cs, *gs, *xs, *us)


def normed_grad_kernel(d_ref, w_ref, out_ref):
    out_ref[...] = lax.dot_general(d_ref[...], w_ref[...], NT, preferred_element_type=F32).astype(BF16)


def normed_grad(d, w):
    vmem = pl.BlockSpec(memory_space=pltpu.VMEM)
    return pl.pallas_call(
        normed_grad_kernel,
        out_shape=jax.ShapeDtypeStruct((d.shape[0], w.shape[0]), BF16),
        in_specs=[vmem, vmem],
        out_specs=vmem,
        compiler_params=pltpu.CompilerParams(vmem_limit_bytes=24 << 20),
        cost_estimate=SMALL,
        name="normed_grad",
    )(d, w)


def late_grads_kernel(where_ref, *refs):
    blocks = refs[:-10]
    d_ref, w_ref, o_ref, da_ref, keep_ref, give_ref, gain_ref, x_ref, held, sems = refs[-10:]
    core, chip = where_ref[0], where_ref[1]
    chips, _, half = keep_ref.shape
    ring = len(blocks)
    copies = []
    for s, block in enumerate(blocks):
        first = lax.rem(where_ref[3] + ring - s, ring) * block.shape[0]
        target = x_ref.at[pl.ds(pl.multiple_of(first, 32), block.shape[0])]
        copies.append(pltpu.make_async_copy(block, target, sems.at[s]))
    for copy in copies:
        copy.start()
    width = x_ref.shape[1]
    rows = width // (2 * chips)
    out_rows = o_ref.shape[1] // (ring * chips)
    mid = rows + rows // 2
    for n, out_ref in enumerate((give_ref, keep_ref)):
        start = pl.multiple_of((core ^ (1 - n)) * half, 128)
        held[...] = lax.dot_general(
            o_ref[...], da_ref[:, pl.ds(start, half)], TN, preferred_element_type=F32
        ).astype(BF16)
        for r in range(chips):
            for q in range(ring):
                first = (q * chips + (chip ^ r)) * out_rows
                out_ref[r, mid + q * out_rows : mid + (q + 1) * out_rows] = held[
                    pl.ds(pl.multiple_of(first, out_rows), out_rows)
                ]
    for copy in copies:
        copy.wait()
    for n, out_ref in enumerate((give_ref, keep_ref)):
        for r in range(chips):
            block = (core ^ (1 - n)) * chips + (chip ^ r)
            start = pl.multiple_of(block * rows, 128)
            grad = lax.dot_general(x_ref[:, pl.ds(start, rows)], d_ref[...], TN, preferred_element_type=F32)
            low = grad.astype(BF16)
            out_ref[r, :rows] = low[:, :half]
            out_ref[r, rows:mid, : half // 2] = low[: rows // 2, half:]
            out_ref[r, rows:mid, half // 2 :] = low[rows // 2 :, half:]
            line = jnp.sum(grad * w_ref[pl.ds(start, rows)].astype(F32), axis=1, keepdims=True)
            gain_ref[pl.ds(block, 1)] = jnp.transpose(jnp.broadcast_to(line, (rows, rows)))[:1]


def late_grads(where, blocks, d, w, o, d_attn):
    width = w.shape[0]
    rows = width // 8
    vmem = pl.BlockSpec(memory_space=pltpu.VMEM)
    shape = jax.ShapeDtypeStruct((4, rows + rows // 2 + o.shape[1] // 4, width // 2), BF16)
    return pl.pallas_call(
        late_grads_kernel,
        out_shape=(shape, shape, jax.ShapeDtypeStruct((8, rows), F32)),
        in_specs=[pl.BlockSpec(memory_space=pltpu.SMEM)] + [pl.BlockSpec(memory_space=pl.ANY)] * len(blocks) + [vmem] * 4,
        out_specs=(vmem,) * 3,
        scratch_shapes=[
            pltpu.VMEM((d.shape[0], width), BF16),
            pltpu.VMEM((o.shape[1], width // 2), BF16),
            pltpu.SemaphoreType.DMA((len(blocks),)),
        ],
        compiler_params=pltpu.CompilerParams(vmem_limit_bytes=56 << 20),
        cost_estimate=SMALL,
        name="late_grads",
    )(where, *blocks, d, w, o, d_attn)


def place_kernel(where_ref, own_ref, other_ref, *out_refs):
    core, chip = where_ref[0], where_ref[1]
    chips, _, half = own_ref.shape
    first = 0
    for target in out_refs:
        units = target.shape[0] // chips
        for r in range(chips):
            rows = pl.ds(pl.multiple_of((chip ^ r) * units, 8), units)
            for n, ref in enumerate((own_ref, other_ref)):
                columns = pl.ds(pl.multiple_of((core ^ n) * half, 128), half)
                target[rows, columns] = ref[r, first : first + units].astype(F32)
        first += units


def place(where, own, other, sizes):
    chips, _, half = own.shape
    vmem = pl.BlockSpec(memory_space=pltpu.VMEM)
    return pl.pallas_call(
        place_kernel,
        out_shape=tuple(jax.ShapeDtypeStruct((chips * size, 2 * half), F32) for size in sizes),
        in_specs=[pl.BlockSpec(memory_space=pltpu.SMEM), vmem, vmem],
        out_specs=(vmem,) * len(sizes),
        compiler_params=pltpu.CompilerParams(vmem_limit_bytes=40 << 20),
        cost_estimate=SMALL,
        name="place",
    )(where, own, other)


def place_late_kernel(where_ref, own_ref, other_ref, *out_refs):
    core, chip = where_ref[0], where_ref[1]
    chips, total, half = own_ref.shape
    projections, out_ref = out_refs[:3], out_refs[3]
    rows, part = projections[0].shape[0] // (2 * chips), projections[0].shape[1]
    mid = rows + rows // 2
    for n, ref in enumerate((own_ref, other_ref)):
        for r in range(chips):
            start = ((core ^ n) * chips + (chip ^ r)) * rows
            target = pl.ds(pl.multiple_of(start, 8), rows)
            for i in range(2):
                projections[i][target] = ref[r, :rows, i * part : (i + 1) * part].astype(F32)
            for i in range(2):
                target = pl.ds(pl.multiple_of(start + i * (rows // 2), 8), rows // 2)
                projections[2][target] = ref[r, rows:mid, i * part : (i + 1) * part].astype(F32)
            start = pl.multiple_of((chip ^ r) * (total - mid), 8)
            columns = pl.ds(pl.multiple_of((core ^ n) * half, 128), half)
            out_ref[pl.ds(start, total - mid), columns] = ref[r, mid:].astype(F32)


def place_late(where, own, other, rows):
    chips, total, half = own.shape
    vmem = pl.BlockSpec(memory_space=pltpu.VMEM)
    projection = jax.ShapeDtypeStruct((2 * chips * rows, half // 2), F32)
    out_rows = chips * (total - rows - rows // 2)
    return pl.pallas_call(
        place_late_kernel,
        out_shape=(projection,) * 3 + (jax.ShapeDtypeStruct((out_rows, 2 * half), F32),),
        in_specs=[pl.BlockSpec(memory_space=pltpu.SMEM), vmem, vmem],
        out_specs=(vmem,) * 4,
        cost_estimate=SMALL,
        name="place_late",
    )(where, own, other)


def place_out_kernel(where_ref, mine_ref, other_ref, out_ref):
    chips, ring, rows, _ = mine_ref.shape
    core, chip, z = where_ref[0], where_ref[1], where_ref[3]
    for s in range(ring):
        quarter = lax.rem(z + ring - s, ring)
        for r in range(chips):
            for n, ref in enumerate((mine_ref, other_ref)):
                start = ((quarter * chips + (chip ^ r)) * 2 + (core ^ n)) * rows
                out_ref[pl.ds(pl.multiple_of(start, rows), rows)] = ref[r, s]


def place_out(where, mine, other):
    chips, ring, rows, width = mine.shape
    vmem = pl.BlockSpec(memory_space=pltpu.VMEM)
    return pl.pallas_call(
        place_out_kernel,
        out_shape=jax.ShapeDtypeStruct((2 * chips * ring * rows, width), mine.dtype),
        in_specs=[pl.BlockSpec(memory_space=pltpu.SMEM), vmem, vmem],
        out_specs=vmem,
        cost_estimate=SMALL,
        name="place_out",
    )(where, mine, other)


ROWS_AXES = ("chips", "core")


def swap(value, mask):
    size = lax.axis_size(ROWS_AXES)
    return lax.ppermute(value, ROWS_AXES, [(i, i ^ mask) for i in range(size)])


def shift(value, step):
    size = lax.axis_size("tensor")
    return lax.ppermute(value, "tensor", [(i, (i + step) % size) for i in range(size)])


def add(left, right):
    return (left.astype(F32) + right.astype(F32)).astype(BF16)


def after(value, *others):
    return lax.optimization_barrier((value, *others))[0]


def bits_from(first):
    bit = first
    while bit < lax.axis_size(ROWS_AXES):
        yield bit
        bit *= 2


def sum_rows(value):
    value = sum(to_chips(value))
    for bit in (1, *bits_from(8)):
        value = value + swap(value, bit)
    return value


def sum_ring(value):
    return value + shift(value, 1) + shift(value, 2) + shift(value, 3)


def dot(left, right, dims=NN):
    return lax.dot_general(left, right, dims, preferred_element_type=F32)


def inverse_rms(values):
    return lax.rsqrt(jnp.mean(values * values, axis=-1, keepdims=True) + EPSILON)


CHIPS = (0, 1, 2, 3)


def to_chips(value):
    return [value] + [swap(value, 2 * mask) for mask in CHIPS[1:]]


def local(
    tokens,
    segment_ids,
    norm1_gain,
    w_query,
    w_key,
    w_value,
    w_out,
    rel_bias,
    norm2_gain,
    gate_weight_matrix,
    upward_weight,
    downward_weight,
    cotangent,
):
    shard, rows_here, width = tokens.shape
    length = segment_ids.shape[1]
    heads = rel_bias.shape[1]
    feats = w_query.shape[1]
    units = downward_weight.shape[0]
    ring = lax.axis_size("tensor")
    n_dp = lax.axis_size(ROWS_AXES)
    z = lax.axis_index("tensor")
    dp = lax.axis_index(ROWS_AXES)
    core = dp & 1
    chip = (dp >> 1) & 3
    where = jnp.stack([core, chip, dp, z]).astype(jnp.int32)

    x_low = tokens.reshape(shard, width)
    cot = cotangent.reshape(shard, width)
    tiles = bias_tiles(rel_bias)
    w_qkv = jnp.concatenate([w_query, w_key, w_value], axis=1)

    out_rows = feats // 8
    out_piece = lax.dynamic_slice_in_dim(w_out, (2 * chip + core) * out_rows, out_rows, 0)
    cs = to_chips(cot)
    sent = jnp.concatenate([x_low, out_piece], axis=0)
    blocks, normed_blocks, qkv_blocks = [], [], []
    for s in range(ring):
        if s == ring - 1:
            sent = after(sent, tiles, qkv_blocks[1], *cs)
        if s:
            sent = shift(sent, 1)
        values = sent[:shard].astype(F32)
        normed = (values * inverse_rms(values) * norm1_gain).astype(BF16)
        blocks.append(sent)
        normed_blocks.append(normed)
        qkv_blocks.append(dot(normed, w_qkv).astype(BF16))
    out_ring = jnp.stack([block[shard:] for block in blocks])
    out_chips = to_chips(out_ring)

    def unit_rows(array):
        return lax.dynamic_slice(array, (chip * (units // 4), core * (width // 2)), (units // 4, width // 2))

    pack = jnp.concatenate(
        [
            unit_rows(jnp.transpose(gate_weight_matrix)),
            unit_rows(jnp.transpose(upward_weight)),
            unit_rows(downward_weight),
        ],
        axis=0,
    )
    weights = lax.all_gather(after(pack, blocks[3]), ("tensor", "core"), axis=0)
    weights = weights.reshape(ring, 2, *pack.shape)

    qkv = jnp.zeros((length, 3 * feats), BF16)
    for s, block in enumerate(qkv_blocks):
        qkv = lax.dynamic_update_slice_in_dim(qkv, block, ((z - s) % ring) * shard, 0)

    o_row, lse = attn_fwd(segment_ids, rel_bias, qkv, tiles)
    out_mine = after(jnp.stack(out_chips), o_row)
    out_all = place_out(where, out_mine, swap(out_mine, 1))
    o_home = lax.all_to_all(o_row, "tensor", 0, 1, tiled=True)
    attn = dot(o_home, out_all)
    x_one = x_low.astype(F32) + attn
    r_two = inverse_rms(x_one)
    norm_two = (x_one * r_two * norm2_gain).astype(BF16)

    xs = to_chips(norm_two)
    parts = []
    for x, c in zip(xs, cs):
        if parts:
            x = after(x, parts[-1][0])
        parts.append(ffn(x, c, weights))

    def returns(which, *others):
        terms = [after(part[which], *others) if others else part[which] for part in parts]
        return [terms[0]] + [swap(terms[mask], 2 * mask) for mask in CHIPS[1:]]

    def total_of(terms):
        return sum(term.astype(F32) for term in terms)

    back = returns(0)
    d_two = total_of(back)
    u_two = d_two * norm2_gain
    d_x_one = cot.astype(F32) + r_two * u_two - x_one * (
        r_two * r_two * r_two * jnp.mean(u_two * x_one, axis=-1, keepdims=True)
    )
    d_attn = d_x_one.astype(BF16)
    d_o = dot(d_attn, out_all, NT).astype(BF16)
    do_row = lax.all_to_all(d_o, "tensor", 1, 0, tiled=True)

    unit_grads = ffn_grads(
        [after(parts[0][2], d_o)] + [part[2] for part in parts[1:]],
        cs,
        [part[3] for part in parts],
        xs,
        [part[4] for part in parts],
        ring,
    )
    ffn_piece = lax.psum_scatter(
        after(unit_grads, do_row).reshape(-1, width // 2), ("tensor", "core"), scatter_dimension=0, tiled=True
    )

    def from_chips(pieces):
        return [pieces[0]] + [swap(pieces[r], 2 * r) for r in CHIPS[1:]]

    ffo_back = returns(1, do_row)
    ffo = total_of(ffo_back)
    y = x_one + ffo
    out_tokens = y.astype(BF16)
    grad_two = jnp.sum(d_two * x_one * r_two, axis=0)
    stats = jnp.stack([jnp.sum(attn * attn), jnp.sum(ffo * ffo), jnp.sum(y * y)])

    do_row = after(do_row, unit_grads)

    dqkv, near, far = attn_bwd(segment_ids, rel_bias, qkv, o_row, do_row, lse, tiles)
    dqkv = after(dqkv, *ffo_back)
    keep, give, grad_one = late_grads(where, normed_blocks, dqkv, w_qkv, o_home, d_attn)
    d_one_part = normed_grad(after(dqkv, give), w_qkv)
    d_one = lax.psum_scatter(after(d_one_part, ffn_piece), "tensor", scatter_dimension=0, tiled=True)
    near = after(near, give)
    row = width // 8
    stats = jnp.pad(stats, (0, row - 3)).reshape(1, row)
    small = jnp.concatenate([grad_two.reshape(8, row), grad_one, stats, bias_grad(near, far)], axis=0)
    got = total_of(from_chips(after(add(keep, swap(give, 1)), small))).astype(BF16)
    small = sum_rows(small)
    mid = got.shape[0] - feats
    by_ring = got[mid:].reshape(ring, feats // 4, width // 2)
    out_parts = [lax.dynamic_index_in_dim(by_ring, (z + s) % ring, 0, keepdims=False) for s in range(ring)]
    small_rows = jnp.pad(small[:17], ((0, 7), (0, 0))).reshape(6, width // 2)
    ring_sum = total_of(
        [
            shift(jnp.concatenate([part.astype(F32), small_rows], axis=0), s) if s else
            jnp.concatenate([part.astype(F32), small_rows], axis=0)
            for s, part in enumerate(out_parts)
        ]
    )
    out_piece = ring_sum[: feats // 4].astype(BF16)
    late = jnp.concatenate([got[:mid], out_piece], axis=0)
    for bit in bits_from(8):
        late = add(late, swap(late, bit))
    piece = after(ffn_piece, got, small)
    for bit in bits_from(8):
        piece = add(piece, swap(piece, bit))
    ffn_parts = to_chips(piece)
    grad_bias = small[17:, :heads]
    small = ring_sum[feats // 4 :].reshape(24, row)
    grad_norm2, grad_norm1 = small[:8].reshape(width), small[8:16].reshape(width) / norm1_gain
    stat_sums = small[16, :3]
    own = jnp.stack([after(part, late, small) for part in ffn_parts])
    late = to_chips(after(late, small))
    grad_gate, grad_up, grad_down = place(where, own, swap(own, 1), (units // 4,) * 3)
    grad_gate, grad_up = jnp.transpose(grad_gate), jnp.transpose(grad_up)
    count = shard * rows_here * width * n_dp * ring
    rms_stats = jnp.sqrt(stat_sums / count)

    late = jnp.stack([after(part, grad_down) for part in late])
    d_one = after(d_one, own).astype(F32)
    x_in = x_low.astype(F32)
    r_one = inverse_rms(x_in)
    u_one = d_one * norm1_gain
    grad_tokens = (
        d_x_one + r_one * u_one - x_in * (r_one * r_one * r_one * jnp.mean(u_one * x_in, axis=-1, keepdims=True))
    ).astype(BF16)

    late = after(late, grad_tokens)
    grad_query, grad_key, grad_value, grad_out = place_late(where, late, swap(late, 1), width // 8)

    shape = (shard, rows_here, width)
    return (
        out_tokens.reshape(shape),
        grad_tokens.reshape(shape),
        grad_norm1,
        grad_query,
        grad_key,
        grad_value,
        grad_out,
        grad_bias,
        grad_norm2,
        grad_gate,
        grad_up,
        grad_down,
        rms_stats,
    )


def solution(mesh):
    n_dp, ring = mesh.devices.shape
    by_core = Mesh(mesh.devices.reshape(n_dp // 2, 2, ring), (*ROWS_AXES, "tensor"))
    in_specs = (
        P("tensor", ROWS_AXES, None),
        P(ROWS_AXES, None),
        P(),
        P(None, "tensor"),
        P(None, "tensor"),
        P(None, "tensor"),
        P("tensor", None),
        P(None, "tensor"),
        P(),
        P(None, "tensor"),
        P(None, "tensor"),
        P("tensor", None),
        P("tensor", ROWS_AXES, None),
    )
    out_specs = (
        P("tensor", ROWS_AXES, None),
        P("tensor", ROWS_AXES, None),
        P(),
        P(None, "tensor"),
        P(None, "tensor"),
        P(None, "tensor"),
        P("tensor", None),
        P(None, "tensor"),
        P(),
        P(None, "tensor"),
        P(None, "tensor"),
        P("tensor", None),
        P(),
    )
    return jax.shard_map(local, mesh=by_core, in_specs=in_specs, out_specs=out_specs, check_vma=False)
```

```python
import functools
import jax
import jax.numpy as jnp
from jax import lax
from jax.experimental import pallas as pl
from jax.experimental.pallas import tpu as pltpu
from jax.sharding import Mesh, PartitionSpec as P

EPSILON = 1e-06
THRESHOLDS = (12, 16, 23, 32, 46, 64, 91)
TILE = 128
SEG = 384
NT = (((1,), (1,)), ((), ()))
NN = (((1,), (0,)), ((), ()))
NN = (((1,), (0,)), ((), ()))
TN = (((0,), (0,)), ((), ()))
F32 = jnp.float32
BF16 = jnp.bfloat16
SMALL = pl.CostEstimate(flops=1000, bytes_accessed=1000, transcendentals=0)


def bucket_of(offset):
    distance = jnp.abs(offset)
    far_bucket = 8 + sum(((distance >= threshold).astype(jnp.int32) for threshold in THRESHOLDS))
    return jnp.where(distance < 8, distance, far_bucket) + 16 * (offset > 0).astype(jnp.int32)


def tile_bucket(delta, key_axis):
    keys = lax.broadcasted_iota(jnp.int32, (TILE, TILE), key_axis)
    queries = lax.broadcasted_iota(jnp.int32, (TILE, TILE), 1 - key_axis)
    return bucket_of(TILE * delta + keys - queries)


def bias_tiles_kernel(bias_ref, out_ref):
    buckets, heads = bias_ref.shape
    for delta in (-1, 0, 1):
        bucket = tile_bucket(delta, 0)
        tiles = [jnp.zeros((TILE, TILE), F32) for _ in range(heads)]
        for b in range(buckets):
            hit = bucket == b
            tiles = [jnp.where(hit, bias_ref[b, h], t) for h, t in enumerate(tiles)]
        for h in range(heads):
            out_ref[h, delta + 1] = tiles[h]


def bias_tiles(rel_bias):
    return pl.pallas_call(
        bias_tiles_kernel,
        out_shape=jax.ShapeDtypeStruct((rel_bias.shape[1], 3, TILE, TILE), F32),
        in_specs=[pl.BlockSpec(memory_space=pltpu.SMEM)],
        out_specs=pl.BlockSpec(memory_space=pltpu.VMEM),
        name="bias_tiles",
    )(rel_bias)


def bias_grad_kernel(near_ref, far_ref, out_ref):
    heads = near_ref.shape[0]
    row = lax.broadcasted_iota(jnp.int32, (32, TILE), 0)
    lane = lax.broadcasted_iota(jnp.int32, (32, TILE), 1)
    bucket = [tile_bucket(delta, 0) for delta in (-1, 0, 1)]
    total = jnp.zeros((32, TILE), F32)
    for h in range(heads):
        near = [near_ref[h, d] for d in range(3)]
        for b in range(32):
            deltas = (0, 1) if b < 16 else (1, 2)
            part = sum(jnp.where(bucket[d] == b, near[d], 0.0) for d in deltas)
            part = jnp.sum(part.reshape(16, 8, TILE), axis=0)
            if b == 15:
                part = part + far_ref[h, 0]
            if b == 31:
                part = part + far_ref[h, 1]
            line = jnp.sum(part, axis=0, keepdims=True)
            total = jnp.where((row == b) & (lane == h), jnp.sum(line, axis=1, keepdims=True), total)
    out_ref[...] = total


def bias_grad(near, far):
    return pl.pallas_call(
        bias_grad_kernel,
        out_shape=jax.ShapeDtypeStruct((32, TILE), F32),
        name="bias_grad",
    )(near, far)


def attn_fwd_kernel(seg_ref, bias_ref, qkv_ref, tile_ref, o_ref, lse_ref, s_ref, p_ref, l_ref, vt_ref, ot_ref):
    length, width = o_ref.shape
    q_ref, k_ref, v_ref = (qkv_ref.at[:, n * width : (n + 1) * width] for n in range(3))
    heads = width // 64
    lane = lax.broadcasted_iota(jnp.int32, (1, width), 1)
    one_example = seg_ref[0, length - 1] == seg_ref[0, 0]
    vt_ref[...] = jnp.transpose(v_ref[...])

    def blocks(h, mask, spans):
        below = bias_ref[15, h]
        above = bias_ref[31, h]
        head = pl.ds(pl.multiple_of(h * 64, 64), 64)
        for lo, hi in spans:
            qh = jnp.where(mask, q_ref[lo:hi], jnp.zeros((), BF16))
            s_ref[lo:hi, lo:hi] = lax.dot_general(k_ref[lo:hi], qh, NT, preferred_element_type=F32)
            tiles = range(lo // TILE, hi // TILE)
            for i in tiles:
                cols = slice(i * TILE, (i + 1) * TILE)
                near_top, sides = None, {-1: None, 1: None}
                for j in tiles:
                    part = s_ref[j * TILE : (j + 1) * TILE, cols]
                    if abs(j - i) <= 1:
                        part = part + tile_ref[h, j - i + 1]
                        s_ref[j * TILE : (j + 1) * TILE, cols] = part
                    part = jnp.max(part.reshape(TILE // 8, 8, TILE), axis=0)
                    if abs(j - i) <= 1:
                        near_top = part if near_top is None else jnp.maximum(near_top, part)
                    else:
                        side = 1 if j > i else -1
                        sides[side] = part if sides[side] is None else jnp.maximum(sides[side], part)
                top = near_top
                for side, constant in ((-1, below), (1, above)):
                    if sides[side] is not None:
                        top = jnp.maximum(top, sides[side] + constant)
                top = jnp.max(top, axis=0, keepdims=True)
                total = jnp.zeros((8, TILE), F32)
                for j in tiles:
                    shift = top
                    if abs(j - i) > 1:
                        shift = top - (below if j < i else above)
                    e = jnp.exp(s_ref[j * TILE : (j + 1) * TILE, cols] - shift)
                    total = total + jnp.sum(e.reshape(TILE // 8, 8, TILE), axis=0)
                    p_ref[j * TILE : (j + 1) * TILE, cols] = e.astype(BF16)
                total = jnp.sum(total, axis=0, keepdims=True)
                l_ref[0:1, cols] = 1.0 / total
                lse_ref[h, 0:1, cols] = top + jnp.log(total)
            ot_ref[head, lo:hi] = (
                lax.dot_general(vt_ref[head, lo:hi], p_ref[lo:hi, lo:hi], NN, preferred_element_type=F32)
                * l_ref[0:1, lo:hi]
            )

    @pl.loop(0, heads)
    def _(h):
        mask = (lane // 64) == h

        @pl.when(one_example)
        def _():
            blocks(h, mask, ((0, length),))

        @pl.when(jnp.logical_not(one_example))
        def _():
            blocks(h, mask, tuple((lo, lo + SEG) for lo in range(0, length, SEG)))

    o_ref[...] = jnp.transpose(ot_ref[...]).astype(BF16)


def attn_fwd(seg, bias, qkv, tiles):
    length, width = qkv.shape[0], qkv.shape[1] // 3
    heads = width // 64
    vmem = pl.BlockSpec(memory_space=pltpu.VMEM)
    smem = pl.BlockSpec(memory_space=pltpu.SMEM)
    return pl.pallas_call(
        attn_fwd_kernel,
        out_shape=(
            jax.ShapeDtypeStruct((length, width), BF16),
            jax.ShapeDtypeStruct((heads, 8, length), F32),
        ),
        in_specs=[smem, smem, vmem, vmem],
        out_specs=(vmem, vmem),
        scratch_shapes=[
            pltpu.VMEM((length, length), F32),
            pltpu.VMEM((length, length), BF16),
            pltpu.VMEM((8, length), F32),
            pltpu.VMEM((width, length), BF16),
            pltpu.VMEM((width, length), F32),
        ],
        compiler_params=pltpu.CompilerParams(vmem_limit_bytes=40 << 20),
        cost_estimate=SMALL,
        name="attn_fwd",
    )(seg, bias, qkv, tiles)


def attn_bwd_kernel(
    seg_ref, bias_ref, qkv_ref, o_ref, do_ref, lse_ref, tile_ref,
    dqkv_ref, near_ref, far_ref,
    s_ref, dp_ref, p_ref, ds_ref, dsum_ref, kt_ref, dqt_ref, dka_ref, dva_ref,
):
    length, width = o_ref.shape
    q_ref, k_ref, v_ref = (qkv_ref.at[:, n * width : (n + 1) * width] for n in range(3))
    heads = width // 64
    lane = lax.broadcasted_iota(jnp.int32, (1, width), 1)
    one_example = seg_ref[0, length - 1] == seg_ref[0, 0]
    kt_ref[...] = jnp.transpose(k_ref[...])
    prod = o_ref[...].astype(F32) * do_ref[...].astype(F32)
    high = prod.astype(BF16)
    low = (prod - high.astype(F32)).astype(BF16)
    head_rows = (
        lax.broadcasted_iota(jnp.int32, (8 * heads, width), 1) // 64
        == lax.broadcasted_iota(jnp.int32, (8 * heads, width), 0) // 8
    ).astype(BF16)
    dsum_ref[...] = lax.dot_general(head_rows, high, NT, preferred_element_type=F32) + lax.dot_general(
        head_rows, low, NT, preferred_element_type=F32
    )
    def blocks(h, mask, spans):
        below = bias_ref[15, h]
        above = bias_ref[31, h]
        near_sum = [None, None, None]
        far_sum = [jnp.zeros((8, TILE), F32)] * 2
        zero = jnp.zeros((), BF16)
        for d in range(3):
            near_ref[h, d] = jnp.zeros((TILE, TILE), F32)
        for lo, hi in spans:
            qh = jnp.where(mask, q_ref[lo:hi], zero)
            dh = jnp.where(mask, do_ref[lo:hi], zero)
            s_ref[lo:hi, lo:hi] = lax.dot_general(k_ref[lo:hi], qh, NT, preferred_element_type=F32)
            dp_ref[lo:hi, lo:hi] = lax.dot_general(v_ref[lo:hi], dh, NT, preferred_element_type=F32)
            for i in range(lo // TILE, hi // TILE):
                cols = slice(i * TILE, (i + 1) * TILE)
                lse = lse_ref[h, 0:1, cols]
                dsum = dsum_ref[pl.ds(pl.multiple_of(h * 8, 8), 1), cols]
                for j in range(lo // TILE, hi // TILE):
                    rows = slice(j * TILE, (j + 1) * TILE)
                    s = s_ref[rows, cols]
                    if abs(j - i) <= 1:
                        e = jnp.exp(s + tile_ref[h, j - i + 1] - lse)
                    else:
                        e = jnp.exp(s - (lse - (below if j < i else above)))
                    ds = e * (dp_ref[rows, cols] - dsum)
                    p_ref[rows, cols] = e.astype(BF16)
                    ds_ref[rows, cols] = ds.astype(BF16)
                    if abs(j - i) <= 1:
                        near_ref[h, j - i + 1] += ds
                    else:
                        side = int(j > i)
                        far_sum[side] = far_sum[side] + jnp.sum(ds.reshape(TILE // 8, 8, TILE), axis=0)
            dv = lax.dot_general(p_ref[lo:hi, lo:hi], dh, NN, preferred_element_type=F32)
            dk = lax.dot_general(ds_ref[lo:hi, lo:hi], qh, NN, preferred_element_type=F32)
            dva_ref[lo:hi] = jnp.where(mask, dv, dva_ref[lo:hi])
            dka_ref[lo:hi] = jnp.where(mask, dk, dka_ref[lo:hi])
            head = pl.ds(pl.multiple_of(h * 64, 64), 64)
            dqt_ref[head, lo:hi] = lax.dot_general(
                kt_ref[head, lo:hi], ds_ref[lo:hi, lo:hi], NN, preferred_element_type=F32
            )
        far_ref[h, 0] = far_sum[0]
        far_ref[h, 1] = far_sum[1]

    @pl.loop(0, heads)
    def _(h):
        mask = (lane // 64) == h

        @pl.when(one_example)
        def _():
            blocks(h, mask, ((0, length),))

        @pl.when(jnp.logical_not(one_example))
        def _():
            blocks(h, mask, tuple((lo, lo + SEG) for lo in range(0, length, SEG)))

    dqkv_ref[:, :width] = jnp.transpose(dqt_ref[...]).astype(BF16)
    dqkv_ref[:, width : 2 * width] = dka_ref[...].astype(BF16)
    dqkv_ref[:, 2 * width :] = dva_ref[...].astype(BF16)


def attn_bwd(seg, bias, qkv, o, do, lse, tiles):
    length, width = o.shape
    heads = width // 64
    vmem = pl.BlockSpec(memory_space=pltpu.VMEM)
    smem = pl.BlockSpec(memory_space=pltpu.SMEM)
    return pl.pallas_call(
        attn_bwd_kernel,
        out_shape=(
            jax.ShapeDtypeStruct((length, 3 * width), BF16),
            jax.ShapeDtypeStruct((heads, 3, TILE, TILE), F32),
            jax.ShapeDtypeStruct((heads, 2, 8, TILE), F32),
        ),
        in_specs=[smem, smem] + [vmem] * 5,
        out_specs=(vmem,) * 3,
        scratch_shapes=[
            pltpu.VMEM((length, length), F32),
            pltpu.VMEM((length, length), F32),
            pltpu.VMEM((length, length), BF16),
            pltpu.VMEM((length, length), BF16),
            pltpu.VMEM((8 * heads, length), F32),
            pltpu.VMEM((width, length), BF16),
            pltpu.VMEM((width, length), F32),
            pltpu.VMEM((length, width), F32),
            pltpu.VMEM((length, width), F32),
        ],
        compiler_params=pltpu.CompilerParams(vmem_limit_bytes=48 << 20),
        cost_estimate=SMALL,
        name="attn_bwd",
    )(seg, bias, qkv, o, do, lse, tiles)


def tanh_gelu(u):
    scale = 0.7978845608028654
    t = jnp.tanh(scale * (u + 0.044715 * (u * u * u)))
    half = 0.5 * (1.0 + t)
    slope = half + (0.5 * u) * (1.0 - t * t) * (scale * (1.0 + 0.134145 * (u * u)))
    return u * half, slope


def ffn_kernel(
    x_ref, c_ref, weights_ref,
    dtwo_ref, ffo_ref, hidden_ref, dgate_ref, dup_ref,
    gate_w, up_w, down_w, sems,
):
    ring, halves, rows, half = weights_ref.shape
    units = rows // 3
    scratches = (gate_w, up_w, down_w)
    copies = [[], [], []]
    for m in range(3):
        for q in range(ring):
            for n in range(halves):
                copies[m].append(
                    pltpu.make_async_copy(
                        weights_ref.at[q, n, m * units : (m + 1) * units],
                        scratches[m].at[q * units : (q + 1) * units, n * half : (n + 1) * half],
                        sems.at[m, halves * q + n],
                    )
                )
    for group in copies:
        for copy in group:
            copy.start()
    for copy in copies[0]:
        copy.wait()
    gate = lax.dot_general(x_ref[...], gate_w[...], NT, preferred_element_type=F32)
    for copy in copies[1]:
        copy.wait()
    up = lax.dot_general(x_ref[...], up_w[...], NT, preferred_element_type=F32)
    for copy in copies[2]:
        copy.wait()
    d_hidden = lax.dot_general(c_ref[...], down_w[...], NT, preferred_element_type=F32)
    value, slope = tanh_gelu(gate)
    hidden = (value * up).astype(BF16)
    d_gate = (d_hidden * up * slope).astype(BF16)
    d_up = (d_hidden * value).astype(BF16)
    hidden_ref[...] = hidden
    dgate_ref[...] = d_gate
    dup_ref[...] = d_up
    dtwo_ref[...] = (
        lax.dot_general(d_gate, gate_w[...], NN, preferred_element_type=F32)
        + lax.dot_general(d_up, up_w[...], NN, preferred_element_type=F32)
    ).astype(dtwo_ref.dtype)
    ffo_ref[...] = lax.dot_general(hidden, down_w[...], NN, preferred_element_type=F32).astype(ffo_ref.dtype)


def ffn(x, c, weights):
    tokens, width = x.shape
    ring, halves, rows, _ = weights.shape
    units = ring * rows // 3
    vmem = pl.BlockSpec(memory_space=pltpu.VMEM)
    anywhere = pl.BlockSpec(memory_space=pl.ANY)
    wide = jax.ShapeDtypeStruct((tokens, width), BF16)
    inner = jax.ShapeDtypeStruct((tokens, units), BF16)
    return pl.pallas_call(
        ffn_kernel,
        out_shape=(wide, wide, inner, inner, inner),
        in_specs=[vmem, vmem, anywhere],
        out_specs=(vmem,) * 5,
        scratch_shapes=[pltpu.VMEM((units, width), BF16)] * 3 + [pltpu.SemaphoreType.DMA((3, halves * ring))],
        compiler_params=pltpu.CompilerParams(vmem_limit_bytes=40 << 20),
        cost_estimate=SMALL,
        name="ffn",
    )(x, c, weights)


def ffn_grads_kernel(n, *refs):
    sources = [refs[i * n : (i + 1) * n] for i in range(5)]
    out_ref = refs[5 * n]
    held = refs[5 * n + 1 : 5 * n + 6]
    sems = refs[5 * n + 6]
    ring, halves, rows, half = out_ref.shape
    units = rows // 3
    tokens = sources[0][0].shape[0]
    copies = [
        [
            pltpu.make_async_copy(ref, target.at[j * tokens : (j + 1) * tokens], sems.at[i, j])
            for j, ref in enumerate(group)
        ]
        for i, (group, target) in enumerate(zip(sources, held))
    ]
    for group in copies:
        for copy in group:
            copy.start()
    waited = set()
    for m, (lhs, rhs) in ((2, (0, 1)), (0, (2, 3)), (1, (4, 3))):
        for i in (lhs, rhs):
            if i not in waited:
                waited.add(i)
                for copy in copies[i]:
                    copy.wait()
        grad = lax.dot_general(held[lhs][...], held[rhs][...], TN, preferred_element_type=F32).astype(BF16)
        for q in range(ring):
            for k in range(halves):
                out_ref[q, k, m * units : (m + 1) * units] = grad[
                    q * units : (q + 1) * units, k * half : (k + 1) * half
                ]


def ffn_grads(hs, cs, gs, xs, us, ring):
    rows, width = xs[0].shape
    units = hs[0].shape[1]
    n = len(xs)
    vmem = pl.BlockSpec(memory_space=pltpu.VMEM)
    anywhere = pl.BlockSpec(memory_space=pl.ANY)
    shape = jax.ShapeDtypeStruct((ring, 2, 3 * units // ring, width // 2), BF16)
    wide, inner = pltpu.VMEM((n * rows, width), BF16), pltpu.VMEM((n * rows, units), BF16)
    return pl.pallas_call(
        functools.partial(ffn_grads_kernel, n),
        out_shape=shape,
        in_specs=[anywhere] * (5 * n),
        out_specs=vmem,
        scratch_shapes=[inner, wide, inner, wide, inner, pltpu.SemaphoreType.DMA((5, n))],
        compiler_params=pltpu.CompilerParams(vmem_limit_bytes=58 << 20),
        cost_estimate=SMALL,
        name="ffn_grads",
    )(*hs, *cs, *gs, *xs, *us)


def normed_grad_kernel(d_ref, w_ref, out_ref):
    out_ref[...] = lax.dot_general(d_ref[...], w_ref[...], NT, preferred_element_type=F32).astype(BF16)


def normed_grad(d, w):
    vmem = pl.BlockSpec(memory_space=pltpu.VMEM)
    return pl.pallas_call(
        normed_grad_kernel,
        out_shape=jax.ShapeDtypeStruct((d.shape[0], w.shape[0]), BF16),
        in_specs=[vmem, vmem],
        out_specs=vmem,
        compiler_params=pltpu.CompilerParams(vmem_limit_bytes=24 << 20),
        cost_estimate=SMALL,
        name="normed_grad",
    )(d, w)


def late_grads_kernel(where_ref, *refs):
    blocks = refs[:-10]
    d_ref, w_ref, o_ref, da_ref, keep_ref, give_ref, gain_ref, x_ref, held, sems = refs[-10:]
    core, chip = where_ref[0], where_ref[1]
    chips, _, half = keep_ref.shape
    ring = len(blocks)
    copies = []
    for s, block in enumerate(blocks):
        first = lax.rem(where_ref[3] + ring - s, ring) * block.shape[0]
        target = x_ref.at[pl.ds(pl.multiple_of(first, 32), block.shape[0])]
        copies.append(pltpu.make_async_copy(block, target, sems.at[s]))
    for copy in copies:
        copy.start()
    width = x_ref.shape[1]
    rows = width // (2 * chips)
    out_rows = o_ref.shape[1] // (ring * chips)
    mid = rows + rows // 2
    for n, out_ref in enumerate((give_ref, keep_ref)):
        start = pl.multiple_of((core ^ (1 - n)) * half, 128)
        held[...] = lax.dot_general(
            o_ref[...], da_ref[:, pl.ds(start, half)], TN, preferred_element_type=F32
        ).astype(BF16)
        for r in range(chips):
            for q in range(ring):
                first = (q * chips + (chip ^ r)) * out_rows
                out_ref[r, mid + q * out_rows : mid + (q + 1) * out_rows] = held[
                    pl.ds(pl.multiple_of(first, out_rows), out_rows)
                ]
    for copy in copies:
        copy.wait()
    for n, out_ref in enumerate((give_ref, keep_ref)):
        for r in range(chips):
            block = (core ^ (1 - n)) * chips + (chip ^ r)
            start = pl.multiple_of(block * rows, 128)
            grad = lax.dot_general(x_ref[:, pl.ds(start, rows)], d_ref[...], TN, preferred_element_type=F32)
            low = grad.astype(BF16)
            out_ref[r, :rows] = low[:, :half]
            out_ref[r, rows:mid, : half // 2] = low[: rows // 2, half:]
            out_ref[r, rows:mid, half // 2 :] = low[rows // 2 :, half:]
            line = jnp.sum(grad * w_ref[pl.ds(start, rows)].astype(F32), axis=1, keepdims=True)
            gain_ref[pl.ds(block, 1)] = jnp.transpose(jnp.broadcast_to(line, (rows, rows)))[:1]


def late_grads(where, blocks, d, w, o, d_attn):
    width = w.shape[0]
    rows = width // 8
    vmem = pl.BlockSpec(memory_space=pltpu.VMEM)
    shape = jax.ShapeDtypeStruct((4, rows + rows // 2 + o.shape[1] // 4, width // 2), BF16)
    return pl.pallas_call(
        late_grads_kernel,
        out_shape=(shape, shape, jax.ShapeDtypeStruct((8, rows), F32)),
        in_specs=[pl.BlockSpec(memory_space=pltpu.SMEM)] + [pl.BlockSpec(memory_space=pl.ANY)] * len(blocks) + [vmem] * 4,
        out_specs=(vmem,) * 3,
        scratch_shapes=[
            pltpu.VMEM((d.shape[0], width), BF16),
            pltpu.VMEM((o.shape[1], width // 2), BF16),
            pltpu.SemaphoreType.DMA((len(blocks),)),
        ],
        compiler_params=pltpu.CompilerParams(vmem_limit_bytes=56 << 20),
        cost_estimate=SMALL,
        name="late_grads",
    )(where, *blocks, d, w, o, d_attn)


def place_kernel(where_ref, own_ref, other_ref, *out_refs):
    core, chip = where_ref[0], where_ref[1]
    chips, _, half = own_ref.shape
    first = 0
    for target in out_refs:
        units = target.shape[0] // chips
        for r in range(chips):
            rows = pl.ds(pl.multiple_of((chip ^ r) * units, 8), units)
            for n, ref in enumerate((own_ref, other_ref)):
                columns = pl.ds(pl.multiple_of((core ^ n) * half, 128), half)
                target[rows, columns] = ref[r, first : first + units].astype(F32)
        first += units


def place(where, own, other, sizes):
    chips, _, half = own.shape
    vmem = pl.BlockSpec(memory_space=pltpu.VMEM)
    return pl.pallas_call(
        place_kernel,
        out_shape=tuple(jax.ShapeDtypeStruct((chips * size, 2 * half), F32) for size in sizes),
        in_specs=[pl.BlockSpec(memory_space=pltpu.SMEM), vmem, vmem],
        out_specs=(vmem,) * len(sizes),
        compiler_params=pltpu.CompilerParams(vmem_limit_bytes=40 << 20),
        cost_estimate=SMALL,
        name="place",
    )(where, own, other)


def place_late_kernel(where_ref, own_ref, other_ref, *out_refs):
    core, chip = where_ref[0], where_ref[1]
    chips, total, half = own_ref.shape
    projections, out_ref = out_refs[:3], out_refs[3]
    rows, part = projections[0].shape[0] // (2 * chips), projections[0].shape[1]
    mid = rows + rows // 2
    for n, ref in enumerate((own_ref, other_ref)):
        for r in range(chips):
            start = ((core ^ n) * chips + (chip ^ r)) * rows
            target = pl.ds(pl.multiple_of(start, 8), rows)
            for i in range(2):
                projections[i][target] = ref[r, :rows, i * part : (i + 1) * part].astype(F32)
            for i in range(2):
                target = pl.ds(pl.multiple_of(start + i * (rows // 2), 8), rows // 2)
                projections[2][target] = ref[r, rows:mid, i * part : (i + 1) * part].astype(F32)
            start = pl.multiple_of((chip ^ r) * (total - mid), 8)
            columns = pl.ds(pl.multiple_of((core ^ n) * half, 128), half)
            out_ref[pl.ds(start, total - mid), columns] = ref[r, mid:].astype(F32)


def place_late(where, own, other, rows):
    chips, total, half = own.shape
    vmem = pl.BlockSpec(memory_space=pltpu.VMEM)
    projection = jax.ShapeDtypeStruct((2 * chips * rows, half // 2), F32)
    out_rows = chips * (total - rows - rows // 2)
    return pl.pallas_call(
        place_late_kernel,
        out_shape=(projection,) * 3 + (jax.ShapeDtypeStruct((out_rows, 2 * half), F32),),
        in_specs=[pl.BlockSpec(memory_space=pltpu.SMEM), vmem, vmem],
        out_specs=(vmem,) * 4,
        cost_estimate=SMALL,
        name="place_late",
    )(where, own, other)


def place_out_kernel(where_ref, mine_ref, other_ref, out_ref):
    chips, ring, rows, _ = mine_ref.shape
    core, chip, z = where_ref[0], where_ref[1], where_ref[3]
    for s in range(ring):
        quarter = lax.rem(z + ring - s, ring)
        for r in range(chips):
            for n, ref in enumerate((mine_ref, other_ref)):
                start = ((quarter * chips + (chip ^ r)) * 2 + (core ^ n)) * rows
                out_ref[pl.ds(pl.multiple_of(start, rows), rows)] = ref[r, s]


def place_out(where, mine, other):
    chips, ring, rows, width = mine.shape
    vmem = pl.BlockSpec(memory_space=pltpu.VMEM)
    return pl.pallas_call(
        place_out_kernel,
        out_shape=jax.ShapeDtypeStruct((2 * chips * ring * rows, width), mine.dtype),
        in_specs=[pl.BlockSpec(memory_space=pltpu.SMEM), vmem, vmem],
        out_specs=vmem,
        cost_estimate=SMALL,
        name="place_out",
    )(where, mine, other)


ROWS_AXES = ("chips", "core")


def swap(value, mask):
    size = lax.axis_size(ROWS_AXES)
    return lax.ppermute(value, ROWS_AXES, [(i, i ^ mask) for i in range(size)])


def shift(value, step):
    size = lax.axis_size("tensor")
    return lax.ppermute(value, "tensor", [(i, (i + step) % size) for i in range(size)])


def add(left, right):
    return (left.astype(F32) + right.astype(F32)).astype(BF16)


def after(value, *others):
    return lax.optimization_barrier((value, *others))[0]


def bits_from(first):
    bit = first
    while bit < lax.axis_size(ROWS_AXES):
        yield bit
        bit *= 2


def sum_rows(value):
    value = sum(to_chips(value))
    for bit in (1, *bits_from(8)):
        value = value + swap(value, bit)
    return value


def sum_ring(value):
    return value + shift(value, 1) + shift(value, 2) + shift(value, 3)


def dot(left, right, dims=NN):
    return lax.dot_general(left, right, dims, preferred_element_type=F32)


def inverse_rms(values):
    return lax.rsqrt(jnp.mean(values * values, axis=-1, keepdims=True) + EPSILON)


CHIPS = (0, 1, 2, 3)


def to_chips(value):
    return [value] + [swap(value, 2 * mask) for mask in CHIPS[1:]]


def local(
    tokens,
    segment_ids,
    norm1_gain,
    w_query,
    w_key,
    w_value,
    w_out,
    rel_bias,
    norm2_gain,
    gate_weight_matrix,
    upward_weight,
    downward_weight,
    cotangent,
):
    shard, rows_here, width = tokens.shape
    length = segment_ids.shape[1]
    heads = rel_bias.shape[1]
    feats = w_query.shape[1]
    units = downward_weight.shape[0]
    ring = lax.axis_size("tensor")
    n_dp = lax.axis_size(ROWS_AXES)
    z = lax.axis_index("tensor")
    dp = lax.axis_index(ROWS_AXES)
    core = dp & 1
    chip = (dp >> 1) & 3
    where = jnp.stack([core, chip, dp, z]).astype(jnp.int32)

    x_low = tokens.reshape(shard, width)
    cot = cotangent.reshape(shard, width)
    tiles = bias_tiles(rel_bias)
    w_qkv = jnp.concatenate([w_query, w_key, w_value], axis=1)

    out_rows = feats // 8
    out_piece = lax.dynamic_slice_in_dim(w_out, (2 * chip + core) * out_rows, out_rows, 0)
    cs = to_chips(cot)
    sent = jnp.concatenate([x_low, out_piece], axis=0)
    blocks, normed_blocks, qkv_blocks = [], [], []
    for s in range(ring):
        if s == ring - 1:
            sent = after(sent, tiles, qkv_blocks[1], *cs)
        if s:
            sent = shift(sent, 1)
        values = sent[:shard].astype(F32)
        normed = (values * inverse_rms(values) * norm1_gain).astype(BF16)
        blocks.append(sent)
        normed_blocks.append(normed)
        qkv_blocks.append(dot(normed, w_qkv).astype(BF16))
    out_ring = jnp.stack([block[shard:] for block in blocks])
    out_chips = to_chips(out_ring)

    def unit_rows(array):
        return lax.dynamic_slice(array, (chip * (units // 4), core * (width // 2)), (units // 4, width // 2))

    pack = jnp.concatenate(
        [
            unit_rows(jnp.transpose(gate_weight_matrix)),
            unit_rows(jnp.transpose(upward_weight)),
            unit_rows(downward_weight),
        ],
        axis=0,
    )
    weights = lax.all_gather(after(pack, blocks[3]), ("tensor", "core"), axis=0)
    weights = weights.reshape(ring, 2, *pack.shape)

    qkv = jnp.zeros((length, 3 * feats), BF16)
    for s, block in enumerate(qkv_blocks):
        qkv = lax.dynamic_update_slice_in_dim(qkv, block, ((z - s) % ring) * shard, 0)

    o_row, lse = attn_fwd(segment_ids, rel_bias, qkv, tiles)
    out_mine = after(jnp.stack(out_chips), o_row)
    out_all = place_out(where, out_mine, swap(out_mine, 1))
    o_home = lax.all_to_all(o_row, "tensor", 0, 1, tiled=True)
    attn = dot(o_home, out_all)
    x_one = x_low.astype(F32) + attn
    r_two = inverse_rms(x_one)
    norm_two = (x_one * r_two * norm2_gain).astype(BF16)

    xs = to_chips(norm_two)
    parts, back = [], []
    for r, (x, c) in enumerate(zip(xs, cs)):
        if parts:
            x = after(x, parts[-1][0])
        if r == 3:
            back.append(swap(parts[1][0], 2))
            x = after(x, back[0])
        parts.append(ffn(x, c, weights))

    def returns(which, *others):
        terms = [after(part[which], *others) if others else part[which] for part in parts]
        return [terms[0]] + [swap(terms[mask], 2 * mask) for mask in CHIPS[1:]]

    def total_of(terms):
        return sum(term.astype(F32) for term in terms)

    back = [parts[0][0], back[0]] + [swap(parts[r][0], 2 * r) for r in (2, 3)]
    d_two = total_of(back)
    u_two = d_two * norm2_gain
    d_x_one = cot.astype(F32) + r_two * u_two - x_one * (
        r_two * r_two * r_two * jnp.mean(u_two * x_one, axis=-1, keepdims=True)
    )
    d_attn = d_x_one.astype(BF16)
    d_o = dot(d_attn, out_all, NT).astype(BF16)
    do_row = lax.all_to_all(d_o, "tensor", 1, 0, tiled=True)

    unit_grads = ffn_grads(
        [after(parts[0][2], d_o)] + [part[2] for part in parts[1:]],
        cs,
        [part[3] for part in parts],
        xs,
        [part[4] for part in parts],
        ring,
    )
    ffn_piece = lax.psum_scatter(
        after(unit_grads, do_row).reshape(-1, width // 2), ("tensor", "core"), scatter_dimension=0, tiled=True
    )

    def from_chips(pieces):
        return [pieces[0]] + [swap(pieces[r], 2 * r) for r in CHIPS[1:]]

    ffo_back = returns(1, do_row)
    ffo = total_of(ffo_back)
    y = x_one + ffo
    out_tokens = y.astype(BF16)
    grad_two = jnp.sum(d_two * x_one * r_two, axis=0)
    stats = jnp.stack([jnp.sum(attn * attn), jnp.sum(ffo * ffo), jnp.sum(y * y)])

    do_row = after(do_row, unit_grads)

    dqkv, near, far = attn_bwd(segment_ids, rel_bias, qkv, o_row, do_row, lse, tiles)
    dqkv = after(dqkv, *ffo_back)
    keep, give, grad_one = late_grads(where, normed_blocks, dqkv, w_qkv, o_home, d_attn)
    d_one_part = normed_grad(after(dqkv, give), w_qkv)
    d_one = lax.psum_scatter(after(d_one_part, ffn_piece), "tensor", scatter_dimension=0, tiled=True)
    summed = add(keep, swap(give, 1))
    near = after(near, summed)
    row = width // 8
    stats = jnp.pad(stats, (0, row - 3)).reshape(1, row)
    small = jnp.concatenate([grad_two.reshape(8, row), grad_one, stats, bias_grad(near, far)], axis=0)
    got = total_of(from_chips(summed)).astype(BF16)
    small = sum_rows(small)
    mid = got.shape[0] - feats
    by_ring = got[mid:].reshape(ring, feats // 4, width // 2)
    out_parts = [lax.dynamic_index_in_dim(by_ring, (z + s) % ring, 0, keepdims=False) for s in range(ring)]
    small_rows = jnp.pad(small[:17], ((0, 7), (0, 0))).reshape(6, width // 2)
    ring_sum = total_of(
        [
            shift(jnp.concatenate([part.astype(F32), small_rows], axis=0), s) if s else
            jnp.concatenate([part.astype(F32), small_rows], axis=0)
            for s, part in enumerate(out_parts)
        ]
    )
    out_piece = ring_sum[: feats // 4].astype(BF16)
    late = jnp.concatenate([got[:mid], out_piece], axis=0)
    for bit in bits_from(8):
        late = add(late, swap(late, bit))
    piece = after(ffn_piece, got, small)
    for bit in bits_from(8):
        piece = add(piece, swap(piece, bit))
    ffn_parts = to_chips(piece)
    grad_bias = small[17:, :heads]
    small = ring_sum[feats // 4 :].reshape(24, row)
    grad_norm2, grad_norm1 = small[:8].reshape(width), small[8:16].reshape(width) / norm1_gain
    stat_sums = small[16, :3]
    own = jnp.stack([after(part, late, small) for part in ffn_parts])
    late = to_chips(after(late, small))
    grad_gate, grad_up, grad_down = place(where, own, swap(own, 1), (units // 4,) * 3)
    grad_gate, grad_up = jnp.transpose(grad_gate), jnp.transpose(grad_up)
    count = shard * rows_here * width * n_dp * ring
    rms_stats = jnp.sqrt(stat_sums / count)

    late = jnp.stack([after(part, grad_down) for part in late])
    d_one = after(d_one, own).astype(F32)
    x_in = x_low.astype(F32)
    r_one = inverse_rms(x_in)
    u_one = d_one * norm1_gain
    grad_tokens = (
        d_x_one + r_one * u_one - x_in * (r_one * r_one * r_one * jnp.mean(u_one * x_in, axis=-1, keepdims=True))
    ).astype(BF16)

    late_other = swap(late, 1)
    late = after(late, grad_tokens)
    grad_query, grad_key, grad_value, grad_out = place_late(where, late, late_other, width // 8)

    shape = (shard, rows_here, width)
    return (
        out_tokens.reshape(shape),
        grad_tokens.reshape(shape),
        grad_norm1,
        grad_query,
        grad_key,
        grad_value,
        grad_out,
        grad_bias,
        grad_norm2,
        grad_gate,
        grad_up,
        grad_down,
        rms_stats,
    )


def solution(mesh):
    n_dp, ring = mesh.devices.shape
    by_core = Mesh(mesh.devices.reshape(n_dp // 2, 2, ring), (*ROWS_AXES, "tensor"))
    in_specs = (
        P("tensor", ROWS_AXES, None),
        P(ROWS_AXES, None),
        P(),
        P(None, "tensor"),
        P(None, "tensor"),
        P(None, "tensor"),
        P("tensor", None),
        P(None, "tensor"),
        P(),
        P(None, "tensor"),
        P(None, "tensor"),
        P("tensor", None),
        P("tensor", ROWS_AXES, None),
    )
    out_specs = (
        P("tensor", ROWS_AXES, None),
        P("tensor", ROWS_AXES, None),
        P(),
        P(None, "tensor"),
        P(None, "tensor"),
        P(None, "tensor"),
        P("tensor", None),
        P(None, "tensor"),
        P(),
        P(None, "tensor"),
        P(None, "tensor"),
        P("tensor", None),
        P(),
    )
    return jax.shard_map(local, mesh=by_core, in_specs=in_specs, out_specs=out_specs, check_vma=False)
```

```python
import functools
import jax
import jax.numpy as jnp
from jax import lax
from jax.experimental import pallas as pl
from jax.experimental.pallas import tpu as pltpu
from jax.sharding import Mesh, PartitionSpec as P

EPSILON = 1e-06
THRESHOLDS = (12, 16, 23, 32, 46, 64, 91)
TILE = 128
SEG = 384
NT = (((1,), (1,)), ((), ()))
NN = (((1,), (0,)), ((), ()))
NN = (((1,), (0,)), ((), ()))
TN = (((0,), (0,)), ((), ()))
F32 = jnp.float32
BF16 = jnp.bfloat16
SMALL = pl.CostEstimate(flops=1000, bytes_accessed=1000, transcendentals=0)


def bucket_of(offset):
    distance = jnp.abs(offset)
    far_bucket = 8 + sum(((distance >= threshold).astype(jnp.int32) for threshold in THRESHOLDS))
    return jnp.where(distance < 8, distance, far_bucket) + 16 * (offset > 0).astype(jnp.int32)


def tile_bucket(delta, key_axis):
    keys = lax.broadcasted_iota(jnp.int32, (TILE, TILE), key_axis)
    queries = lax.broadcasted_iota(jnp.int32, (TILE, TILE), 1 - key_axis)
    return bucket_of(TILE * delta + keys - queries)


def bias_tiles_kernel(bias_ref, out_ref):
    buckets, heads = bias_ref.shape
    for delta in (-1, 0, 1):
        bucket = tile_bucket(delta, 0)
        tiles = [jnp.zeros((TILE, TILE), F32) for _ in range(heads)]
        for b in range(buckets):
            hit = bucket == b
            tiles = [jnp.where(hit, bias_ref[b, h], t) for h, t in enumerate(tiles)]
        for h in range(heads):
            out_ref[h, delta + 1] = tiles[h]


def bias_tiles(rel_bias):
    return pl.pallas_call(
        bias_tiles_kernel,
        out_shape=jax.ShapeDtypeStruct((rel_bias.shape[1], 3, TILE, TILE), F32),
        in_specs=[pl.BlockSpec(memory_space=pltpu.SMEM)],
        out_specs=pl.BlockSpec(memory_space=pltpu.VMEM),
        name="bias_tiles",
    )(rel_bias)


def bias_grad_kernel(near_ref, far_ref, out_ref):
    heads = near_ref.shape[0]
    row = lax.broadcasted_iota(jnp.int32, (32, TILE), 0)
    lane = lax.broadcasted_iota(jnp.int32, (32, TILE), 1)
    bucket = [tile_bucket(delta, 0) for delta in (-1, 0, 1)]
    total = jnp.zeros((32, TILE), F32)
    for h in range(heads):
        near = [near_ref[h, d] for d in range(3)]
        for b in range(32):
            deltas = (0, 1) if b < 16 else (1, 2)
            part = sum(jnp.where(bucket[d] == b, near[d], 0.0) for d in deltas)
            part = jnp.sum(part.reshape(16, 8, TILE), axis=0)
            if b == 15:
                part = part + far_ref[h, 0]
            if b == 31:
                part = part + far_ref[h, 1]
            line = jnp.sum(part, axis=0, keepdims=True)
            total = jnp.where((row == b) & (lane == h), jnp.sum(line, axis=1, keepdims=True), total)
    out_ref[...] = total


def bias_grad(near, far):
    return pl.pallas_call(
        bias_grad_kernel,
        out_shape=jax.ShapeDtypeStruct((32, TILE), F32),
        name="bias_grad",
    )(near, far)


def attn_fwd_kernel(seg_ref, bias_ref, qkv_ref, tile_ref, o_ref, lse_ref, s_ref, p_ref, l_ref, vt_ref, ot_ref):
    length, width = o_ref.shape
    q_ref, k_ref, v_ref = (qkv_ref.at[:, n * width : (n + 1) * width] for n in range(3))
    heads = width // 64
    lane = lax.broadcasted_iota(jnp.int32, (1, width), 1)
    one_example = seg_ref[0, length - 1] == seg_ref[0, 0]
    vt_ref[...] = jnp.transpose(v_ref[...])

    def blocks(h, mask, spans):
        below = bias_ref[15, h]
        above = bias_ref[31, h]
        head = pl.ds(pl.multiple_of(h * 64, 64), 64)
        for lo, hi in spans:
            qh = jnp.where(mask, q_ref[lo:hi], jnp.zeros((), BF16))
            s_ref[lo:hi, lo:hi] = lax.dot_general(k_ref[lo:hi], qh, NT, preferred_element_type=F32)
            tiles = range(lo // TILE, hi // TILE)
            for i in tiles:
                cols = slice(i * TILE, (i + 1) * TILE)
                near_top, sides = None, {-1: None, 1: None}
                for j in tiles:
                    part = s_ref[j * TILE : (j + 1) * TILE, cols]
                    if abs(j - i) <= 1:
                        part = part + tile_ref[h, j - i + 1]
                        s_ref[j * TILE : (j + 1) * TILE, cols] = part
                    part = jnp.max(part.reshape(TILE // 8, 8, TILE), axis=0)
                    if abs(j - i) <= 1:
                        near_top = part if near_top is None else jnp.maximum(near_top, part)
                    else:
                        side = 1 if j > i else -1
                        sides[side] = part if sides[side] is None else jnp.maximum(sides[side], part)
                top = near_top
                for side, constant in ((-1, below), (1, above)):
                    if sides[side] is not None:
                        top = jnp.maximum(top, sides[side] + constant)
                top = jnp.max(top, axis=0, keepdims=True)
                total = jnp.zeros((8, TILE), F32)
                for j in tiles:
                    shift = top
                    if abs(j - i) > 1:
                        shift = top - (below if j < i else above)
                    e = jnp.exp(s_ref[j * TILE : (j + 1) * TILE, cols] - shift)
                    total = total + jnp.sum(e.reshape(TILE // 8, 8, TILE), axis=0)
                    p_ref[j * TILE : (j + 1) * TILE, cols] = e.astype(BF16)
                total = jnp.sum(total, axis=0, keepdims=True)
                l_ref[0:1, cols] = 1.0 / total
                lse_ref[h, 0:1, cols] = top + jnp.log(total)
            ot_ref[head, lo:hi] = (
                lax.dot_general(vt_ref[head, lo:hi], p_ref[lo:hi, lo:hi], NN, preferred_element_type=F32)
                * l_ref[0:1, lo:hi]
            )

    @pl.loop(0, heads)
    def _(h):
        mask = (lane // 64) == h

        @pl.when(one_example)
        def _():
            blocks(h, mask, ((0, length),))

        @pl.when(jnp.logical_not(one_example))
        def _():
            blocks(h, mask, tuple((lo, lo + SEG) for lo in range(0, length, SEG)))

    o_ref[...] = jnp.transpose(ot_ref[...]).astype(BF16)


def attn_fwd(seg, bias, qkv, tiles):
    length, width = qkv.shape[0], qkv.shape[1] // 3
    heads = width // 64
    vmem = pl.BlockSpec(memory_space=pltpu.VMEM)
    smem = pl.BlockSpec(memory_space=pltpu.SMEM)
    return pl.pallas_call(
        attn_fwd_kernel,
        out_shape=(
            jax.ShapeDtypeStruct((length, width), BF16),
            jax.ShapeDtypeStruct((heads, 8, length), F32),
        ),
        in_specs=[smem, smem, vmem, vmem],
        out_specs=(vmem, vmem),
        scratch_shapes=[
            pltpu.VMEM((length, length), F32),
            pltpu.VMEM((length, length), BF16),
            pltpu.VMEM((8, length), F32),
            pltpu.VMEM((width, length), BF16),
            pltpu.VMEM((width, length), F32),
        ],
        compiler_params=pltpu.CompilerParams(vmem_limit_bytes=40 << 20),
        cost_estimate=SMALL,
        name="attn_fwd",
    )(seg, bias, qkv, tiles)


def attn_bwd_kernel(
    seg_ref, bias_ref, qkv_ref, o_ref, do_ref, lse_ref, tile_ref,
    dqkv_ref, near_ref, far_ref,
    s_ref, dp_ref, p_ref, ds_ref, dsum_ref, kt_ref, dqt_ref, dka_ref, dva_ref,
):
    length, width = o_ref.shape
    q_ref, k_ref, v_ref = (qkv_ref.at[:, n * width : (n + 1) * width] for n in range(3))
    heads = width // 64
    lane = lax.broadcasted_iota(jnp.int32, (1, width), 1)
    one_example = seg_ref[0, length - 1] == seg_ref[0, 0]
    kt_ref[...] = jnp.transpose(k_ref[...])
    prod = o_ref[...].astype(F32) * do_ref[...].astype(F32)
    high = prod.astype(BF16)
    low = (prod - high.astype(F32)).astype(BF16)
    head_rows = (
        lax.broadcasted_iota(jnp.int32, (8 * heads, width), 1) // 64
        == lax.broadcasted_iota(jnp.int32, (8 * heads, width), 0) // 8
    ).astype(BF16)
    dsum_ref[...] = lax.dot_general(head_rows, high, NT, preferred_element_type=F32) + lax.dot_general(
        head_rows, low, NT, preferred_element_type=F32
    )
    def blocks(h, mask, spans):
        below = bias_ref[15, h]
        above = bias_ref[31, h]
        near_sum = [None, None, None]
        far_sum = [jnp.zeros((8, TILE), F32)] * 2
        zero = jnp.zeros((), BF16)
        for d in range(3):
            near_ref[h, d] = jnp.zeros((TILE, TILE), F32)
        for lo, hi in spans:
            qh = jnp.where(mask, q_ref[lo:hi], zero)
            dh = jnp.where(mask, do_ref[lo:hi], zero)
            s_ref[lo:hi, lo:hi] = lax.dot_general(k_ref[lo:hi], qh, NT, preferred_element_type=F32)
            dp_ref[lo:hi, lo:hi] = lax.dot_general(v_ref[lo:hi], dh, NT, preferred_element_type=F32)
            for i in range(lo // TILE, hi // TILE):
                cols = slice(i * TILE, (i + 1) * TILE)
                lse = lse_ref[h, 0:1, cols]
                dsum = dsum_ref[pl.ds(pl.multiple_of(h * 8, 8), 1), cols]
                for j in range(lo // TILE, hi // TILE):
                    rows = slice(j * TILE, (j + 1) * TILE)
                    s = s_ref[rows, cols]
                    if abs(j - i) <= 1:
                        e = jnp.exp(s + tile_ref[h, j - i + 1] - lse)
                    else:
                        e = jnp.exp(s - (lse - (below if j < i else above)))
                    ds = e * (dp_ref[rows, cols] - dsum)
                    p_ref[rows, cols] = e.astype(BF16)
                    ds_ref[rows, cols] = ds.astype(BF16)
                    if abs(j - i) <= 1:
                        near_ref[h, j - i + 1] += ds
                    else:
                        side = int(j > i)
                        far_sum[side] = far_sum[side] + jnp.sum(ds.reshape(TILE // 8, 8, TILE), axis=0)
            dv = lax.dot_general(p_ref[lo:hi, lo:hi], dh, NN, preferred_element_type=F32)
            dk = lax.dot_general(ds_ref[lo:hi, lo:hi], qh, NN, preferred_element_type=F32)
            dva_ref[lo:hi] = jnp.where(mask, dv, dva_ref[lo:hi])
            dka_ref[lo:hi] = jnp.where(mask, dk, dka_ref[lo:hi])
            head = pl.ds(pl.multiple_of(h * 64, 64), 64)
            dqt_ref[head, lo:hi] = lax.dot_general(
                kt_ref[head, lo:hi], ds_ref[lo:hi, lo:hi], NN, preferred_element_type=F32
            )
        far_ref[h, 0] = far_sum[0]
        far_ref[h, 1] = far_sum[1]

    @pl.loop(0, heads)
    def _(h):
        mask = (lane // 64) == h

        @pl.when(one_example)
        def _():
            blocks(h, mask, ((0, length),))

        @pl.when(jnp.logical_not(one_example))
        def _():
            blocks(h, mask, tuple((lo, lo + SEG) for lo in range(0, length, SEG)))

    dqkv_ref[:, :width] = jnp.transpose(dqt_ref[...]).astype(BF16)
    dqkv_ref[:, width : 2 * width] = dka_ref[...].astype(BF16)
    dqkv_ref[:, 2 * width :] = dva_ref[...].astype(BF16)


def attn_bwd(seg, bias, qkv, o, do, lse, tiles):
    length, width = o.shape
    heads = width // 64
    vmem = pl.BlockSpec(memory_space=pltpu.VMEM)
    smem = pl.BlockSpec(memory_space=pltpu.SMEM)
    return pl.pallas_call(
        attn_bwd_kernel,
        out_shape=(
            jax.ShapeDtypeStruct((length, 3 * width), BF16),
            jax.ShapeDtypeStruct((heads, 3, TILE, TILE), F32),
            jax.ShapeDtypeStruct((heads, 2, 8, TILE), F32),
        ),
        in_specs=[smem, smem] + [vmem] * 5,
        out_specs=(vmem,) * 3,
        scratch_shapes=[
            pltpu.VMEM((length, length), F32),
            pltpu.VMEM((length, length), F32),
            pltpu.VMEM((length, length), BF16),
            pltpu.VMEM((length, length), BF16),
            pltpu.VMEM((8 * heads, length), F32),
            pltpu.VMEM((width, length), BF16),
            pltpu.VMEM((width, length), F32),
            pltpu.VMEM((length, width), F32),
            pltpu.VMEM((length, width), F32),
        ],
        compiler_params=pltpu.CompilerParams(vmem_limit_bytes=48 << 20),
        cost_estimate=SMALL,
        name="attn_bwd",
    )(seg, bias, qkv, o, do, lse, tiles)


def tanh_gelu(u):
    scale = 0.7978845608028654
    t = jnp.tanh(scale * (u + 0.044715 * (u * u * u)))
    half = 0.5 * (1.0 + t)
    slope = half + (0.5 * u) * (1.0 - t * t) * (scale * (1.0 + 0.134145 * (u * u)))
    return u * half, slope


def ffn_kernel(
    x_ref, c_ref, weights_ref,
    dtwo_ref, ffo_ref, hidden_ref, dgate_ref, dup_ref,
    gate_w, up_w, down_w, sems,
):
    ring, halves, rows, half = weights_ref.shape
    units = rows // 3
    scratches = (gate_w, up_w, down_w)
    copies = [[], [], []]
    for m in range(3):
        for q in range(ring):
            for n in range(halves):
                copies[m].append(
                    pltpu.make_async_copy(
                        weights_ref.at[q, n, m * units : (m + 1) * units],
                        scratches[m].at[q * units : (q + 1) * units, n * half : (n + 1) * half],
                        sems.at[m, halves * q + n],
                    )
                )
    for group in copies:
        for copy in group:
            copy.start()
    for copy in copies[0]:
        copy.wait()
    gate = lax.dot_general(x_ref[...], gate_w[...], NT, preferred_element_type=F32)
    for copy in copies[1]:
        copy.wait()
    up = lax.dot_general(x_ref[...], up_w[...], NT, preferred_element_type=F32)
    for copy in copies[2]:
        copy.wait()
    d_hidden = lax.dot_general(c_ref[...], down_w[...], NT, preferred_element_type=F32)
    value, slope = tanh_gelu(gate)
    hidden = (value * up).astype(BF16)
    d_gate = (d_hidden * up * slope).astype(BF16)
    d_up = (d_hidden * value).astype(BF16)
    hidden_ref[...] = hidden
    dgate_ref[...] = d_gate
    dup_ref[...] = d_up
    dtwo_ref[...] = (
        lax.dot_general(d_gate, gate_w[...], NN, preferred_element_type=F32)
        + lax.dot_general(d_up, up_w[...], NN, preferred_element_type=F32)
    ).astype(dtwo_ref.dtype)
    ffo_ref[...] = lax.dot_general(hidden, down_w[...], NN, preferred_element_type=F32).astype(ffo_ref.dtype)


def ffn(x, c, weights):
    tokens, width = x.shape
    ring, halves, rows, _ = weights.shape
    units = ring * rows // 3
    vmem = pl.BlockSpec(memory_space=pltpu.VMEM)
    anywhere = pl.BlockSpec(memory_space=pl.ANY)
    wide = jax.ShapeDtypeStruct((tokens, width), BF16)
    inner = jax.ShapeDtypeStruct((tokens, units), BF16)
    return pl.pallas_call(
        ffn_kernel,
        out_shape=(wide, wide, inner, inner, inner),
        in_specs=[vmem, vmem, anywhere],
        out_specs=(vmem,) * 5,
        scratch_shapes=[pltpu.VMEM((units, width), BF16)] * 3 + [pltpu.SemaphoreType.DMA((3, halves * ring))],
        compiler_params=pltpu.CompilerParams(vmem_limit_bytes=40 << 20),
        cost_estimate=SMALL,
        name="ffn",
    )(x, c, weights)


def ffn_grads_kernel(n, *refs):
    sources = [refs[i * n : (i + 1) * n] for i in range(5)]
    out_ref = refs[5 * n]
    held = refs[5 * n + 1 : 5 * n + 6]
    sems = refs[5 * n + 6]
    ring, halves, rows, half = out_ref.shape
    units = rows // 3
    tokens = sources[0][0].shape[0]
    copies = [
        [
            pltpu.make_async_copy(ref, target.at[j * tokens : (j + 1) * tokens], sems.at[i, j])
            for j, ref in enumerate(group)
        ]
        for i, (group, target) in enumerate(zip(sources, held))
    ]
    for group in copies:
        for copy in group:
            copy.start()
    waited = set()
    for m, (lhs, rhs) in ((2, (0, 1)), (0, (2, 3)), (1, (4, 3))):
        for i in (lhs, rhs):
            if i not in waited:
                waited.add(i)
                for copy in copies[i]:
                    copy.wait()
        grad = lax.dot_general(held[lhs][...], held[rhs][...], TN, preferred_element_type=F32).astype(BF16)
        for q in range(ring):
            for k in range(halves):
                out_ref[q, k, m * units : (m + 1) * units] = grad[
                    q * units : (q + 1) * units, k * half : (k + 1) * half
                ]


def ffn_grads(hs, cs, gs, xs, us, ring):
    rows, width = xs[0].shape
    units = hs[0].shape[1]
    n = len(xs)
    vmem = pl.BlockSpec(memory_space=pltpu.VMEM)
    anywhere = pl.BlockSpec(memory_space=pl.ANY)
    shape = jax.ShapeDtypeStruct((ring, 2, 3 * units // ring, width // 2), BF16)
    wide, inner = pltpu.VMEM((n * rows, width), BF16), pltpu.VMEM((n * rows, units), BF16)
    return pl.pallas_call(
        functools.partial(ffn_grads_kernel, n),
        out_shape=shape,
        in_specs=[anywhere] * (5 * n),
        out_specs=vmem,
        scratch_shapes=[inner, wide, inner, wide, inner, pltpu.SemaphoreType.DMA((5, n))],
        compiler_params=pltpu.CompilerParams(vmem_limit_bytes=58 << 20),
        cost_estimate=SMALL,
        name="ffn_grads",
    )(*hs, *cs, *gs, *xs, *us)


def normed_grad_kernel(d_ref, w_ref, out_ref):
    out_ref[...] = lax.dot_general(d_ref[...], w_ref[...], NT, preferred_element_type=F32).astype(BF16)


def normed_grad(d, w):
    vmem = pl.BlockSpec(memory_space=pltpu.VMEM)
    return pl.pallas_call(
        normed_grad_kernel,
        out_shape=jax.ShapeDtypeStruct((d.shape[0], w.shape[0]), BF16),
        in_specs=[vmem, vmem],
        out_specs=vmem,
        compiler_params=pltpu.CompilerParams(vmem_limit_bytes=24 << 20),
        cost_estimate=SMALL,
        name="normed_grad",
    )(d, w)


def late_grads_kernel(where_ref, *refs):
    blocks = refs[:-10]
    d_ref, w_ref, o_ref, da_ref, keep_ref, give_ref, gain_ref, x_ref, held, sems = refs[-10:]
    core, chip = where_ref[0], where_ref[1]
    chips, _, half = keep_ref.shape
    ring = len(blocks)
    copies = []
    for s, block in enumerate(blocks):
        first = lax.rem(where_ref[3] + ring - s, ring) * block.shape[0]
        target = x_ref.at[pl.ds(pl.multiple_of(first, 32), block.shape[0])]
        copies.append(pltpu.make_async_copy(block, target, sems.at[s]))
    for copy in copies:
        copy.start()
    width = x_ref.shape[1]
    rows = width // (2 * chips)
    out_rows = o_ref.shape[1] // (ring * chips)
    mid = rows + rows // 2
    for n, out_ref in enumerate((give_ref, keep_ref)):
        start = pl.multiple_of((core ^ (1 - n)) * half, 128)
        held[...] = lax.dot_general(
            o_ref[...], da_ref[:, pl.ds(start, half)], TN, preferred_element_type=F32
        ).astype(BF16)
        for r in range(chips):
            for q in range(ring):
                first = (q * chips + (chip ^ r)) * out_rows
                out_ref[r, mid + q * out_rows : mid + (q + 1) * out_rows] = held[
                    pl.ds(pl.multiple_of(first, out_rows), out_rows)
                ]
    for copy in copies:
        copy.wait()
    for n, out_ref in enumerate((give_ref, keep_ref)):
        for r in range(chips):
            block = (core ^ (1 - n)) * chips + (chip ^ r)
            start = pl.multiple_of(block * rows, 128)
            grad = lax.dot_general(x_ref[:, pl.ds(start, rows)], d_ref[...], TN, preferred_element_type=F32)
            low = grad.astype(BF16)
            out_ref[r, :rows] = low[:, :half]
            out_ref[r, rows:mid, : half // 2] = low[: rows // 2, half:]
            out_ref[r, rows:mid, half // 2 :] = low[rows // 2 :, half:]
            line = jnp.sum(grad * w_ref[pl.ds(start, rows)].astype(F32), axis=1, keepdims=True)
            gain_ref[pl.ds(block, 1)] = jnp.transpose(jnp.broadcast_to(line, (rows, rows)))[:1]


def late_grads(where, blocks, d, w, o, d_attn):
    width = w.shape[0]
    rows = width // 8
    vmem = pl.BlockSpec(memory_space=pltpu.VMEM)
    shape = jax.ShapeDtypeStruct((4, rows + rows // 2 + o.shape[1] // 4, width // 2), BF16)
    return pl.pallas_call(
        late_grads_kernel,
        out_shape=(shape, shape, jax.ShapeDtypeStruct((8, rows), F32)),
        in_specs=[pl.BlockSpec(memory_space=pltpu.SMEM)] + [pl.BlockSpec(memory_space=pl.ANY)] * len(blocks) + [vmem] * 4,
        out_specs=(vmem,) * 3,
        scratch_shapes=[
            pltpu.VMEM((d.shape[0], width), BF16),
            pltpu.VMEM((o.shape[1], width // 2), BF16),
            pltpu.SemaphoreType.DMA((len(blocks),)),
        ],
        compiler_params=pltpu.CompilerParams(vmem_limit_bytes=56 << 20),
        cost_estimate=SMALL,
        name="late_grads",
    )(where, *blocks, d, w, o, d_attn)


def place_kernel(where_ref, own_ref, other_ref, *out_refs):
    core, chip = where_ref[0], where_ref[1]
    chips, _, half = own_ref.shape
    first = 0
    for target in out_refs:
        units = target.shape[0] // chips
        for r in range(chips):
            rows = pl.ds(pl.multiple_of((chip ^ r) * units, 8), units)
            for n, ref in enumerate((own_ref, other_ref)):
                columns = pl.ds(pl.multiple_of((core ^ n) * half, 128), half)
                target[rows, columns] = ref[r, first : first + units].astype(F32)
        first += units


def place(where, own, other, sizes):
    chips, _, half = own.shape
    vmem = pl.BlockSpec(memory_space=pltpu.VMEM)
    return pl.pallas_call(
        place_kernel,
        out_shape=tuple(jax.ShapeDtypeStruct((chips * size, 2 * half), F32) for size in sizes),
        in_specs=[pl.BlockSpec(memory_space=pltpu.SMEM), vmem, vmem],
        out_specs=(vmem,) * len(sizes),
        compiler_params=pltpu.CompilerParams(vmem_limit_bytes=40 << 20),
        cost_estimate=SMALL,
        name="place",
    )(where, own, other)


def place_late_kernel(where_ref, own_ref, other_ref, *out_refs):
    core, chip = where_ref[0], where_ref[1]
    chips, total, half = own_ref.shape
    projections, out_ref = out_refs[:3], out_refs[3]
    rows, part = projections[0].shape[0] // (2 * chips), projections[0].shape[1]
    mid = rows + rows // 2
    for n, ref in enumerate((own_ref, other_ref)):
        for r in range(chips):
            start = ((core ^ n) * chips + (chip ^ r)) * rows
            target = pl.ds(pl.multiple_of(start, 8), rows)
            for i in range(2):
                projections[i][target] = ref[r, :rows, i * part : (i + 1) * part].astype(F32)
            for i in range(2):
                target = pl.ds(pl.multiple_of(start + i * (rows // 2), 8), rows // 2)
                projections[2][target] = ref[r, rows:mid, i * part : (i + 1) * part].astype(F32)
            start = pl.multiple_of((chip ^ r) * (total - mid), 8)
            columns = pl.ds(pl.multiple_of((core ^ n) * half, 128), half)
            out_ref[pl.ds(start, total - mid), columns] = ref[r, mid:].astype(F32)


def place_late(where, own, other, rows):
    chips, total, half = own.shape
    vmem = pl.BlockSpec(memory_space=pltpu.VMEM)
    projection = jax.ShapeDtypeStruct((2 * chips * rows, half // 2), F32)
    out_rows = chips * (total - rows - rows // 2)
    return pl.pallas_call(
        place_late_kernel,
        out_shape=(projection,) * 3 + (jax.ShapeDtypeStruct((out_rows, 2 * half), F32),),
        in_specs=[pl.BlockSpec(memory_space=pltpu.SMEM), vmem, vmem],
        out_specs=(vmem,) * 4,
        cost_estimate=SMALL,
        name="place_late",
    )(where, own, other)


def place_out_kernel(where_ref, mine_ref, other_ref, out_ref):
    chips, ring, rows, _ = mine_ref.shape
    core, chip, z = where_ref[0], where_ref[1], where_ref[3]
    for s in range(ring):
        quarter = lax.rem(z + ring - s, ring)
        for r in range(chips):
            for n, ref in enumerate((mine_ref, other_ref)):
                start = ((quarter * chips + (chip ^ r)) * 2 + (core ^ n)) * rows
                out_ref[pl.ds(pl.multiple_of(start, rows), rows)] = ref[r, s]


def place_out(where, mine, other):
    chips, ring, rows, width = mine.shape
    vmem = pl.BlockSpec(memory_space=pltpu.VMEM)
    return pl.pallas_call(
        place_out_kernel,
        out_shape=jax.ShapeDtypeStruct((2 * chips * ring * rows, width), mine.dtype),
        in_specs=[pl.BlockSpec(memory_space=pltpu.SMEM), vmem, vmem],
        out_specs=vmem,
        cost_estimate=SMALL,
        name="place_out",
    )(where, mine, other)


ROWS_AXES = ("chips", "core")


def swap(value, mask):
    size = lax.axis_size(ROWS_AXES)
    return lax.ppermute(value, ROWS_AXES, [(i, i ^ mask) for i in range(size)])


def shift(value, step):
    size = lax.axis_size("tensor")
    return lax.ppermute(value, "tensor", [(i, (i + step) % size) for i in range(size)])


def add(left, right):
    return (left.astype(F32) + right.astype(F32)).astype(BF16)


def after(value, *others):
    return lax.optimization_barrier((value, *others))[0]


def bits_from(first):
    bit = first
    while bit < lax.axis_size(ROWS_AXES):
        yield bit
        bit *= 2


def sum_rows(value):
    value = sum(to_chips(value))
    for bit in (1, *bits_from(8)):
        value = value + swap(value, bit)
    return value


def sum_ring(value):
    return value + shift(value, 1) + shift(value, 2) + shift(value, 3)


def dot(left, right, dims=NN):
    return lax.dot_general(left, right, dims, preferred_element_type=F32)


def inverse_rms(values):
    return lax.rsqrt(jnp.mean(values * values, axis=-1, keepdims=True) + EPSILON)


CHIPS = (0, 1, 2, 3)


def to_chips(value):
    return [value] + [swap(value, 2 * mask) for mask in CHIPS[1:]]


def local(
    tokens,
    segment_ids,
    norm1_gain,
    w_query,
    w_key,
    w_value,
    w_out,
    rel_bias,
    norm2_gain,
    gate_weight_matrix,
    upward_weight,
    downward_weight,
    cotangent,
):
    shard, rows_here, width = tokens.shape
    length = segment_ids.shape[1]
    heads = rel_bias.shape[1]
    feats = w_query.shape[1]
    units = downward_weight.shape[0]
    ring = lax.axis_size("tensor")
    n_dp = lax.axis_size(ROWS_AXES)
    z = lax.axis_index("tensor")
    dp = lax.axis_index(ROWS_AXES)
    core = dp & 1
    chip = (dp >> 1) & 3
    where = jnp.stack([core, chip, dp, z]).astype(jnp.int32)

    x_low = tokens.reshape(shard, width)
    cot = cotangent.reshape(shard, width)
    tiles = bias_tiles(rel_bias)
    w_qkv = jnp.concatenate([w_query, w_key, w_value], axis=1)

    out_rows = feats // 8
    out_piece = lax.dynamic_slice_in_dim(w_out, (2 * chip + core) * out_rows, out_rows, 0)
    cs = to_chips(cot)
    sent = jnp.concatenate([x_low, out_piece], axis=0)
    blocks, normed_blocks, qkv_blocks = [], [], []
    for s in range(ring):
        if s == ring - 1:
            sent = after(sent, tiles, qkv_blocks[1], *cs)
        if s:
            sent = shift(sent, 1)
        values = sent[:shard].astype(F32)
        normed = (values * inverse_rms(values) * norm1_gain).astype(BF16)
        blocks.append(sent)
        normed_blocks.append(normed)
        qkv_blocks.append(dot(normed, w_qkv).astype(BF16))
    out_ring = jnp.stack([block[shard:] for block in blocks])

    def unit_rows(array):
        return lax.dynamic_slice(array, (chip * (units // 4), core * (width // 2)), (units // 4, width // 2))

    pack = jnp.concatenate(
        [
            unit_rows(jnp.transpose(gate_weight_matrix)),
            unit_rows(jnp.transpose(upward_weight)),
            unit_rows(downward_weight),
        ],
        axis=0,
    )
    weights = lax.all_gather(after(pack, blocks[3]), ("tensor", "core"), axis=0)
    weights = weights.reshape(ring, 2, *pack.shape)

    qkv = jnp.zeros((length, 3 * feats), BF16)
    for s, block in enumerate(qkv_blocks):
        qkv = lax.dynamic_update_slice_in_dim(qkv, block, ((z - s) % ring) * shard, 0)

    o_row, lse = attn_fwd(segment_ids, rel_bias, qkv, tiles)
    out_mine = jnp.stack(to_chips(after(out_ring, o_row)))
    out_all = place_out(where, out_mine, swap(out_mine, 1))
    o_home = lax.all_to_all(o_row, "tensor", 0, 1, tiled=True)
    attn = dot(o_home, out_all)
    x_one = x_low.astype(F32) + attn
    r_two = inverse_rms(x_one)
    norm_two = (x_one * r_two * norm2_gain).astype(BF16)

    xs = to_chips(norm_two)
    parts, back = [], []
    for r, (x, c) in enumerate(zip(xs, cs)):
        if parts:
            x = after(x, parts[-1][0])
        if r == 3:
            back.append(swap(parts[1][0], 2))
            x = after(x, back[0])
        parts.append(ffn(x, c, weights))

    def returns(which, *others):
        terms = [after(part[which], *others) if others else part[which] for part in parts]
        return [terms[0]] + [swap(terms[mask], 2 * mask) for mask in CHIPS[1:]]

    def total_of(terms):
        return sum(term.astype(F32) for term in terms)

    back = [parts[0][0], back[0]] + [swap(parts[r][0], 2 * r) for r in (2, 3)]
    d_two = total_of(back)
    u_two = d_two * norm2_gain
    d_x_one = cot.astype(F32) + r_two * u_two - x_one * (
        r_two * r_two * r_two * jnp.mean(u_two * x_one, axis=-1, keepdims=True)
    )
    d_attn = d_x_one.astype(BF16)
    d_o = dot(d_attn, out_all, NT).astype(BF16)
    do_row = lax.all_to_all(d_o, "tensor", 1, 0, tiled=True)

    unit_grads = ffn_grads(
        [after(parts[0][2], d_o)] + [part[2] for part in parts[1:]],
        cs,
        [part[3] for part in parts],
        xs,
        [part[4] for part in parts],
        ring,
    )
    ffn_piece = lax.psum_scatter(
        after(unit_grads, do_row).reshape(-1, width // 2), ("tensor", "core"), scatter_dimension=0, tiled=True
    )

    def from_chips(pieces):
        return [pieces[0]] + [swap(pieces[r], 2 * r) for r in CHIPS[1:]]

    ffo_back = returns(1, do_row)
    ffo = total_of(ffo_back)
    y = x_one + ffo
    out_tokens = y.astype(BF16)
    grad_two = jnp.sum(d_two * x_one * r_two, axis=0)
    stats = jnp.stack([jnp.sum(attn * attn), jnp.sum(ffo * ffo), jnp.sum(y * y)])

    do_row = after(do_row, unit_grads)

    dqkv, near, far = attn_bwd(segment_ids, rel_bias, qkv, o_row, do_row, lse, tiles)
    dqkv = after(dqkv, *ffo_back)
    keep, give, grad_one = late_grads(where, normed_blocks, dqkv, w_qkv, o_home, d_attn)
    d_one_part = normed_grad(after(dqkv, give), w_qkv)
    d_one = lax.psum_scatter(after(d_one_part, ffn_piece), "tensor", scatter_dimension=0, tiled=True)
    summed = add(keep, swap(give, 1))
    chip_parts = from_chips(summed)
    near = after(near, chip_parts[1])
    row = width // 8
    stats = jnp.pad(stats, (0, row - 3)).reshape(1, row)
    small = jnp.concatenate([grad_two.reshape(8, row), grad_one, stats, bias_grad(near, far)], axis=0)
    got = total_of(chip_parts).astype(BF16)
    small = sum_rows(small)
    mid = got.shape[0] - feats
    by_ring = got[mid:].reshape(ring, feats // 4, width // 2)
    out_parts = [lax.dynamic_index_in_dim(by_ring, (z + s) % ring, 0, keepdims=False) for s in range(ring)]
    small_rows = jnp.pad(small[:17], ((0, 7), (0, 0))).reshape(6, width // 2)
    ring_sum = total_of(
        [
            shift(jnp.concatenate([part.astype(F32), small_rows], axis=0), s) if s else
            jnp.concatenate([part.astype(F32), small_rows], axis=0)
            for s, part in enumerate(out_parts)
        ]
    )
    out_piece = ring_sum[: feats // 4].astype(BF16)
    late = jnp.concatenate([got[:mid], out_piece], axis=0)
    for bit in bits_from(8):
        late = add(late, swap(late, bit))
    piece = after(ffn_piece, got, small)
    for bit in bits_from(8):
        piece = add(piece, swap(piece, bit))
    ffn_parts = to_chips(piece)
    grad_bias = small[17:, :heads]
    small = ring_sum[feats // 4 :].reshape(24, row)
    grad_norm2, grad_norm1 = small[:8].reshape(width), small[8:16].reshape(width) / norm1_gain
    stat_sums = small[16, :3]
    own = jnp.stack([after(part, late, small) for part in ffn_parts])
    late = to_chips(after(late, small))
    grad_gate, grad_up, grad_down = place(where, own, swap(own, 1), (units // 4,) * 3)
    grad_gate, grad_up = jnp.transpose(grad_gate), jnp.transpose(grad_up)
    count = shard * rows_here * width * n_dp * ring
    rms_stats = jnp.sqrt(stat_sums / count)

    late = jnp.stack([after(part, grad_down) for part in late])
    d_one = after(d_one, own).astype(F32)
    x_in = x_low.astype(F32)
    r_one = inverse_rms(x_in)
    u_one = d_one * norm1_gain
    grad_tokens = (
        d_x_one + r_one * u_one - x_in * (r_one * r_one * r_one * jnp.mean(u_one * x_in, axis=-1, keepdims=True))
    ).astype(BF16)

    late_other = swap(late, 1)
    late = after(late, grad_tokens)
    grad_query, grad_key, grad_value, grad_out = place_late(where, late, late_other, width // 8)

    shape = (shard, rows_here, width)
    return (
        out_tokens.reshape(shape),
        grad_tokens.reshape(shape),
        grad_norm1,
        grad_query,
        grad_key,
        grad_value,
        grad_out,
        grad_bias,
        grad_norm2,
        grad_gate,
        grad_up,
        grad_down,
        rms_stats,
    )


def solution(mesh):
    n_dp, ring = mesh.devices.shape
    by_core = Mesh(mesh.devices.reshape(n_dp // 2, 2, ring), (*ROWS_AXES, "tensor"))
    in_specs = (
        P("tensor", ROWS_AXES, None),
        P(ROWS_AXES, None),
        P(),
        P(None, "tensor"),
        P(None, "tensor"),
        P(None, "tensor"),
        P("tensor", None),
        P(None, "tensor"),
        P(),
        P(None, "tensor"),
        P(None, "tensor"),
        P("tensor", None),
        P("tensor", ROWS_AXES, None),
    )
    out_specs = (
        P("tensor", ROWS_AXES, None),
        P("tensor", ROWS_AXES, None),
        P(),
        P(None, "tensor"),
        P(None, "tensor"),
        P(None, "tensor"),
        P("tensor", None),
        P(None, "tensor"),
        P(),
        P(None, "tensor"),
        P(None, "tensor"),
        P("tensor", None),
        P(),
    )
    return jax.shard_map(local, mesh=by_core, in_specs=in_specs, out_specs=out_specs, check_vma=False)
```

```python
import functools
import jax
import jax.numpy as jnp
from jax import lax
from jax.experimental import pallas as pl
from jax.experimental.pallas import tpu as pltpu
from jax.sharding import Mesh, PartitionSpec as P

EPSILON = 1e-06
THRESHOLDS = (12, 16, 23, 32, 46, 64, 91)
TILE = 128
SEG = 384
NT = (((1,), (1,)), ((), ()))
NN = (((1,), (0,)), ((), ()))
NN = (((1,), (0,)), ((), ()))
TN = (((0,), (0,)), ((), ()))
F32 = jnp.float32
BF16 = jnp.bfloat16
SMALL = pl.CostEstimate(flops=1000, bytes_accessed=1000, transcendentals=0)


def bucket_of(offset):
    distance = jnp.abs(offset)
    far_bucket = 8 + sum(((distance >= threshold).astype(jnp.int32) for threshold in THRESHOLDS))
    return jnp.where(distance < 8, distance, far_bucket) + 16 * (offset > 0).astype(jnp.int32)


def tile_bucket(delta, key_axis):
    keys = lax.broadcasted_iota(jnp.int32, (TILE, TILE), key_axis)
    queries = lax.broadcasted_iota(jnp.int32, (TILE, TILE), 1 - key_axis)
    return bucket_of(TILE * delta + keys - queries)


def bias_tiles_kernel(bias_ref, out_ref):
    buckets, heads = bias_ref.shape
    for delta in (-1, 0, 1):
        bucket = tile_bucket(delta, 0)
        tiles = [jnp.zeros((TILE, TILE), F32) for _ in range(heads)]
        for b in range(buckets):
            hit = bucket == b
            tiles = [jnp.where(hit, bias_ref[b, h], t) for h, t in enumerate(tiles)]
        for h in range(heads):
            out_ref[h, delta + 1] = tiles[h]


def bias_tiles(rel_bias):
    return pl.pallas_call(
        bias_tiles_kernel,
        out_shape=jax.ShapeDtypeStruct((rel_bias.shape[1], 3, TILE, TILE), F32),
        in_specs=[pl.BlockSpec(memory_space=pltpu.SMEM)],
        out_specs=pl.BlockSpec(memory_space=pltpu.VMEM),
        name="bias_tiles",
    )(rel_bias)


def bias_grad_kernel(near_ref, far_ref, out_ref):
    heads = near_ref.shape[0]
    row = lax.broadcasted_iota(jnp.int32, (32, TILE), 0)
    lane = lax.broadcasted_iota(jnp.int32, (32, TILE), 1)
    bucket = [tile_bucket(delta, 0) for delta in (-1, 0, 1)]
    total = jnp.zeros((32, TILE), F32)
    for h in range(heads):
        near = [near_ref[h, d] for d in range(3)]
        for b in range(32):
            deltas = (0, 1) if b < 16 else (1, 2)
            part = sum(jnp.where(bucket[d] == b, near[d], 0.0) for d in deltas)
            part = jnp.sum(part.reshape(16, 8, TILE), axis=0)
            if b == 15:
                part = part + far_ref[h, 0]
            if b == 31:
                part = part + far_ref[h, 1]
            line = jnp.sum(part, axis=0, keepdims=True)
            total = jnp.where((row == b) & (lane == h), jnp.sum(line, axis=1, keepdims=True), total)
    out_ref[...] = total


def bias_grad(near, far):
    return pl.pallas_call(
        bias_grad_kernel,
        out_shape=jax.ShapeDtypeStruct((32, TILE), F32),
        name="bias_grad",
    )(near, far)


def attn_fwd_kernel(seg_ref, bias_ref, qkv_ref, tile_ref, o_ref, lse_ref, s_ref, p_ref, l_ref, vt_ref, ot_ref):
    length, width = o_ref.shape
    q_ref, k_ref, v_ref = (qkv_ref.at[:, n * width : (n + 1) * width] for n in range(3))
    heads = width // 64
    lane = lax.broadcasted_iota(jnp.int32, (1, width), 1)
    one_example = seg_ref[0, length - 1] == seg_ref[0, 0]
    vt_ref[...] = jnp.transpose(v_ref[...])

    def blocks(h, mask, spans):
        below = bias_ref[15, h]
        above = bias_ref[31, h]
        head = pl.ds(pl.multiple_of(h * 64, 64), 64)
        for lo, hi in spans:
            qh = jnp.where(mask, q_ref[lo:hi], jnp.zeros((), BF16))
            s_ref[lo:hi, lo:hi] = lax.dot_general(k_ref[lo:hi], qh, NT, preferred_element_type=F32)
            tiles = range(lo // TILE, hi // TILE)
            for i in tiles:
                cols = slice(i * TILE, (i + 1) * TILE)
                near_top, sides = None, {-1: None, 1: None}
                for j in tiles:
                    part = s_ref[j * TILE : (j + 1) * TILE, cols]
                    if abs(j - i) <= 1:
                        part = part + tile_ref[h, j - i + 1]
                        s_ref[j * TILE : (j + 1) * TILE, cols] = part
                    part = jnp.max(part.reshape(TILE // 8, 8, TILE), axis=0)
                    if abs(j - i) <= 1:
                        near_top = part if near_top is None else jnp.maximum(near_top, part)
                    else:
                        side = 1 if j > i else -1
                        sides[side] = part if sides[side] is None else jnp.maximum(sides[side], part)
                top = near_top
                for side, constant in ((-1, below), (1, above)):
                    if sides[side] is not None:
                        top = jnp.maximum(top, sides[side] + constant)
                top = jnp.max(top, axis=0, keepdims=True)
                total = jnp.zeros((8, TILE), F32)
                for j in tiles:
                    shift = top
                    if abs(j - i) > 1:
                        shift = top - (below if j < i else above)
                    e = jnp.exp(s_ref[j * TILE : (j + 1) * TILE, cols] - shift)
                    total = total + jnp.sum(e.reshape(TILE // 8, 8, TILE), axis=0)
                    p_ref[j * TILE : (j + 1) * TILE, cols] = e.astype(BF16)
                total = jnp.sum(total, axis=0, keepdims=True)
                l_ref[0:1, cols] = 1.0 / total
                lse_ref[h, 0:1, cols] = top + jnp.log(total)
            ot_ref[head, lo:hi] = (
                lax.dot_general(vt_ref[head, lo:hi], p_ref[lo:hi, lo:hi], NN, preferred_element_type=F32)
                * l_ref[0:1, lo:hi]
            )

    @pl.loop(0, heads)
    def _(h):
        mask = (lane // 64) == h

        @pl.when(one_example)
        def _():
            blocks(h, mask, ((0, length),))

        @pl.when(jnp.logical_not(one_example))
        def _():
            blocks(h, mask, tuple((lo, lo + SEG) for lo in range(0, length, SEG)))

    o_ref[...] = jnp.transpose(ot_ref[...]).astype(BF16)


def attn_fwd(seg, bias, qkv, tiles):
    length, width = qkv.shape[0], qkv.shape[1] // 3
    heads = width // 64
    vmem = pl.BlockSpec(memory_space=pltpu.VMEM)
    smem = pl.BlockSpec(memory_space=pltpu.SMEM)
    return pl.pallas_call(
        attn_fwd_kernel,
        out_shape=(
            jax.ShapeDtypeStruct((length, width), BF16),
            jax.ShapeDtypeStruct((heads, 8, length), F32),
        ),
        in_specs=[smem, smem, vmem, vmem],
        out_specs=(vmem, vmem),
        scratch_shapes=[
            pltpu.VMEM((length, length), F32),
            pltpu.VMEM((length, length), BF16),
            pltpu.VMEM((8, length), F32),
            pltpu.VMEM((width, length), BF16),
            pltpu.VMEM((width, length), F32),
        ],
        compiler_params=pltpu.CompilerParams(vmem_limit_bytes=40 << 20),
        cost_estimate=SMALL,
        name="attn_fwd",
    )(seg, bias, qkv, tiles)


def attn_bwd_kernel(
    seg_ref, bias_ref, qkv_ref, o_ref, do_ref, lse_ref, tile_ref,
    dqkv_ref, near_ref, far_ref,
    s_ref, dp_ref, p_ref, ds_ref, dsum_ref, kt_ref, dqt_ref, dka_ref, dva_ref,
):
    length, width = o_ref.shape
    q_ref, k_ref, v_ref = (qkv_ref.at[:, n * width : (n + 1) * width] for n in range(3))
    heads = width // 64
    lane = lax.broadcasted_iota(jnp.int32, (1, width), 1)
    one_example = seg_ref[0, length - 1] == seg_ref[0, 0]
    kt_ref[...] = jnp.transpose(k_ref[...])
    prod = o_ref[...].astype(F32) * do_ref[...].astype(F32)
    high = prod.astype(BF16)
    low = (prod - high.astype(F32)).astype(BF16)
    head_rows = (
        lax.broadcasted_iota(jnp.int32, (8 * heads, width), 1) // 64
        == lax.broadcasted_iota(jnp.int32, (8 * heads, width), 0) // 8
    ).astype(BF16)
    dsum_ref[...] = lax.dot_general(head_rows, high, NT, preferred_element_type=F32) + lax.dot_general(
        head_rows, low, NT, preferred_element_type=F32
    )
    def blocks(h, mask, spans):
        below = bias_ref[15, h]
        above = bias_ref[31, h]
        near_sum = [None, None, None]
        far_sum = [jnp.zeros((8, TILE), F32)] * 2
        zero = jnp.zeros((), BF16)
        for d in range(3):
            near_ref[h, d] = jnp.zeros((TILE, TILE), F32)
        for lo, hi in spans:
            qh = jnp.where(mask, q_ref[lo:hi], zero)
            dh = jnp.where(mask, do_ref[lo:hi], zero)
            s_ref[lo:hi, lo:hi] = lax.dot_general(k_ref[lo:hi], qh, NT, preferred_element_type=F32)
            dp_ref[lo:hi, lo:hi] = lax.dot_general(v_ref[lo:hi], dh, NT, preferred_element_type=F32)
            for i in range(lo // TILE, hi // TILE):
                cols = slice(i * TILE, (i + 1) * TILE)
                lse = lse_ref[h, 0:1, cols]
                dsum = dsum_ref[pl.ds(pl.multiple_of(h * 8, 8), 1), cols]
                for j in range(lo // TILE, hi // TILE):
                    rows = slice(j * TILE, (j + 1) * TILE)
                    s = s_ref[rows, cols]
                    if abs(j - i) <= 1:
                        e = jnp.exp(s + tile_ref[h, j - i + 1] - lse)
                    else:
                        e = jnp.exp(s - (lse - (below if j < i else above)))
                    ds = e * (dp_ref[rows, cols] - dsum)
                    p_ref[rows, cols] = e.astype(BF16)
                    ds_ref[rows, cols] = ds.astype(BF16)
                    if abs(j - i) <= 1:
                        near_ref[h, j - i + 1] += ds
                    else:
                        side = int(j > i)
                        far_sum[side] = far_sum[side] + jnp.sum(ds.reshape(TILE // 8, 8, TILE), axis=0)
            dv = lax.dot_general(p_ref[lo:hi, lo:hi], dh, NN, preferred_element_type=F32)
            dk = lax.dot_general(ds_ref[lo:hi, lo:hi], qh, NN, preferred_element_type=F32)
            dva_ref[lo:hi] = jnp.where(mask, dv, dva_ref[lo:hi])
            dka_ref[lo:hi] = jnp.where(mask, dk, dka_ref[lo:hi])
            head = pl.ds(pl.multiple_of(h * 64, 64), 64)
            dqt_ref[head, lo:hi] = lax.dot_general(
                kt_ref[head, lo:hi], ds_ref[lo:hi, lo:hi], NN, preferred_element_type=F32
            )
        far_ref[h, 0] = far_sum[0]
        far_ref[h, 1] = far_sum[1]

    @pl.loop(0, heads)
    def _(h):
        mask = (lane // 64) == h

        @pl.when(one_example)
        def _():
            blocks(h, mask, ((0, length),))

        @pl.when(jnp.logical_not(one_example))
        def _():
            blocks(h, mask, tuple((lo, lo + SEG) for lo in range(0, length, SEG)))

    dqkv_ref[:, :width] = jnp.transpose(dqt_ref[...]).astype(BF16)
    dqkv_ref[:, width : 2 * width] = dka_ref[...].astype(BF16)
    dqkv_ref[:, 2 * width :] = dva_ref[...].astype(BF16)


def attn_bwd(seg, bias, qkv, o, do, lse, tiles):
    length, width = o.shape
    heads = width // 64
    vmem = pl.BlockSpec(memory_space=pltpu.VMEM)
    smem = pl.BlockSpec(memory_space=pltpu.SMEM)
    return pl.pallas_call(
        attn_bwd_kernel,
        out_shape=(
            jax.ShapeDtypeStruct((length, 3 * width), BF16),
            jax.ShapeDtypeStruct((heads, 3, TILE, TILE), F32),
            jax.ShapeDtypeStruct((heads, 2, 8, TILE), F32),
        ),
        in_specs=[smem, smem] + [vmem] * 5,
        out_specs=(vmem,) * 3,
        scratch_shapes=[
            pltpu.VMEM((length, length), F32),
            pltpu.VMEM((length, length), F32),
            pltpu.VMEM((length, length), BF16),
            pltpu.VMEM((length, length), BF16),
            pltpu.VMEM((8 * heads, length), F32),
            pltpu.VMEM((width, length), BF16),
            pltpu.VMEM((width, length), F32),
            pltpu.VMEM((length, width), F32),
            pltpu.VMEM((length, width), F32),
        ],
        compiler_params=pltpu.CompilerParams(vmem_limit_bytes=48 << 20),
        cost_estimate=SMALL,
        name="attn_bwd",
    )(seg, bias, qkv, o, do, lse, tiles)


def tanh_gelu(u):
    scale = 0.7978845608028654
    t = jnp.tanh(scale * (u + 0.044715 * (u * u * u)))
    half = 0.5 * (1.0 + t)
    slope = half + (0.5 * u) * (1.0 - t * t) * (scale * (1.0 + 0.134145 * (u * u)))
    return u * half, slope


def ffn_kernel(
    x_ref, c_ref, weights_ref,
    dtwo_ref, ffo_ref, hidden_ref, dgate_ref, dup_ref,
    gate_w, up_w, down_w, sems,
):
    ring, halves, rows, half = weights_ref.shape
    units = rows // 3
    scratches = (gate_w, up_w, down_w)
    copies = [[], [], []]
    for m in range(3):
        for q in range(ring):
            for n in range(halves):
                copies[m].append(
                    pltpu.make_async_copy(
                        weights_ref.at[q, n, m * units : (m + 1) * units],
                        scratches[m].at[q * units : (q + 1) * units, n * half : (n + 1) * half],
                        sems.at[m, halves * q + n],
                    )
                )
    for group in copies:
        for copy in group:
            copy.start()
    for copy in copies[0]:
        copy.wait()
    gate = lax.dot_general(x_ref[...], gate_w[...], NT, preferred_element_type=F32)
    for copy in copies[1]:
        copy.wait()
    up = lax.dot_general(x_ref[...], up_w[...], NT, preferred_element_type=F32)
    for copy in copies[2]:
        copy.wait()
    d_hidden = lax.dot_general(c_ref[...], down_w[...], NT, preferred_element_type=F32)
    value, slope = tanh_gelu(gate)
    hidden = (value * up).astype(BF16)
    d_gate = (d_hidden * up * slope).astype(BF16)
    d_up = (d_hidden * value).astype(BF16)
    hidden_ref[...] = hidden
    dgate_ref[...] = d_gate
    dup_ref[...] = d_up
    dtwo_ref[...] = (
        lax.dot_general(d_gate, gate_w[...], NN, preferred_element_type=F32)
        + lax.dot_general(d_up, up_w[...], NN, preferred_element_type=F32)
    ).astype(dtwo_ref.dtype)
    ffo_ref[...] = lax.dot_general(hidden, down_w[...], NN, preferred_element_type=F32).astype(ffo_ref.dtype)


def ffn(x, c, weights):
    tokens, width = x.shape
    ring, halves, rows, _ = weights.shape
    units = ring * rows // 3
    vmem = pl.BlockSpec(memory_space=pltpu.VMEM)
    anywhere = pl.BlockSpec(memory_space=pl.ANY)
    wide = jax.ShapeDtypeStruct((tokens, width), BF16)
    inner = jax.ShapeDtypeStruct((tokens, units), BF16)
    return pl.pallas_call(
        ffn_kernel,
        out_shape=(wide, wide, inner, inner, inner),
        in_specs=[vmem, vmem, anywhere],
        out_specs=(vmem,) * 5,
        scratch_shapes=[pltpu.VMEM((units, width), BF16)] * 3 + [pltpu.SemaphoreType.DMA((3, halves * ring))],
        compiler_params=pltpu.CompilerParams(vmem_limit_bytes=40 << 20),
        cost_estimate=SMALL,
        name="ffn",
    )(x, c, weights)


def ffn_grads_kernel(n, *refs):
    sources = [refs[i * n : (i + 1) * n] for i in range(5)]
    out_ref = refs[5 * n]
    held = refs[5 * n + 1 : 5 * n + 6]
    sems = refs[5 * n + 6]
    ring, halves, rows, half = out_ref.shape
    units = rows // 3
    tokens = sources[0][0].shape[0]
    copies = [
        [
            pltpu.make_async_copy(ref, target.at[j * tokens : (j + 1) * tokens], sems.at[i, j])
            for j, ref in enumerate(group)
        ]
        for i, (group, target) in enumerate(zip(sources, held))
    ]
    for group in copies:
        for copy in group:
            copy.start()
    waited = set()
    for m, (lhs, rhs) in ((2, (0, 1)), (0, (2, 3)), (1, (4, 3))):
        for i in (lhs, rhs):
            if i not in waited:
                waited.add(i)
                for copy in copies[i]:
                    copy.wait()
        grad = lax.dot_general(held[lhs][...], held[rhs][...], TN, preferred_element_type=F32).astype(BF16)
        for q in range(ring):
            for k in range(halves):
                out_ref[q, k, m * units : (m + 1) * units] = grad[
                    q * units : (q + 1) * units, k * half : (k + 1) * half
                ]


def ffn_grads(hs, cs, gs, xs, us, ring):
    rows, width = xs[0].shape
    units = hs[0].shape[1]
    n = len(xs)
    vmem = pl.BlockSpec(memory_space=pltpu.VMEM)
    anywhere = pl.BlockSpec(memory_space=pl.ANY)
    shape = jax.ShapeDtypeStruct((ring, 2, 3 * units // ring, width // 2), BF16)
    wide, inner = pltpu.VMEM((n * rows, width), BF16), pltpu.VMEM((n * rows, units), BF16)
    return pl.pallas_call(
        functools.partial(ffn_grads_kernel, n),
        out_shape=shape,
        in_specs=[anywhere] * (5 * n),
        out_specs=vmem,
        scratch_shapes=[inner, wide, inner, wide, inner, pltpu.SemaphoreType.DMA((5, n))],
        compiler_params=pltpu.CompilerParams(vmem_limit_bytes=58 << 20),
        cost_estimate=SMALL,
        name="ffn_grads",
    )(*hs, *cs, *gs, *xs, *us)


def normed_grad_kernel(d_ref, w_ref, out_ref):
    out_ref[...] = lax.dot_general(d_ref[...], w_ref[...], NT, preferred_element_type=F32).astype(BF16)


def normed_grad(d, w):
    vmem = pl.BlockSpec(memory_space=pltpu.VMEM)
    return pl.pallas_call(
        normed_grad_kernel,
        out_shape=jax.ShapeDtypeStruct((d.shape[0], w.shape[0]), BF16),
        in_specs=[vmem, vmem],
        out_specs=vmem,
        compiler_params=pltpu.CompilerParams(vmem_limit_bytes=24 << 20),
        cost_estimate=SMALL,
        name="normed_grad",
    )(d, w)


def late_grads_kernel(where_ref, *refs):
    blocks = refs[:-10]
    d_ref, w_ref, o_ref, da_ref, keep_ref, give_ref, gain_ref, x_ref, held, sems = refs[-10:]
    core, chip = where_ref[0], where_ref[1]
    chips, _, half = keep_ref.shape
    ring = len(blocks)
    copies = []
    for s, block in enumerate(blocks):
        first = lax.rem(where_ref[3] + ring - s, ring) * block.shape[0]
        target = x_ref.at[pl.ds(pl.multiple_of(first, 32), block.shape[0])]
        copies.append(pltpu.make_async_copy(block, target, sems.at[s]))
    for copy in copies:
        copy.start()
    width = x_ref.shape[1]
    rows = width // (2 * chips)
    out_rows = o_ref.shape[1] // (ring * chips)
    mid = rows + rows // 2
    for n, out_ref in enumerate((give_ref, keep_ref)):
        start = pl.multiple_of((core ^ (1 - n)) * half, 128)
        held[...] = lax.dot_general(
            o_ref[...], da_ref[:, pl.ds(start, half)], TN, preferred_element_type=F32
        ).astype(BF16)
        for r in range(chips):
            for q in range(ring):
                first = (q * chips + (chip ^ r)) * out_rows
                out_ref[r, mid + q * out_rows : mid + (q + 1) * out_rows] = held[
                    pl.ds(pl.multiple_of(first, out_rows), out_rows)
                ]
    for copy in copies:
        copy.wait()
    for n, out_ref in enumerate((give_ref, keep_ref)):
        for r in range(chips):
            block = (core ^ (1 - n)) * chips + (chip ^ r)
            start = pl.multiple_of(block * rows, 128)
            grad = lax.dot_general(x_ref[:, pl.ds(start, rows)], d_ref[...], TN, preferred_element_type=F32)
            low = grad.astype(BF16)
            out_ref[r, :rows] = low[:, :half]
            out_ref[r, rows:mid, : half // 2] = low[: rows // 2, half:]
            out_ref[r, rows:mid, half // 2 :] = low[rows // 2 :, half:]
            line = jnp.sum(grad * w_ref[pl.ds(start, rows)].astype(F32), axis=1, keepdims=True)
            gain_ref[pl.ds(block, 1)] = jnp.transpose(jnp.broadcast_to(line, (rows, rows)))[:1]


def late_grads(where, blocks, d, w, o, d_attn):
    width = w.shape[0]
    rows = width // 8
    vmem = pl.BlockSpec(memory_space=pltpu.VMEM)
    shape = jax.ShapeDtypeStruct((4, rows + rows // 2 + o.shape[1] // 4, width // 2), BF16)
    return pl.pallas_call(
        late_grads_kernel,
        out_shape=(shape, shape, jax.ShapeDtypeStruct((8, rows), F32)),
        in_specs=[pl.BlockSpec(memory_space=pltpu.SMEM)] + [pl.BlockSpec(memory_space=pl.ANY)] * len(blocks) + [vmem] * 4,
        out_specs=(vmem,) * 3,
        scratch_shapes=[
            pltpu.VMEM((d.shape[0], width), BF16),
            pltpu.VMEM((o.shape[1], width // 2), BF16),
            pltpu.SemaphoreType.DMA((len(blocks),)),
        ],
        compiler_params=pltpu.CompilerParams(vmem_limit_bytes=56 << 20),
        cost_estimate=SMALL,
        name="late_grads",
    )(where, *blocks, d, w, o, d_attn)


def place_kernel(where_ref, own_ref, other_ref, *out_refs):
    core, chip = where_ref[0], where_ref[1]
    chips, _, half = own_ref.shape
    first = 0
    for target in out_refs:
        units = target.shape[0] // chips
        for r in range(chips):
            rows = pl.ds(pl.multiple_of((chip ^ r) * units, 8), units)
            for n, ref in enumerate((own_ref, other_ref)):
                columns = pl.ds(pl.multiple_of((core ^ n) * half, 128), half)
                target[rows, columns] = ref[r, first : first + units].astype(F32)
        first += units


def place(where, own, other, sizes):
    chips, _, half = own.shape
    vmem = pl.BlockSpec(memory_space=pltpu.VMEM)
    return pl.pallas_call(
        place_kernel,
        out_shape=tuple(jax.ShapeDtypeStruct((chips * size, 2 * half), F32) for size in sizes),
        in_specs=[pl.BlockSpec(memory_space=pltpu.SMEM), vmem, vmem],
        out_specs=(vmem,) * len(sizes),
        compiler_params=pltpu.CompilerParams(vmem_limit_bytes=40 << 20),
        cost_estimate=SMALL,
        name="place",
    )(where, own, other)


def place_late_kernel(where_ref, own_ref, other_ref, *out_refs):
    core, chip = where_ref[0], where_ref[1]
    chips, total, half = own_ref.shape
    projections, out_ref = out_refs[:3], out_refs[3]
    rows, part = projections[0].shape[0] // (2 * chips), projections[0].shape[1]
    mid = rows + rows // 2
    for n, ref in enumerate((own_ref, other_ref)):
        for r in range(chips):
            start = ((core ^ n) * chips + (chip ^ r)) * rows
            target = pl.ds(pl.multiple_of(start, 8), rows)
            for i in range(2):
                projections[i][target] = ref[r, :rows, i * part : (i + 1) * part].astype(F32)
            for i in range(2):
                target = pl.ds(pl.multiple_of(start + i * (rows // 2), 8), rows // 2)
                projections[2][target] = ref[r, rows:mid, i * part : (i + 1) * part].astype(F32)
            start = pl.multiple_of((chip ^ r) * (total - mid), 8)
            columns = pl.ds(pl.multiple_of((core ^ n) * half, 128), half)
            out_ref[pl.ds(start, total - mid), columns] = ref[r, mid:].astype(F32)


def place_late(where, own, other, rows):
    chips, total, half = own.shape
    vmem = pl.BlockSpec(memory_space=pltpu.VMEM)
    projection = jax.ShapeDtypeStruct((2 * chips * rows, half // 2), F32)
    out_rows = chips * (total - rows - rows // 2)
    return pl.pallas_call(
        place_late_kernel,
        out_shape=(projection,) * 3 + (jax.ShapeDtypeStruct((out_rows, 2 * half), F32),),
        in_specs=[pl.BlockSpec(memory_space=pltpu.SMEM), vmem, vmem],
        out_specs=(vmem,) * 4,
        cost_estimate=SMALL,
        name="place_late",
    )(where, own, other)


def place_out_kernel(where_ref, *refs):
    pieces, out_ref = refs[:-1], refs[-1]
    _, ring, rows, _ = pieces[0].shape
    core, chip, z = where_ref[0], where_ref[1], where_ref[3]
    for s in range(ring):
        quarter = lax.rem(z + ring - s, ring)
        for r, ref in enumerate(pieces):
            for n in range(2):
                start = ((quarter * len(pieces) + (chip ^ r)) * 2 + (core ^ n)) * rows
                out_ref[pl.ds(pl.multiple_of(start, rows), rows)] = ref[n, s]


def place_out(where, pieces):
    _, ring, rows, width = pieces[0].shape
    vmem = pl.BlockSpec(memory_space=pltpu.VMEM)
    return pl.pallas_call(
        place_out_kernel,
        out_shape=jax.ShapeDtypeStruct((2 * len(pieces) * ring * rows, width), pieces[0].dtype),
        in_specs=[pl.BlockSpec(memory_space=pltpu.SMEM)] + [vmem] * len(pieces),
        out_specs=vmem,
        cost_estimate=SMALL,
        name="place_out",
    )(where, *pieces)


ROWS_AXES = ("chips", "core")


def swap(value, mask):
    size = lax.axis_size(ROWS_AXES)
    return lax.ppermute(value, ROWS_AXES, [(i, i ^ mask) for i in range(size)])


def shift(value, step):
    size = lax.axis_size("tensor")
    return lax.ppermute(value, "tensor", [(i, (i + step) % size) for i in range(size)])


def add(left, right):
    return (left.astype(F32) + right.astype(F32)).astype(BF16)


def after(value, *others):
    return lax.optimization_barrier((value, *others))[0]


def bits_from(first):
    bit = first
    while bit < lax.axis_size(ROWS_AXES):
        yield bit
        bit *= 2


def sum_rows(value):
    value = sum(to_chips(value))
    for bit in (1, *bits_from(8)):
        value = value + swap(value, bit)
    return value


def sum_ring(value):
    return value + shift(value, 1) + shift(value, 2) + shift(value, 3)


def dot(left, right, dims=NN):
    return lax.dot_general(left, right, dims, preferred_element_type=F32)


def inverse_rms(values):
    return lax.rsqrt(jnp.mean(values * values, axis=-1, keepdims=True) + EPSILON)


CHIPS = (0, 1, 2, 3)


def to_chips(value):
    return [value] + [swap(value, 2 * mask) for mask in CHIPS[1:]]


def local(
    tokens,
    segment_ids,
    norm1_gain,
    w_query,
    w_key,
    w_value,
    w_out,
    rel_bias,
    norm2_gain,
    gate_weight_matrix,
    upward_weight,
    downward_weight,
    cotangent,
):
    shard, rows_here, width = tokens.shape
    length = segment_ids.shape[1]
    heads = rel_bias.shape[1]
    feats = w_query.shape[1]
    units = downward_weight.shape[0]
    ring = lax.axis_size("tensor")
    n_dp = lax.axis_size(ROWS_AXES)
    z = lax.axis_index("tensor")
    dp = lax.axis_index(ROWS_AXES)
    core = dp & 1
    chip = (dp >> 1) & 3
    where = jnp.stack([core, chip, dp, z]).astype(jnp.int32)

    x_low = tokens.reshape(shard, width)
    cot = cotangent.reshape(shard, width)
    tiles = bias_tiles(rel_bias)
    w_qkv = jnp.concatenate([w_query, w_key, w_value], axis=1)

    out_rows = feats // 8
    out_piece = lax.dynamic_slice_in_dim(w_out, (2 * chip + core) * out_rows, out_rows, 0)
    cs = to_chips(cot)
    sent = jnp.concatenate([x_low, out_piece], axis=0)
    blocks, normed_blocks, qkv_blocks = [], [], []
    for s in range(ring):
        if s == ring - 1:
            sent = after(sent, tiles, qkv_blocks[1], *cs)
        if s:
            sent = shift(sent, 1)
        values = sent[:shard].astype(F32)
        normed = (values * inverse_rms(values) * norm1_gain).astype(BF16)
        blocks.append(sent)
        normed_blocks.append(normed)
        qkv_blocks.append(dot(normed, w_qkv).astype(BF16))
    out_ring = jnp.stack([block[shard:] for block in blocks])

    def unit_rows(array):
        return lax.dynamic_slice(array, (chip * (units // 4), core * (width // 2)), (units // 4, width // 2))

    pack = jnp.concatenate(
        [
            unit_rows(jnp.transpose(gate_weight_matrix)),
            unit_rows(jnp.transpose(upward_weight)),
            unit_rows(downward_weight),
        ],
        axis=0,
    )
    weights = lax.all_gather(after(pack, blocks[3]), ("tensor", "core"), axis=0)
    weights = weights.reshape(ring, 2, *pack.shape)

    qkv = jnp.zeros((length, 3 * feats), BF16)
    for s, block in enumerate(qkv_blocks):
        qkv = lax.dynamic_update_slice_in_dim(qkv, block, ((z - s) % ring) * shard, 0)

    o_row, lse = attn_fwd(segment_ids, rel_bias, qkv, tiles)
    out_pair = jnp.stack([out_ring, swap(out_ring, 1)])
    out_all = place_out(where, to_chips(after(out_pair, o_row)))
    o_home = lax.all_to_all(o_row, "tensor", 0, 1, tiled=True)
    attn = dot(o_home, out_all)
    x_one = x_low.astype(F32) + attn
    r_two = inverse_rms(x_one)
    norm_two = (x_one * r_two * norm2_gain).astype(BF16)

    xs = to_chips(norm_two)
    parts, back = [], []
    for r, (x, c) in enumerate(zip(xs, cs)):
        if parts:
            x = after(x, parts[-1][0])
        if r == 3:
            back.append(swap(parts[1][0], 2))
            x = after(x, back[0])
        parts.append(ffn(x, c, weights))

    def returns(which, *others):
        terms = [after(part[which], *others) if others else part[which] for part in parts]
        return [terms[0]] + [swap(terms[mask], 2 * mask) for mask in CHIPS[1:]]

    def total_of(terms):
        return sum(term.astype(F32) for term in terms)

    back = [parts[0][0], back[0]] + [swap(parts[r][0], 2 * r) for r in (2, 3)]
    d_two = total_of(back)
    u_two = d_two * norm2_gain
    d_x_one = cot.astype(F32) + r_two * u_two - x_one * (
        r_two * r_two * r_two * jnp.mean(u_two * x_one, axis=-1, keepdims=True)
    )
    d_attn = d_x_one.astype(BF16)
    d_o = dot(d_attn, out_all, NT).astype(BF16)
    do_row = lax.all_to_all(d_o, "tensor", 1, 0, tiled=True)

    unit_grads = ffn_grads(
        [after(parts[0][2], d_o)] + [part[2] for part in parts[1:]],
        cs,
        [part[3] for part in parts],
        xs,
        [part[4] for part in parts],
        ring,
    )
    ffn_piece = lax.psum_scatter(
        after(unit_grads, do_row).reshape(-1, width // 2), ("tensor", "core"), scatter_dimension=0, tiled=True
    )

    def from_chips(pieces):
        return [pieces[0]] + [swap(pieces[r], 2 * r) for r in CHIPS[1:]]

    ffo_back = returns(1, do_row)
    ffo = total_of(ffo_back)
    y = x_one + ffo
    out_tokens = y.astype(BF16)
    grad_two = jnp.sum(d_two * x_one * r_two, axis=0)
    stats = jnp.stack([jnp.sum(attn * attn), jnp.sum(ffo * ffo), jnp.sum(y * y)])

    do_row = after(do_row, unit_grads)

    dqkv, near, far = attn_bwd(segment_ids, rel_bias, qkv, o_row, do_row, lse, tiles)
    dqkv = after(dqkv, *ffo_back)
    keep, give, grad_one = late_grads(where, normed_blocks, dqkv, w_qkv, o_home, d_attn)
    d_one_part = normed_grad(after(dqkv, give), w_qkv)
    d_one = lax.psum_scatter(after(d_one_part, ffn_piece), "tensor", scatter_dimension=0, tiled=True)
    summed = add(keep, swap(give, 1))
    chip_parts = from_chips(summed)
    near = after(near, chip_parts[1])
    row = width // 8
    stats = jnp.pad(stats, (0, row - 3)).reshape(1, row)
    small = jnp.concatenate([grad_two.reshape(8, row), grad_one, stats, bias_grad(near, far)], axis=0)
    got = total_of(chip_parts).astype(BF16)
    small = sum_rows(small)
    mid = got.shape[0] - feats
    by_ring = got[mid:].reshape(ring, feats // 4, width // 2)
    out_parts = [lax.dynamic_index_in_dim(by_ring, (z + s) % ring, 0, keepdims=False) for s in range(ring)]
    small_rows = jnp.pad(small[:17], ((0, 7), (0, 0))).reshape(6, width // 2)
    ring_sum = total_of(
        [
            shift(jnp.concatenate([part.astype(F32), small_rows], axis=0), s) if s else
            jnp.concatenate([part.astype(F32), small_rows], axis=0)
            for s, part in enumerate(out_parts)
        ]
    )
    out_piece = ring_sum[: feats // 4].astype(BF16)
    late = jnp.concatenate([got[:mid], out_piece], axis=0)
    for bit in bits_from(8):
        late = add(late, swap(late, bit))
    piece = after(ffn_piece, got, small)
    for bit in bits_from(8):
        piece = add(piece, swap(piece, bit))
    ffn_parts = to_chips(piece)
    grad_bias = small[17:, :heads]
    small = ring_sum[feats // 4 :].reshape(24, row)
    grad_norm2, grad_norm1 = small[:8].reshape(width), small[8:16].reshape(width) / norm1_gain
    stat_sums = small[16, :3]
    own = jnp.stack([after(part, late, small) for part in ffn_parts])
    late = to_chips(after(late, small))
    grad_gate, grad_up, grad_down = place(where, own, swap(own, 1), (units // 4,) * 3)
    grad_gate, grad_up = jnp.transpose(grad_gate), jnp.transpose(grad_up)
    count = shard * rows_here * width * n_dp * ring
    rms_stats = jnp.sqrt(stat_sums / count)

    late = jnp.stack([after(part, grad_down) for part in late])
    d_one = after(d_one, own).astype(F32)
    x_in = x_low.astype(F32)
    r_one = inverse_rms(x_in)
    u_one = d_one * norm1_gain
    grad_tokens = (
        d_x_one + r_one * u_one - x_in * (r_one * r_one * r_one * jnp.mean(u_one * x_in, axis=-1, keepdims=True))
    ).astype(BF16)

    late_other = swap(late, 1)
    late = after(late, grad_tokens)
    grad_query, grad_key, grad_value, grad_out = place_late(where, late, late_other, width // 8)

    shape = (shard, rows_here, width)
    return (
        out_tokens.reshape(shape),
        grad_tokens.reshape(shape),
        grad_norm1,
        grad_query,
        grad_key,
        grad_value,
        grad_out,
        grad_bias,
        grad_norm2,
        grad_gate,
        grad_up,
        grad_down,
        rms_stats,
    )


def solution(mesh):
    n_dp, ring = mesh.devices.shape
    by_core = Mesh(mesh.devices.reshape(n_dp // 2, 2, ring), (*ROWS_AXES, "tensor"))
    in_specs = (
        P("tensor", ROWS_AXES, None),
        P(ROWS_AXES, None),
        P(),
        P(None, "tensor"),
        P(None, "tensor"),
        P(None, "tensor"),
        P("tensor", None),
        P(None, "tensor"),
        P(),
        P(None, "tensor"),
        P(None, "tensor"),
        P("tensor", None),
        P("tensor", ROWS_AXES, None),
    )
    out_specs = (
        P("tensor", ROWS_AXES, None),
        P("tensor", ROWS_AXES, None),
        P(),
        P(None, "tensor"),
        P(None, "tensor"),
        P(None, "tensor"),
        P("tensor", None),
        P(None, "tensor"),
        P(),
        P(None, "tensor"),
        P(None, "tensor"),
        P("tensor", None),
        P(),
    )
    return jax.shard_map(local, mesh=by_core, in_specs=in_specs, out_specs=out_specs, check_vma=False)
```
